32 devices in a mesh: slab: 4 (over y, core), sub: 8 (over z, x).
Axes of the slice: x: 2, y: 2, z: 4, core: 2. Of those that a mesh axis runs over, the one named last changes fastest.
Arguments:
- positions: float32 [3, 2097152], P(None, ('slab', 'sub')), may hold values from 0 to 32, as said below
- masses: float32 [2097152], P(('slab', 'sub')), may hold values from 0.001 to 0.01
- leaf_counts: int32 [8192], P(('slab', 'sub')), may hold values from 64 to 256, as said below
- send_leaves: int32 [32, 256], P(('slab', 'sub')), may hold values from 0 to 255, as said below
- send_parents: int32 [32, 64], P(('slab', 'sub')), may hold values from 0 to 31, as said below
- near_pairs: int32 [32, 3, 256], P(('slab', 'sub')), may hold values from -1 to 511, as said below
- far_pairs: int32 [32, 3, 1024], P(('slab', 'sub')), may hold values from -1 to 511, as said below
- parent_pairs: int32 [32, 3, 64], P(('slab', 'sub')), may hold values from -1 to 95, as said below
Outputs:
- field: float32 [4, 2097152], P(None, ('slab', 'sub'))
The draws below stay inside these ranges and needn't reach their ends.
Inputs may be any that keep to these rules, and one draw needn't show every extreme that they name: `positions`: the coordinates of a body of leaf c on device (s, u) lie within one unit above that leaf's integer coordinates along each dimension. `leaf_counts`: every device has a leaf whose 256 slots are all used. `send_leaves`: within one direction of a row, the 64 leaves are different. `send_parents`: within one direction of a row, the 16 parent cells are different. `near_pairs`: row 0 is an own leaf, row 1 a leaf table entry or -1 for an unused entry (unused entries come last), row 2 the z image -1, 0 or 1 (0 where unused). Own pairs have a < b; no pair repeats; pairs are leaves at most one leaf apart along each dimension after the image. `far_pairs`: as near_pairs, for leaves whose squared separation after the image is 4 to 12 leaf units. `parent_pairs`: as near_pairs, for parent cells whose squared separation after the image is 2 parent units or more, with the parent table.
All inputs are finite; a program needn't handle non-finite values.
Results may differ from the reference program's by a relative error of at most 0.0003.
Values sent between devices are 32-bit elements; how exact they have to be, the bound alone decides.
No kernel may reach another device: no remote copies, remote signals or barrier semaphores. Data moves between devices by JAX's collectives and lax.ppermute only.
A program may use at most 320 MiB of HBM per device.

```python
import math
import jax
import jax.numpy as jnp
from jax import lax

LEAF = 256
CX = 2
CY = 4
CZ = 32
LEAVES = 256
PARENTS = 32
SLOTS = 64
PSLOTS = 16
NEAR = 256
FAR = 1024
PFAR = 64
BODIES = 2097152
N_SLAB = 4
N_SUB = 8


slab_steps = (1, 0, 1, 1)


sub_steps = (0, 1, 1, -1)


def cell_coords(cell_ids, span_y, span_z):
    return (cell_ids // (span_y * span_z), cell_ids // span_z % span_y, cell_ids % span_z)


def send_table(key, cell_total, slots):
    devices = N_SLAB * N_SUB

    def one_device(device_id):
        device_key = jax.random.fold_in(key, device_id)
        chosen = [jax.random.permutation(jax.random.fold_in(device_key, direction), cell_total)[:slots] for direction in range(4)]
        return jnp.concatenate(chosen).astype(jnp.int32)
    return jax.vmap(one_device)(jnp.arange(devices, dtype=jnp.int32))


def pair_lists(key, span_x, span_y, span_z, slots, length, lower, upper, sent_table):
    devices = N_SLAB * N_SUB
    local_total = span_x * span_y * span_z
    table_total = local_total + 4 * slots
    full_device = jax.random.randint(jax.random.fold_in(key, 7), (), 0, devices)

    def one_device(device_id):
        slab_at = device_id // N_SUB
        sub_at = device_id % N_SUB
        local_ids = jnp.arange(local_total, dtype=jnp.int32)
        own_x, own_y, own_z = cell_coords(local_ids, span_y, span_z)
        table_x = [slab_at * span_x + own_x]
        table_y = [sub_at * span_y + own_y]
        table_z = [own_z]
        for direction in range(4):
            reach_x = slab_at + slab_steps[direction]
            reach_y = sub_at + sub_steps[direction]
            partner = reach_x % N_SLAB * N_SUB + reach_y % N_SUB
            sent_ids = sent_table[partner][direction * slots:(direction + 1) * slots]
            cell_x, cell_y, cell_z = cell_coords(sent_ids, span_y, span_z)
            table_x.append(reach_x * span_x + cell_x)
            table_y.append(reach_y * span_y + cell_y)
            table_z.append(cell_z)
        table_x = jnp.concatenate(table_x)
        table_y = jnp.concatenate(table_y)
        table_z = jnp.concatenate(table_z)
        gap_x = table_x[None, :] - own_x[:, None] - slab_at * span_x
        gap_y = table_y[None, :] - own_y[:, None] - sub_at * span_y
        gap_z = table_z[None, :] - own_z[:, None]
        z_image = jnp.where(gap_z > span_z // 2, -1, jnp.where(gap_z < -(span_z // 2), 1, 0))
        gap_z = gap_z + z_image * span_z
        squared = gap_x * gap_x + gap_y * gap_y + gap_z * gap_z
        others = jnp.arange(table_total, dtype=jnp.int32)
        allowed = (others[None, :] >= local_total) | (local_ids[:, None] < others[None, :])
        wanted = allowed & (squared >= lower) & (squared <= upper)
        device_key = jax.random.fold_in(key, device_id)
        ordering = jax.random.permutation(jax.random.fold_in(device_key, 1), local_total * table_total).astype(jnp.int32)
        scores = jnp.where(wanted.reshape(-1), ordering + local_total * table_total, ordering)
        ranked, chosen = lax.top_k(scores, length)
        owned_ids = chosen // table_total
        partner_ids = chosen % table_total
        lifts = z_image.reshape(-1)[chosen]
        live_count = jax.random.randint(jax.random.fold_in(device_key, 2), (), length // 2, length + 1)
        live_count = jnp.where(device_id == full_device, length, live_count)
        active = jnp.arange(length) < live_count
        return jnp.stack([owned_ids, jnp.where(active, partner_ids, -1), jnp.where(active, lifts, 0)]).astype(jnp.int32)
    return jax.vmap(one_device)(jnp.arange(devices, dtype=jnp.int32))


def draw_positions(key, part):
    total = N_SLAB * N_SUB * LEAVES * LEAF
    body_ids = jnp.arange(total, dtype=jnp.int32)
    device_id = body_ids // (LEAVES * LEAF)
    cell_ids = body_ids // LEAF % LEAVES
    slab_at = device_id // N_SUB
    sub_at = device_id % N_SUB
    cell_x, cell_y, cell_z = cell_coords(cell_ids, CY, CZ)
    corner = jnp.stack([slab_at * CX + cell_x, sub_at * CY + cell_y, cell_z]).astype(jnp.float32)
    inside = jax.random.uniform(key, (3, total), jnp.float32, 0.02, 0.98)
    return corner + inside


def draw_leaf_counts(key, part):
    devices = N_SLAB * N_SUB
    counts = jax.random.randint(jax.random.fold_in(key, 11), (devices, LEAVES), LEAF // 4, LEAF + 1)
    full_leaf = jax.random.randint(jax.random.fold_in(key, 12), (devices, 1), 0, LEAVES)
    counts = jnp.where(jnp.arange(LEAVES)[None, :] == full_leaf, LEAF, counts)
    return counts.reshape(-1).astype(jnp.int32)


def draw_send_leaves(key, part):
    return send_table(jax.random.fold_in(key, 101), LEAVES, SLOTS)


def draw_send_parents(key, part):
    return send_table(jax.random.fold_in(key, 202), PARENTS, PSLOTS)


def draw_near_pairs(key, part):
    sent_table = send_table(jax.random.fold_in(key, 101), LEAVES, SLOTS)
    return pair_lists(jax.random.fold_in(key, 303), CX, CY, CZ, SLOTS, NEAR, 1, 3, sent_table)


def draw_far_pairs(key, part):
    sent_table = send_table(jax.random.fold_in(key, 101), LEAVES, SLOTS)
    return pair_lists(jax.random.fold_in(key, 404), CX, CY, CZ, SLOTS, FAR, 4, 12, sent_table)


def draw_parent_pairs(key, part):
    sent_table = send_table(jax.random.fold_in(key, 202), PARENTS, PSLOTS)
    return pair_lists(jax.random.fold_in(key, 505), CX // 2, CY // 2, CZ // 2, PSLOTS, PFAR, 2, 1000000, sent_table)


def steps_of(rng, shape, cuts, smallest, top_value):
    gain, own = 1.0, jax.random.fold_in(rng, 6)
    for axis_at, shards_of in cuts:
        draws = jnp.exp(jax.random.uniform(jax.random.fold_in(own, axis_at), (shards_of,), jnp.float32, smallest / len(cuts), top_value / len(cuts)))
        gain = gain * jnp.repeat(draws, shape[axis_at] // shards_of).reshape([-1 if axis == axis_at else 1 for axis in range(len(shape))])
    return gain


def setup_inputs(seed: int = 0) -> dict:
    key_list = jax.random.split(jax.random.key(seed), 9)
    positions = draw_positions(jax.random.fold_in(key_list[8], 71), 0)
    masses = jnp.clip(jnp.exp(math.log(0.01) - 2.30258502 * jax.random.uniform(key_list[1], (BODIES,), jnp.float32) ** steps_of(key_list[1], (BODIES,), ((0, 32),), -0.2, 0.2)), 0.001, 0.01)
    leaf_counts = draw_leaf_counts(jax.random.fold_in(key_list[8], 71), 0)
    send_leaves = draw_send_leaves(jax.random.fold_in(key_list[8], 71), 0)
    send_parents = draw_send_parents(jax.random.fold_in(key_list[8], 71), 0)
    near_pairs = draw_near_pairs(jax.random.fold_in(key_list[8], 71), 0)
    far_pairs = draw_far_pairs(jax.random.fold_in(key_list[8], 71), 0)
    parent_pairs = draw_parent_pairs(jax.random.fold_in(key_list[8], 71), 0)
    return {"positions": positions, "masses": masses, "leaf_counts": leaf_counts, "send_leaves": send_leaves, "send_parents": send_parents, "near_pairs": near_pairs, "far_pairs": far_pairs, "parent_pairs": parent_pairs}


tensor_offsets = (0, 1, 4, 13, 40, 121)
factorials = (1.0, 1.0, 2.0, 6.0, 24.0)
soft_square = 0.0025
slab_steps = (1, 0, 1, 1)
sub_steps = (0, 1, 1, -1)

def outer_powers(offset):
    tail = offset.shape[1:]
    powers = [jnp.ones((1,) + tail, offset.dtype)]
    for degree in range(4):
        before = powers[-1]
        grown = before[:, None] * offset[None, :]
        powers.append(grown.reshape((before.shape[0] * 3,) + tail))
    return powers

def inverse_distance(vector):
    return 1.0 / jnp.sqrt(jnp.sum(vector * vector))

def jacobian_of(inner):

    def result(vector):
        values, pullback = jax.vjp(inner, vector)
        unit_rows = jnp.eye(values.shape[0], dtype=values.dtype)
        stacked = jax.vmap(pullback)(unit_rows)[0]
        return stacked.reshape(-1)
    return result

def derivative_tensors(separation):
    first_grad = jax.grad(inverse_distance)
    second_grad = jacobian_of(first_grad)
    third_grad = jacobian_of(second_grad)
    fourth_grad = jacobian_of(third_grad)

    def single(vector):
        return (inverse_distance(vector).reshape(1), first_grad(vector).reshape(-1), second_grad(vector).reshape(-1), third_grad(vector).reshape(-1), fourth_grad(vector).reshape(-1))
    return jax.vmap(single)(separation)

def mutual_locals(moments_a, moments_b, separation):
    tensors = derivative_tensors(separation)
    pair_count = separation.shape[0]
    locals_a = []
    locals_b = []
    for degree in range(5):
        summed_a = jnp.zeros((pair_count, 3 ** degree), jnp.float32)
        summed_b = jnp.zeros((pair_count, 3 ** degree), jnp.float32)
        for source in range(5 - degree):
            tensor_block = tensors[source + degree].reshape(pair_count, 3 ** source, 3 ** degree)
            piece_b = moments_b[:, tensor_offsets[source]:tensor_offsets[source + 1]]
            piece_a = moments_a[:, tensor_offsets[source]:tensor_offsets[source + 1]]
            summed_a = summed_a + (-1.0) ** source / factorials[source] * jnp.einsum('pa,pab->pb', piece_b, tensor_block, precision=lax.Precision.HIGHEST)
            summed_b = summed_b + 1.0 / factorials[source] * jnp.einsum('pa,pab->pb', piece_a, tensor_block, precision=lax.Precision.HIGHEST)
        locals_a.append(-summed_a)
        locals_b.append(-(-1.0) ** degree * summed_b)
    return (jnp.concatenate(locals_a, 1), jnp.concatenate(locals_b, 1))

def shift_locals(parent_terms, offset):
    powers = outer_powers(offset)
    result = []
    for degree in range(5):
        summed = jnp.zeros((3 ** degree,) + offset.shape[1:], jnp.float32)
        for source in range(degree, 5):
            spacing = source - degree
            tensor_block = parent_terms[tensor_offsets[source]:tensor_offsets[source + 1]].reshape((3 ** spacing, 3 ** degree) + offset.shape[1:])
            summed = summed + lax.optimization_barrier(jnp.sum(tensor_block * powers[spacing][:, None], 0)) / factorials[spacing]
        result.append(summed)
    return jnp.concatenate(result, 0)

def evaluate_locals(leaf_terms, powers):
    cell_count = leaf_terms.shape[1]
    potential = jnp.zeros(powers[0].shape[1:], jnp.float32)
    accel = jnp.zeros((3,) + powers[0].shape[1:], jnp.float32)
    for degree in range(5):
        tensor_block = leaf_terms[tensor_offsets[degree]:tensor_offsets[degree + 1]]
        potential = potential + lax.optimization_barrier(jnp.sum(tensor_block[:, :, None] * powers[degree], 0)) / factorials[degree]
        if degree < 4:
            upper = leaf_terms[tensor_offsets[degree + 1]:tensor_offsets[degree + 2]].reshape(3 ** degree, 3, cell_count)
            accel = accel - lax.optimization_barrier(jnp.sum(upper[:, :, :, None] * powers[degree][:, None], 0)) / factorials[degree]
    return jnp.concatenate([potential[None], accel], 0)

def pair_block(place_a, weight_a, place_b, weight_b):
    spacing = place_a[:, :, None] - place_b[:, None, :]
    inverse = lax.rsqrt(lax.optimization_barrier(jnp.sum(spacing * spacing, 0)) + soft_square)
    cubed = inverse * inverse * inverse
    potential_a = -lax.optimization_barrier(jnp.sum(weight_b[None, :] * inverse, 1))
    potential_b = -lax.optimization_barrier(jnp.sum(weight_a[:, None] * inverse, 0))
    accel_a = -lax.optimization_barrier(jnp.sum(spacing * (weight_b[None, :] * cubed)[None], 2))
    accel_b = lax.optimization_barrier(jnp.sum(spacing * (weight_a[:, None] * cubed)[None], 1))
    return (jnp.concatenate([potential_a[None], accel_a], 0), jnp.concatenate([potential_b[None], accel_b], 0))

def self_block(places, weight_row):
    slot_count = weight_row.shape[0]
    spacing = places[:, :, None] - places[:, None, :]
    apart = lax.broadcasted_iota(jnp.int32, (slot_count, slot_count), 0) != lax.broadcasted_iota(jnp.int32, (slot_count, slot_count), 1)
    inverse = jnp.where(apart, lax.rsqrt(lax.optimization_barrier(jnp.sum(spacing * spacing, 0)) + soft_square), 0.0)
    cubed = inverse * inverse * inverse
    potential = -lax.optimization_barrier(jnp.sum(weight_row[None, :] * inverse, 1))
    accel = -lax.optimization_barrier(jnp.sum(spacing * (weight_row[None, :] * cubed)[None], 2))
    return jnp.concatenate([potential[None], accel], 0)

def self_work(body_data):
    leaf_total = body_data.shape[1]
    leaf_size = body_data.shape[2]
    grouped = body_data.reshape(4, leaf_total // 8, 8, leaf_size).transpose(1, 0, 2, 3)

    def one_group(bundle):
        return jax.vmap(self_block, in_axes=(1, 0))(bundle[:3], bundle[3])
    fields = lax.map(one_group, grouped)
    return fields.reshape(leaf_total, 4, leaf_size).transpose(1, 0, 2)

def near_work(table_bodies, pair_list):
    owned_ids = pair_list[0]
    partner_ids = jnp.maximum(pair_list[1], 0)
    active = pair_list[1] >= 0
    z_lift = pair_list[2].astype(jnp.float32) * CZ
    pair_count = owned_ids.shape[0]

    def one_group(bundle):
        ids_a, ids_b, lifts, actives = bundle
        place_a = jnp.take(table_bodies[:3], ids_a, axis=1)
        place_b = jnp.take(table_bodies[:3], ids_b, axis=1)
        place_b = place_b.at[2].add(lifts[:, None])
        weight_a = jnp.take(table_bodies[3], ids_a, axis=0)
        weight_b = jnp.take(table_bodies[3], ids_b, axis=0)
        part_a, part_b = jax.vmap(pair_block, in_axes=(1, 0, 1, 0))(place_a, weight_a, place_b, weight_b)
        keeper = actives[:, None, None]
        return (jnp.where(keeper, part_a, 0.0), jnp.where(keeper, part_b, 0.0))

    def shaped(values):
        return values.reshape(pair_count // 8, 8)
    part_a, part_b = lax.map(one_group, (shaped(owned_ids), shaped(partner_ids), shaped(z_lift), shaped(active)))
    part_a = part_a.reshape(pair_count, 4, -1).transpose(1, 0, 2)
    part_b = part_b.reshape(pair_count, 4, -1).transpose(1, 0, 2)
    summed = jnp.zeros(table_bodies.shape, jnp.float32)
    return summed.at[:, owned_ids].add(part_a).at[:, partner_ids].add(part_b)

def far_work(table_cells, pair_list):
    owned_ids = pair_list[0]
    partner_ids = jnp.maximum(pair_list[1], 0)
    active = pair_list[1] >= 0
    z_lift = pair_list[2].astype(jnp.float32) * CZ
    centre_a = jnp.take(table_cells[121:], owned_ids, axis=1)
    centre_b = jnp.take(table_cells[121:], partner_ids, axis=1)
    centre_b = centre_b.at[2].add(z_lift)
    separation = jnp.where(active[None], centre_a - centre_b, 3.0).T
    moments_a = jnp.take(table_cells[:121], owned_ids, axis=1).T
    moments_b = jnp.take(table_cells[:121], partner_ids, axis=1).T
    locals_a, locals_b = mutual_locals(moments_a, moments_b, separation)
    locals_a = jnp.where(active[:, None], locals_a, 0.0)
    locals_b = jnp.where(active[:, None], locals_b, 0.0)
    summed = jnp.zeros((121, table_cells.shape[1]), jnp.float32)
    return summed.at[:, owned_ids].add(locals_a.T).at[:, partner_ids].add(locals_b.T)

def geometry(slab_at, sub_at):
    leaf_ids = jnp.arange(CX * CY * CZ, dtype=jnp.int32)
    cell_x = leaf_ids // (CY * CZ)
    cell_y = leaf_ids // CZ % CY
    cell_z = leaf_ids % CZ
    base_x = slab_at * CX
    base_y = sub_at * CY
    centres = jnp.stack([base_x + cell_x, base_y + cell_y, cell_z]).astype(jnp.float32) + 0.5
    half_y = CY // 2
    half_z = CZ // 2
    parent_of = (cell_x // 2 * half_y + cell_y // 2) * half_z + cell_z // 2
    parent_ids = jnp.arange(CX // 2 * half_y * half_z, dtype=jnp.int32)
    parent_x = parent_ids // (half_y * half_z)
    parent_y = parent_ids // half_z % half_y
    parent_z = parent_ids % half_z
    parent_centres = jnp.stack([base_x + 2 * parent_x, base_y + 2 * parent_y, 2 * parent_z]).astype(jnp.float32) + 1.0
    return (centres, parent_centres, parent_of)

def image_shift(slab_at, sub_at, slab_count, sub_count):
    rows_out = []
    for direction in range(4):
        reach_x = slab_at + slab_steps[direction]
        reach_y = sub_at + sub_steps[direction]
        jump_x = (reach_x - reach_x % slab_count) * CX
        jump_y = (reach_y - reach_y % sub_count) * CY
        rows_out.append(jnp.stack([jump_x, jump_y, jnp.zeros_like(jump_x)]))
    return jnp.stack(rows_out).astype(jnp.float32)

def neighbour_ranks(slab_at, sub_at, slab_count, sub_count, facing):
    return jnp.stack([(slab_at + facing * slab_steps[direction]) % slab_count * sub_count + (sub_at + facing * sub_steps[direction]) % sub_count for direction in range(4)]).astype(jnp.int32)

def device_front(positions, masses, leaf_counts, send_leaves, send_parents, slab_at, sub_at):
    leaf_total = leaf_counts.shape[0]
    leaf_size = masses.shape[0] // leaf_total
    places = positions.reshape(3, leaf_total, leaf_size)
    filled = lax.broadcasted_iota(jnp.int32, (leaf_total, leaf_size), 1) < leaf_counts[:, None]
    weights = jnp.where(filled, masses.reshape(leaf_total, leaf_size), 0.0)
    centres, parent_centres, parent_of = geometry(slab_at, sub_at)
    parent_total = parent_centres.shape[1]
    leaf_powers = outer_powers(places - centres[:, :, None])
    moments = lax.optimization_barrier(jnp.sum(jnp.concatenate(leaf_powers, 0) * weights[None], 2))
    parent_powers = jnp.concatenate(outer_powers(places - jnp.take(parent_centres, parent_of, axis=1)[:, :, None]), 0)
    per_leaf = lax.optimization_barrier(jnp.sum(parent_powers * weights[None], 2))
    belongs = (parent_of[:, None] == jnp.arange(parent_total, dtype=jnp.int32)[None, :]).astype(jnp.float32)
    parent_moments = jnp.dot(per_leaf, belongs, precision=lax.Precision.HIGHEST)
    body_data = jnp.concatenate([places, weights[None]], 0)
    leaf_rows = jnp.concatenate([moments, centres], 0)
    parent_rows = jnp.concatenate([parent_moments, parent_centres], 0)
    sent_leaf = send_leaves.reshape(4, -1)
    sent_parent = send_parents.reshape(4, -1)
    out_bodies = jnp.take(body_data, sent_leaf, axis=1).transpose(1, 0, 2, 3).reshape(4, -1)
    out_leaf = jnp.take(leaf_rows, sent_leaf, axis=1).transpose(1, 0, 2).reshape(4, -1)
    out_parent = jnp.take(parent_rows, sent_parent, axis=1).transpose(1, 0, 2).reshape(4, -1)
    outgoing = jnp.concatenate([out_bodies, out_leaf, out_parent], 1)
    return (filled, leaf_powers, body_data, leaf_rows, parent_rows, centres, parent_centres, parent_of, sent_leaf, sent_parent, outgoing)

def device_middle(body_data, leaf_rows, parent_rows, incoming, image, near_list, far_list, parent_list):
    leaf_total = body_data.shape[1]
    leaf_size = body_data.shape[2]
    parent_total = parent_rows.shape[1]
    slots = leaf_total // 4
    parent_slots = parent_total // 2
    cut_a = 4 * slots * leaf_size
    cut_b = cut_a + 124 * slots
    body_lift = jnp.concatenate([image, jnp.zeros((4, 1), jnp.float32)], 1)
    cell_lift = jnp.concatenate([jnp.zeros((4, 121), jnp.float32), image], 1)
    in_bodies = incoming[:, :cut_a].reshape(4, 4, slots, leaf_size) + body_lift[:, :, None, None]
    in_leaf = incoming[:, cut_a:cut_b].reshape(4, 124, slots) + cell_lift[:, :, None]
    in_parent = incoming[:, cut_b:].reshape(4, 124, parent_slots) + cell_lift[:, :, None]
    table_bodies = jnp.concatenate([body_data, in_bodies.transpose(1, 0, 2, 3).reshape(4, 4 * slots, leaf_size)], 1)
    table_leaf = jnp.concatenate([leaf_rows, in_leaf.transpose(1, 0, 2).reshape(124, 4 * slots)], 1)
    table_parent = jnp.concatenate([parent_rows, in_parent.transpose(1, 0, 2).reshape(124, 4 * parent_slots)], 1)
    near_table = near_work(table_bodies, near_list)
    local_near = near_table[:, :leaf_total] + self_work(body_data)
    leaf_table = far_work(table_leaf, far_list)
    parent_table = far_work(table_parent, parent_list)
    back_bodies = near_table[:, leaf_total:].reshape(4, 4, slots, leaf_size).transpose(1, 0, 2, 3).reshape(4, -1)
    back_leaf = leaf_table[:, leaf_total:].reshape(121, 4, slots).transpose(1, 0, 2).reshape(4, -1)
    back_parent = parent_table[:, parent_total:].reshape(121, 4, parent_slots).transpose(1, 0, 2).reshape(4, -1)
    returning = jnp.concatenate([back_bodies, back_leaf, back_parent], 1)
    return (returning, local_near, leaf_table[:, :leaf_total], parent_table[:, :parent_total])

def device_back(local_near, leaf_terms, parent_terms, arrived, sent_leaf, sent_parent, leaf_powers, centres, parent_centres, parent_of, filled):
    leaf_size = local_near.shape[2]
    slots = sent_leaf.shape[1]
    cut_a = 4 * slots * leaf_size
    cut_b = cut_a + 121 * slots
    flat_leaf = sent_leaf.reshape(-1)
    flat_parent = sent_parent.reshape(-1)
    got_bodies = arrived[:, :cut_a].reshape(4, 4, slots, leaf_size).transpose(1, 0, 2, 3).reshape(4, 4 * slots, leaf_size)
    got_leaf = arrived[:, cut_a:cut_b].reshape(4, 121, slots).transpose(1, 0, 2).reshape(121, -1)
    got_parent = arrived[:, cut_b:].reshape(4, 121, -1).transpose(1, 0, 2).reshape(121, -1)
    local_near = local_near.at[:, flat_leaf].add(got_bodies)
    leaf_terms = leaf_terms.at[:, flat_leaf].add(got_leaf)
    parent_terms = parent_terms.at[:, flat_parent].add(got_parent)
    leaf_terms = leaf_terms + shift_locals(jnp.take(parent_terms, parent_of, axis=1), centres - jnp.take(parent_centres, parent_of, axis=1))
    result = evaluate_locals(leaf_terms, leaf_powers) + local_near
    result = jnp.where(filled[None], result, 0.0)
    return result.reshape(4, -1)

def reference(positions, masses, leaf_counts, send_leaves, send_parents, near_pairs, far_pairs, parent_pairs):
    devices = N_SLAB * N_SUB
    per_device = masses.shape[0] // devices
    leaf_total = leaf_counts.shape[0] // devices
    place_blocks = positions.reshape(3, devices, per_device).transpose(1, 0, 2)
    mass_blocks = masses.reshape(devices, per_device)
    count_blocks = leaf_counts.reshape(devices, leaf_total)
    device_ids = jnp.arange(devices, dtype=jnp.int32)
    directions = jnp.arange(4, dtype=jnp.int32)

    def front(device_id):
        slab_at = device_id // N_SUB
        sub_at = device_id % N_SUB
        return device_front(place_blocks[device_id], mass_blocks[device_id], count_blocks[device_id], send_leaves[device_id], send_parents[device_id], slab_at, sub_at)

    def front_outgoing(device_id):
        return front(device_id)[-1]
    outgoing_all = lax.map(front_outgoing, device_ids)

    def middle(device_id):
        parts = front(device_id)
        slab_at = device_id // N_SUB
        sub_at = device_id % N_SUB
        sources = neighbour_ranks(slab_at, sub_at, N_SLAB, N_SUB, 1)
        incoming = outgoing_all[sources, directions]
        image = image_shift(slab_at, sub_at, N_SLAB, N_SUB)
        return device_middle(parts[2], parts[3], parts[4], incoming, image, near_pairs[device_id], far_pairs[device_id], parent_pairs[device_id])
    returning_all, near_all, leaf_all, parent_all = lax.map(middle, device_ids)

    def back(device_id):
        parts = front(device_id)
        slab_at = device_id // N_SUB
        sub_at = device_id % N_SUB
        targets = neighbour_ranks(slab_at, sub_at, N_SLAB, N_SUB, -1)
        arrived = returning_all[targets, directions]
        return device_back(near_all[device_id], leaf_all[device_id], parent_all[device_id], arrived, parts[8], parts[9], parts[1], parts[5], parts[6], parts[7], parts[0])
    fields = lax.map(back, device_ids)
    return fields.transpose(1, 0, 2).reshape(4, -1)
```

```python
import functools
import math

import jax
import jax.numpy as jnp
import numpy as np
from jax import lax
from jax.experimental import pallas as pl
from jax.experimental.pallas import tpu as pltpu
from jax.sharding import PartitionSpec as P

CX = 2
CY = 4
CZ = 32

soft_square = 0.0025
slab_steps = (1, 0, 1, 1)
sub_steps = (0, 1, 1, -1)

LEAVES = CX * CY * CZ
PARENTS = LEAVES // 8
SLOTS = LEAVES // 4
PSLOTS = PARENTS // 2
HALF = 128
LEAF = 2 * HALF
BODY_ROWS = 8 * SLOTS
PACK_ROWS = BODY_ROWS + SLOTS + PSLOTS
GROUP = 8
bf16 = jnp.bfloat16
f32 = jnp.float32
i32 = jnp.int32

MULTI = [
    (i, j, n - i - j) for n in range(5) for i in range(n, -1, -1) for j in range(n - i, -1, -1)
]
PLACE = {alpha: at for at, alpha in enumerate(MULTI)}
TERMS = len(MULTI)
CENTRE = TERMS
FEATS = 40
OWN = LEAVES + PARENTS
ENTRIES = 640
FAR_BLOCKS = 9


def fact(alpha):
    return math.prod(math.factorial(a) for a in alpha)


def added(alpha, beta):
    return tuple(a + b for a, b in zip(alpha, beta))


def taken(alpha, beta):
    return tuple(a - b for a, b in zip(alpha, beta))


def octant(at):
    return tuple(0.5 if bit else -0.5 for bit in (at >> 2 & 1, at >> 1 & 1, at & 1))


def power(delta, alpha):
    return math.prod(d**a for d, a in zip(delta, alpha))


def shift_matrices():
    up = np.zeros((8, 128, 128), np.float32)
    down = np.zeros((8, 128, 128), np.float32)
    for at in range(8):
        delta = octant(at)
        for alpha in MULTI:
            for beta in MULTI:
                rest = taken(alpha, beta)
                if min(rest) < 0:
                    continue
                choose = math.prod(math.comb(a, b) for a, b in zip(alpha, beta))
                up[at, PLACE[beta], PLACE[alpha]] = choose * power(delta, rest)
                down[at, PLACE[alpha], PLACE[beta]] = power(delta, rest) / fact(rest)
    return up.reshape(8 * 128, 128), down.transpose(1, 0, 2).reshape(128, 8 * 128)


UP, DOWN = shift_matrices()


def row_ids(shape):
    return lax.broadcasted_iota(i32, shape, 0)


def lane_ids(shape):
    return lax.broadcasted_iota(i32, shape, 1)


def monomials(x, y, z):
    table = {(0, 0, 0): None}
    axes = (x, y, z)
    for alpha in MULTI[1:]:
        lead = max(axis for axis in range(3) if alpha[axis])
        less = tuple(a - (axis == lead) for axis, a in enumerate(alpha))
        table[alpha] = axes[lead] if table[less] is None else table[less] * axes[lead]
    return table


def split3(value):
    high = value.astype(bf16).astype(f32)
    rest = value - high
    middle = rest.astype(bf16).astype(f32)
    return high, middle, rest - middle


def spread(tile):
    row = row_ids((8, HALF))
    turned = pltpu.roll(tile, 4, 0)
    low = row < 4
    return jnp.concatenate([jnp.where(low, tile, turned), jnp.where(low, turned, tile)], 1)


def fold(field):
    row = row_ids((8, HALF))
    return jnp.where(row < 4, field[:, :HALF], pltpu.roll(field[:, HALF:], 4, 0))


def offset_rows(ox, oy, oz):
    row = row_ids((8, LEAF)) & 3
    return jnp.where(row == 1, ox, jnp.where(row == 2, oy, jnp.where(row == 3, oz, 0.0)))


def features(tile, offset, as_row, as_column, as_weight):
    wide = spread(tile)
    row = row_ids((8, LEAF))
    first = (row & 3) == 0
    low = row < 4
    weight = jnp.broadcast_to(wide[0:1], (8, LEAF))
    x = jnp.where(first, 0.0, wide + offset)
    square = x * x
    pairwise = square + pltpu.roll(square, 1, 0)
    q = pairwise + pltpu.roll(pairwise, 2, 0)
    y = jnp.where(first, q, x)
    zero = jnp.zeros((8, LEAF), f32)
    out = [x, q]
    if as_row:
        h, m, l = split3(y)
        part_a = jnp.where(row == 4, m, h)
        part_b = jnp.where(row == 0, l, jnp.where(row == 4, 1.0, m))
        part_c = jnp.where(first, 1.0, jnp.where(low, h, l))
        out.append(jnp.concatenate([part_a, part_b, part_c, zero], 0).astype(bf16))
    if as_column:
        h, m, l = split3(jnp.where(first, q + soft_square, x * -2.0))
        mixed = jnp.where(low, h, m)
        part_a = jnp.where(first, 1.0, mixed)
        part_b = jnp.where(row == 0, 1.0, jnp.where(row == 4, h, mixed))
        part_c = jnp.where(row == 0, m, jnp.where(row == 4, l, jnp.where(low, l, h)))
        out.append(jnp.concatenate([part_a, part_b, part_c, zero], 0).astype(bf16))
    if as_weight:
        heavy = jnp.where(low, y, 1.0) * weight
        out.append(jnp.concatenate(list(split3(heavy)) + [zero], 0).astype(bf16))
    return out


def field_of(sums, x, q):
    total = sums[0:8] + sums[8:16] + sums[16:24]
    row = row_ids((8, LEAF))
    first = (row & 3) == 0
    plain = pltpu.roll(total, 4, 0)
    inner = total - jnp.where(first, q - soft_square, x) * plain
    along = x * inner
    dots = along[1:2] + along[2:3] + along[3:4]
    return fold(jnp.where(row == 0, 2.0 * dots - inner, inner))


def cubes(row_part, column_part):
    square = lax.dot_general(
        row_part, column_part, (((0,), (0,)), ((), ())), preferred_element_type=f32
    )
    inverse = lax.rsqrt(square)
    return inverse * inverse * inverse


def padded(sums):
    lanes = sums.shape[1]
    if lanes == LEAF:
        return sums
    return jnp.concatenate([sums, jnp.zeros((sums.shape[0], LEAF - lanes), f32)], 1)


def pipeline(count, group, early, late):
    @pl.when(count > 0)
    def _():
        for u in range(group):
            early(0, 0, u)

        def step(k, carry):
            for slot in range(2):
                done = []
                for u in range(group):
                    done.append(late(2 * k + slot, slot, u))
                    early(2 * k + slot + 1, 1 - slot, u)
                for store in done:
                    store()
            return carry

        lax.fori_loop(0, (count + 2 * group - 1) // (2 * group), step, 0)


def leaf_centre(place, leaf):
    return (
        -(place[0] + leaf // (CY * CZ)).astype(f32) - 0.5,
        -(place[1] + leaf // CZ % CY).astype(f32) - 0.5,
        -(leaf % CZ).astype(f32) - 0.5,
    )


def self_loop(words, at, count, group, size, place, bodies, field, scratch):
    cube_refs, weight_refs, spot_refs = scratch

    def early(k, slot, u):
        leaf = words[at, k * group + u]
        x, q, rows, columns, weights = features(
            bodies[leaf], offset_rows(*leaf_centre(place, leaf & (LEAVES - 1))), True, True, True
        )
        c = cubes(rows[:, :size], columns[:, :size])
        c = jnp.where(row_ids((size, size)) == lane_ids((size, size)), 0.0, c)
        high = c.astype(bf16)
        cube_refs[slot][u, :size, :size] = high
        cube_refs[slot][u, size : 2 * size, :size] = (c - high.astype(f32)).astype(bf16)
        weight_refs[slot][u, :, :size] = weights[:, :size]
        spot_refs[slot][u, 0] = x
        spot_refs[slot][u, 1] = q

    def late(k, slot, u):
        leaf = words[at, k * group + u]
        w = weight_refs[slot][u, :, :size]
        sums = jnp.dot(
            jnp.concatenate([w, w], 1),
            cube_refs[slot][u, : 2 * size, :size],
            preferred_element_type=f32,
        )
        result = field_of(padded(sums), spot_refs[slot][u, 0], spot_refs[slot][u, 1])

        def store():
            field[leaf] = field[leaf] + result

        return store

    pipeline(count, group, early, late)


def pair_loop(words, at, count, group, size, place, bodies, others, field, other_field, scratch):
    cube_refs, row_refs, column_refs, spot_refs = scratch
    turned = (((1,), (1,)), ((), ()))

    def unpack(k, u):
        word = words[at, k * group + u]
        return word & 511, word >> 9 & 511, word >> 18 & 1, (word >> 19 & 3) - 1, word >> 21 & 7

    def early(k, slot, u):
        row_leaf, column_leaf, swapped, lift, way = unpack(k, u)
        frame = jnp.where(swapped == 1, column_leaf, row_leaf) & (LEAVES - 1)
        cx, cy, cz = leaf_centre(place, frame)
        raised = (lift * CZ).astype(f32)
        swap = (swapped == 1).astype(f32)
        jump_x = place[2 + 2 * way].astype(f32)
        jump_y = place[3 + 2 * way].astype(f32)
        row_offset = offset_rows(cx, cy, cz + swap * raised)
        column_offset = offset_rows(cx + jump_x, cy + jump_y, cz + (1.0 - swap) * raised)
        xr, qr, rows, row_weights = features(bodies[row_leaf], row_offset, True, False, True)
        xc, qc, columns, column_weights = features(
            others[column_leaf], column_offset, False, True, True
        )
        c = cubes(rows[:, :size], columns)
        high = c.astype(bf16)
        cube_refs[slot][u, :size] = high
        cube_refs[slot][u, size : 2 * size] = (c - high.astype(f32)).astype(bf16)
        row_refs[slot][u, :, :size] = row_weights[:, :size]
        column_refs[slot][u] = column_weights
        spot_refs[slot][u, 0] = xr
        spot_refs[slot][u, 1] = qr
        spot_refs[slot][u, 2] = xc
        spot_refs[slot][u, 3] = qc

    def late(k, slot, u):
        row_leaf, column_leaf, _, _, _ = unpack(k, u)
        wr = row_refs[slot][u, :, :size]
        wc = column_refs[slot][u]
        column_sums = jnp.dot(
            jnp.concatenate([wr, wr], 1),
            cube_refs[slot][u, : 2 * size],
            preferred_element_type=f32,
        )
        row_sums = lax.dot_general(
            wc, cube_refs[slot][u, :size], turned, preferred_element_type=f32
        ) + lax.dot_general(
            wc, cube_refs[slot][u, size : 2 * size], turned, preferred_element_type=f32
        )
        row_field = field_of(padded(row_sums), spot_refs[slot][u, 0], spot_refs[slot][u, 1])
        column_field = field_of(column_sums, spot_refs[slot][u, 2], spot_refs[slot][u, 3])

        def store():
            field[row_leaf] = field[row_leaf] + row_field
            other_field[column_leaf] = other_field[column_leaf] + column_field

        return store

    pipeline(count, group, early, late)


def pair_scratch(group):
    return (
        [pltpu.VMEM((group, 2 * LEAF, LEAF), bf16)] * 2
        + [pltpu.VMEM((group, 32, LEAF), bf16)] * 2
        + [pltpu.VMEM((group, 32, LEAF), bf16)] * 2
        + [pltpu.VMEM((group, 4, 8, LEAF), f32)] * 2
    )


def paired(scratch):
    return [scratch[0:2], scratch[2:4], scratch[4:6], scratch[6:8]]


def front_kernel(place, send, send_p, spots, weights, up, bodies, moments, parents, *outs):
    def group_step(g, carry):
        rows = pl.ds(pl.multiple_of(8 * g, 8), 8)
        w = weights[rows, :]
        px = spots[0, rows, :]
        py = spots[1, rows, :]
        pz = spots[2, rows, :]
        for at, value in enumerate((w, px, py, pz)):
            bodies[pl.ds(64 * g + at, 8, stride=8), :] = value[:, :HALF]
            bodies[pl.ds(64 * g + 4 + at, 8, stride=8), :] = value[:, HALF:]
        cx = (place[0] + g // (CY * CZ // 8)).astype(f32) + 0.5
        cy = (place[1] + g // (CZ // 8) % CY).astype(f32) + 0.5
        base_z = (8 * (g % (CZ // 8))).astype(f32) + 0.5
        cz = row_ids((8, 1)).astype(f32) + base_z
        x, y, z = px - cx, py - cy, pz - cz
        table = {(0, 0, 0): w}
        axes = (x, y, z)
        lane = lane_ids((8, 128))
        built = jnp.zeros((8, 128), f32)
        for alpha in MULTI:
            if alpha not in table:
                lead = max(axis for axis in range(3) if alpha[axis])
                less = tuple(a - (axis == lead) for axis, a in enumerate(alpha))
                table[alpha] = table[less] * axes[lead]
            value = table[alpha]
            total = jnp.sum(value[:, :HALF] + value[:, HALF:], axis=1, keepdims=True)
            built = jnp.where(lane == PLACE[alpha], total, built)
        built = jnp.where(lane == CENTRE, cx, built)
        built = jnp.where(lane == CENTRE + 1, cy, built)
        built = jnp.where(lane == CENTRE + 2, cz, built)
        moments[rows, :] = built
        return carry

    lax.fori_loop(0, LEAVES // 8, group_step, 0, unroll=2)
    row = row_ids((8, HALF)) & 3
    bx = place[0].astype(f32) + 0.5
    by = place[1].astype(f32) + 0.5
    bodies[8 * LEAVES : 8 * LEAVES + 8, :] = jnp.where(
        row == 1, bx, jnp.where(row == 2, by, jnp.where(row == 3, 0.5, 0.0))
    )
    half_z = CZ // 2
    summed = jnp.zeros((PARENTS, 128), f32)
    for at in range(8):
        first = (at >> 2 & 1) * CY * CZ + (at >> 1 & 1) * CZ + (at & 1)
        piece = jnp.concatenate(
            [moments[pl.ds(first + 2 * CZ * py, half_z, stride=2), :] for py in range(CY // 2)], 0
        )
        summed = summed + jnp.dot(
            piece,
            up[128 * at : 128 * at + 128, :],
            precision=lax.Precision.HIGHEST,
            preferred_element_type=f32,
        )
    lane = lane_ids((PARENTS, 128))
    cell = row_ids((PARENTS, 128))
    summed = jnp.where(lane == CENTRE, place[0].astype(f32) + 1.0, summed)
    summed = jnp.where(
        lane == CENTRE + 1,
        place[1].astype(f32) + 1.0 + 2.0 * (cell // half_z).astype(f32),
        summed,
    )
    summed = jnp.where(lane == CENTRE + 2, 1.0 + 2.0 * (cell % half_z).astype(f32), summed)
    parents[...] = summed
    for way in range(4):

        def leaf_step(k, carry, way=way):
            leaf = send[0, way * SLOTS + k]
            outs[way][pl.ds(pl.multiple_of(8 * k, 8), 8), :] = bodies[
                pl.ds(pl.multiple_of(8 * leaf, 8), 8), :
            ]
            outs[way][pl.ds(BODY_ROWS + k, 1), :] = moments[pl.ds(leaf, 1), :]
            return carry

        lax.fori_loop(0, SLOTS, leaf_step, 0, unroll=8)

        def parent_step(k, carry, way=way):
            cell = send_p[0, way * PSLOTS + k]
            outs[way][pl.ds(BODY_ROWS + SLOTS + k, 1), :] = parents[pl.ds(cell, 1), :]
            return carry

        lax.fori_loop(0, PSLOTS, parent_step, 0, unroll=8)


def fill_tail(words, at, count, word, length):
    def step(k, carry):
        words[at, count + k] = word
        return carry

    lax.fori_loop(0, length, step, 0, unroll=8)


def self_kernel(place, counts, bodies, field, words, *scratch):
    field[...] = jnp.zeros_like(field)

    def sort_step(leaf, taken_so_far):
        short, long = taken_so_far
        is_short = counts[leaf] <= HALF
        at = jnp.where(is_short, 0, 1)
        words[at, jnp.where(is_short, short, long)] = leaf
        return jnp.where(is_short, short + 1, short), jnp.where(is_short, long, long + 1)

    short, long = lax.fori_loop(0, LEAVES, sort_step, (jnp.int32(0), jnp.int32(0)), unroll=8)
    fill_tail(words, 0, short, LEAVES, 3 * GROUP)
    fill_tail(words, 1, long, LEAVES, 3 * GROUP)
    refs = (scratch[0:2], scratch[2:4], scratch[4:6])
    self_loop(words, 0, short, GROUP, HALF, place, bodies, field, refs)
    self_loop(words, 1, long, GROUP, LEAF, place, bodies, field, refs)


def near_kernel(place, counts, pairs, bodies, field_in, field, words, *scratch):
    field[...] = field_in[...]

    def sort_step(k, taken_so_far):
        short, long = taken_so_far
        a = pairs[0, 0, k]
        b = pairs[0, 1, k]
        own = jnp.logical_and(b >= 0, b < LEAVES)
        b = jnp.where(own, b, 0)
        count_a = counts[a]
        count_b = counts[b]
        swapped = jnp.where(count_b < count_a, 1, 0)
        row_leaf = jnp.where(swapped == 1, b, a)
        column_leaf = jnp.where(swapped == 1, a, b)
        word = row_leaf | column_leaf << 9 | swapped << 18 | (pairs[0, 2, k] + 1) << 19 | 4 << 21
        is_short = jnp.minimum(count_a, count_b) <= HALF
        at = jnp.where(own, jnp.where(is_short, 0, 1), 2)
        words[at, jnp.where(is_short, short, long)] = word
        short = jnp.where(at == 0, short + 1, short)
        long = jnp.where(at == 1, long + 1, long)
        return short, long

    short, long = lax.fori_loop(
        0, pairs.shape[2], sort_step, (jnp.int32(0), jnp.int32(0)), unroll=8
    )
    empty = LEAVES << 9 | 1 << 19 | 4 << 21
    fill_tail(words, 0, short, empty, 3 * GROUP)
    fill_tail(words, 1, long, empty, 3 * GROUP)
    refs = paired(scratch)
    pair_loop(words, 0, short, GROUP, HALF, place, bodies, bodies, field, field, refs)
    pair_loop(words, 1, long, GROUP, LEAF, place, bodies, bodies, field, field, refs)


def derivatives(x, y, z):
    inverse = lax.rsqrt(x * x + y * y + z * z)
    square = inverse * inverse
    odd = [inverse]
    for _ in range(4):
        odd.append(odd[-1] * square)
    powers = monomials(x, y, z)
    result = {}
    for alpha in MULTI:
        degree = sum(alpha)
        total = None
        for p in range(alpha[0] // 2 + 1):
            for q in range(alpha[1] // 2 + 1):
                for s in range(alpha[2] // 2 + 1):
                    m = p + q + s
                    ways = math.prod(
                        math.factorial(a) // (2**c * math.factorial(c) * math.factorial(a - 2 * c))
                        for a, c in zip(alpha, (p, q, s))
                    )
                    sign = (-1.0) ** (degree - m)
                    double = math.prod(range(1, 2 * (degree - m), 2))
                    term = odd[degree - m] * (sign * double * ways)
                    rest = (alpha[0] - 2 * p, alpha[1] - 2 * q, alpha[2] - 2 * s)
                    if powers[rest] is not None:
                        term = term * powers[rest]
                    total = term if total is None else total + term
        result[alpha] = total
    return result


def remote_kernel(
    place,
    counts,
    pairs,
    far_a,
    far_b,
    far_lift,
    far_live,
    bodies,
    moments,
    parents,
    in_0,
    in_1,
    in_2,
    in_3,
    field_in,
    field,
    leaf_terms,
    parent_terms,
    out_0,
    out_1,
    out_2,
    out_3,
    words,
    far_bodies,
    far_field,
    gather_a,
    gather_b,
    *scratch,
):
    incoming = (in_0, in_1, in_2, in_3)
    outgoing = (out_0, out_1, out_2, out_3)
    field[...] = field_in[...]
    for way in range(4):
        far_bodies[way * SLOTS : (way + 1) * SLOTS] = incoming[way][:BODY_ROWS, :].reshape(
            SLOTS, 8, HALF
        )
    far_bodies[4 * SLOTS] = bodies[LEAVES]
    far_field[...] = jnp.zeros_like(far_field)

    def sort_step(k, taken_so_far):
        short, long = taken_so_far
        a = pairs[0, 0, k]
        b = pairs[0, 1, k]
        remote = b >= LEAVES
        b = jnp.maximum(b - LEAVES, 0)
        word = a | b << 9 | (pairs[0, 2, k] + 1) << 19 | (b // SLOTS) << 21
        is_short = counts[a] <= HALF
        at = jnp.where(remote, jnp.where(is_short, 0, 1), 2)
        words[at, jnp.where(is_short, short, long)] = word
        short = jnp.where(at == 0, short + 1, short)
        long = jnp.where(at == 1, long + 1, long)
        return short, long

    short, long = lax.fori_loop(
        0, pairs.shape[2], sort_step, (jnp.int32(0), jnp.int32(0)), unroll=8
    )
    empty = (4 * SLOTS) << 9 | 1 << 19 | 4 << 21
    fill_tail(words, 0, short, empty, 3 * GROUP)
    fill_tail(words, 1, long, empty, 3 * GROUP)
    refs = paired(scratch)
    group = GROUP // 2
    pair_loop(words, 0, short, group, HALF, place, bodies, far_bodies, field, far_field, refs)
    pair_loop(words, 1, long, group, LEAF, place, bodies, far_bodies, field, far_field, refs)
    for way in range(4):
        outgoing[way][:BODY_ROWS, :] = far_field[way * SLOTS : (way + 1) * SLOTS].reshape(
            BODY_ROWS, HALF
        )

    def moved(rows, way):
        lane = lane_ids(rows.shape)
        rows = jnp.where(lane == CENTRE, rows + place[2 + 2 * way].astype(f32), rows)
        return jnp.where(lane == CENTRE + 1, rows + place[3 + 2 * way].astype(f32), rows)

    table = [moments[...], parents[...]]
    for way in range(4):
        table.append(moved(incoming[way][BODY_ROWS : BODY_ROWS + SLOTS, :], way))
    for way in range(4):
        table.append(moved(incoming[way][BODY_ROWS + SLOTS :, :], way))
    table.append(jnp.zeros((ENTRIES - OWN - 4 * SLOTS - 4 * PSLOTS, 128), f32))
    columns = jnp.concatenate(table, 0).T[:FEATS]
    columns = jnp.concatenate(split3(columns), 0).astype(bf16)

    def one_hot(index, entries):
        return jnp.where(row_ids((entries, 128)) == index, 1.0, 0.0).astype(bf16)

    def joined(parts):
        return parts[:FEATS] + parts[FEATS : 2 * FEATS] + parts[2 * FEATS :]

    gather_a[...] = jnp.zeros_like(gather_a)
    gather_b[...] = jnp.zeros_like(gather_b)
    for block in range(FAR_BLOCKS):
        lanes = slice(128 * block, 128 * block + 128)
        rows = slice(FEATS * block, FEATS * block + FEATS)
        hot_a = one_hot(far_a[:, lanes], OWN)
        hot_b = one_hot(far_b[:, lanes], ENTRIES)
        gather_a[rows, :] = joined(jnp.dot(columns[:, :OWN], hot_a, preferred_element_type=f32))
        gather_b[rows, :] = joined(jnp.dot(columns, hot_b, preferred_element_type=f32))
    for chunk in range(2):
        start = 8 * chunk * FEATS

        def feature(ref, at, start=start):
            return ref[pl.ds(start + at, 8, stride=FEATS), :]

        def gap(axis):
            return feature(gather_a, CENTRE + axis) - feature(gather_b, CENTRE + axis)

        part = slice(8 * chunk, 8 * chunk + 8)
        live = far_live[part, :] > 0.0
        x = jnp.where(live, gap(0), 3.0)
        y = jnp.where(live, gap(1), 3.0)
        z = jnp.where(live, gap(2) - far_lift[part, :], 3.0)
        tensors = derivatives(x, y, z)
        held_a = {}
        held_b = {}
        for alpha in MULTI:
            held_a[alpha] = feature(gather_a, PLACE[alpha]) * (-1.0 / fact(alpha))
            held_b[alpha] = feature(gather_b, PLACE[alpha]) * (
                -((-1.0) ** sum(alpha)) / fact(alpha)
            )
        for beta in MULTI:
            to_a = None
            to_b = None
            for alpha in MULTI:
                if sum(alpha) + sum(beta) > 4:
                    continue
                tensor = tensors[added(alpha, beta)]
                term_a = held_b[alpha] * tensor
                term_b = held_a[alpha] * tensor
                to_a = term_a if to_a is None else to_a + term_a
                to_b = term_b if to_b is None else to_b + term_b
            if sum(beta) % 2:
                to_b = -to_b
            gather_a[pl.ds(start + PLACE[beta], 8, stride=FEATS), :] = to_a
            gather_b[pl.ds(start + PLACE[beta], 8, stride=FEATS), :] = to_b
    sums_a = jnp.zeros((3 * FEATS, OWN), f32)
    sums_b = jnp.zeros((3 * FEATS, ENTRIES), f32)
    turned = (((1,), (1,)), ((), ()))
    for block in range(FAR_BLOCKS):
        lanes = slice(128 * block, 128 * block + 128)
        rows = slice(FEATS * block, FEATS * block + FEATS)
        parts_a = jnp.concatenate(split3(gather_a[rows, :]), 0).astype(bf16)
        parts_b = jnp.concatenate(split3(gather_b[rows, :]), 0).astype(bf16)
        hot_a = one_hot(far_a[:, lanes], OWN)
        hot_b = one_hot(far_b[:, lanes], ENTRIES)
        sums_a = sums_a + lax.dot_general(parts_a, hot_a, turned, preferred_element_type=f32)
        sums_b = sums_b + lax.dot_general(parts_b, hot_b, turned, preferred_element_type=f32)
    got_a = jnp.concatenate([joined(sums_a), jnp.zeros((128 - FEATS, OWN), f32)], 0)
    got_b = jnp.concatenate([joined(sums_b), jnp.zeros((128 - FEATS, ENTRIES), f32)], 0)
    keep = lane_ids((1, 128)) < TERMS
    terms_a = jnp.where(keep, got_a.T, 0.0)
    terms_b = jnp.where(keep, got_b.T, 0.0)
    leaf_terms[...] = terms_a[:LEAVES] + terms_b[:LEAVES]
    parent_terms[...] = terms_a[LEAVES:OWN] + terms_b[LEAVES:OWN]
    leaf_start = OWN
    parent_start = OWN + 4 * SLOTS
    for way in range(4):
        first = leaf_start + way * SLOTS
        outgoing[way][BODY_ROWS : BODY_ROWS + SLOTS, :] = terms_b[first : first + SLOTS]
        first = parent_start + way * PSLOTS
        outgoing[way][BODY_ROWS + SLOTS :, :] = terms_b[first : first + PSLOTS]


def back_kernel(
    place,
    counts,
    send,
    send_p,
    spots,
    field_in,
    leaf_in,
    parent_in,
    down,
    in_0,
    in_1,
    in_2,
    in_3,
    out,
    leaf_terms,
    parent_terms,
    field,
    tiles,
):
    incoming = (in_0, in_1, in_2, in_3)
    leaf_terms[...] = leaf_in[...]
    parent_terms[...] = parent_in[...]
    field[...] = field_in[...]
    for way in range(4):

        def leaf_step(k, carry, way=way):
            leaf = send[0, way * SLOTS + k]
            field[leaf] = field[leaf] + incoming[way][pl.ds(pl.multiple_of(8 * k, 8), 8), :]
            leaf_terms[pl.ds(leaf, 1), :] = (
                leaf_terms[pl.ds(leaf, 1), :] + incoming[way][pl.ds(BODY_ROWS + k, 1), :]
            )
            return carry

        lax.fori_loop(0, SLOTS, leaf_step, 0, unroll=8)

        def parent_step(k, carry, way=way):
            cell = send_p[0, way * PSLOTS + k]
            parent_terms[pl.ds(cell, 1), :] = (
                parent_terms[pl.ds(cell, 1), :] + incoming[way][pl.ds(BODY_ROWS + SLOTS + k, 1), :]
            )
            return carry

        lax.fori_loop(0, PSLOTS, parent_step, 0, unroll=8)
    half_z = CZ // 2
    for at in range(8):
        moved = jnp.dot(
            parent_terms[...],
            down[:, 128 * at : 128 * at + 128],
            precision=lax.Precision.HIGHEST,
            preferred_element_type=f32,
        )
        first = (at >> 2 & 1) * CY * CZ + (at >> 1 & 1) * CZ + (at & 1)
        for py in range(CY // 2):
            rows = pl.ds(first + 2 * CZ * py, half_z, stride=2)
            leaf_terms[rows, :] = leaf_terms[rows, :] + moved[half_z * py : half_z * py + half_z]

    def group_step(g, carry):
        rows = pl.ds(pl.multiple_of(8 * g, 8), 8)
        cx = (place[0] + g // (CY * CZ // 8)).astype(f32) + 0.5
        cy = (place[1] + g // (CZ // 8) % CY).astype(f32) + 0.5
        base_z = (8 * (g % (CZ // 8))).astype(f32) + 0.5
        cz = row_ids((8, 1)).astype(f32) + base_z
        x = spots[0, rows, :] - cx
        y = spots[1, rows, :] - cy
        z = spots[2, rows, :] - cz
        terms = leaf_terms[rows, :]
        powers = monomials(x, y, z)
        column = {
            alpha: jnp.broadcast_to(terms[:, PLACE[alpha] : PLACE[alpha] + 1], (8, LEAF))
            for alpha in MULTI
        }
        totals = [None] * 4
        for beta in MULTI:
            scale = 1.0 / fact(beta)
            base = powers[beta]
            if base is not None and scale != 1.0:
                base = base * scale
            kinds = [beta] + (
                [added(beta, unit) for unit in ((1, 0, 0), (0, 1, 0), (0, 0, 1))]
                if sum(beta) < 4
                else []
            )
            for at, kind in enumerate(kinds):
                term = column[kind] if base is None else column[kind] * base
                totals[at] = term if totals[at] is None else totals[at] + term
        values = [totals[0], -totals[1], -totals[2], -totals[3]]
        for at, value in enumerate(values):
            tiles[pl.ds(at, 8, stride=8), :] = value[:, :HALF]
            tiles[pl.ds(4 + at, 8, stride=8), :] = value[:, HALF:]
        row = row_ids((8, HALF))
        body = lane_ids((8, HALF)) + jnp.where(row < 4, 0, HALF)
        for u in range(8):
            leaf = 8 * g + u
            tile = tiles[8 * u : 8 * u + 8, :] + field[leaf]
            tile = jnp.where(body < counts[leaf], tile, 0.0)
            start = pl.multiple_of(leaf * LEAF, LEAF)
            out[:, pl.ds(start, HALF)] = tile[:4]
            out[:, pl.ds(start + HALF, HALF)] = tile[4:]
        return carry

    lax.fori_loop(0, LEAVES // 8, group_step, 0)


VMEM = pl.BlockSpec(memory_space=pltpu.VMEM)
SMEM = pl.BlockSpec(memory_space=pltpu.SMEM)
params = pltpu.CompilerParams(vmem_limit_bytes=56 * 1024 * 1024)
packed = jax.ShapeDtypeStruct((PACK_ROWS, 128), f32)
tiled = jax.ShapeDtypeStruct((LEAVES + 1, 8, HALF), f32)


def shaped(*dims):
    return jax.ShapeDtypeStruct(dims, f32)


def on_device(
    positions, masses, leaf_counts, send_leaves, send_parents, near_pairs, far_pairs, parent_pairs
):
    slab_count = lax.axis_size("slab")
    sub_count = lax.axis_size("sub")
    slab_at = lax.axis_index("slab")
    sub_at = lax.axis_index("sub")
    spots = positions.reshape(3, LEAVES, LEAF)
    filled = lax.broadcasted_iota(i32, (LEAVES, LEAF), 1) < leaf_counts[:, None]
    weights = jnp.where(filled, masses.reshape(LEAVES, LEAF), 0.0)
    numbers = [slab_at * CX, sub_at * CY]
    for way in range(4):
        reach_x = slab_at + slab_steps[way]
        reach_y = sub_at + sub_steps[way]
        numbers.append((reach_x - reach_x % slab_count) * CX)
        numbers.append((reach_y - reach_y % sub_count) * CY)
    zero = jnp.zeros((), i32)
    place = jnp.stack(numbers + [zero] * 6).astype(i32)

    sent = pl.pallas_call(
        front_kernel,
        out_shape=[shaped(8 * LEAVES + 8, HALF), shaped(LEAVES, 128), shaped(PARENTS, 128)]
        + [packed] * 4,
        in_specs=[SMEM, SMEM, SMEM, VMEM, VMEM, VMEM],
        out_specs=[VMEM] * 7,
        compiler_params=params,
        name="moments_and_packing",
    )(place, send_leaves, send_parents, spots, weights, jnp.asarray(UP))
    bodies = sent[0].reshape(LEAVES + 1, 8, HALF)
    moments, parents = sent[1], sent[2]

    def exchange(value, way, back):
        pairs = []
        for s in range(slab_count):
            for u in range(sub_count):
                here = s * sub_count + u
                there = (s + slab_steps[way]) % slab_count * sub_count + (
                    u + sub_steps[way]
                ) % sub_count
                pairs.append((here, there) if back else (there, here))
        return lax.ppermute(value, ("slab", "sub"), pairs)

    incoming = [exchange(sent[3 + way], way, False) for way in range(4)]

    field = pl.pallas_call(
        self_kernel,
        out_shape=tiled,
        in_specs=[SMEM, SMEM, VMEM],
        out_specs=VMEM,
        scratch_shapes=[pltpu.SMEM((2, LEAVES + 4 * GROUP), i32)]
        + [pltpu.VMEM((GROUP, 2 * LEAF, LEAF), bf16)] * 2
        + [pltpu.VMEM((GROUP, 32, LEAF), bf16)] * 2
        + [pltpu.VMEM((GROUP, 2, 8, LEAF), f32)] * 2,
        compiler_params=params,
        cost_estimate=pl.CostEstimate(
            flops=20_000_000_000, bytes_accessed=2_000_000, transcendentals=0
        ),
        name="self_pairs",
    )(place, leaf_counts, bodies)

    def far_row(leaf_part, parent_part, fill):
        count = FAR_BLOCKS * 128 - leaf_part.shape[0] - parent_part.shape[0]
        return jnp.concatenate([leaf_part, parent_part, jnp.full((count,), fill, leaf_part.dtype)])

    far = far_pairs[0]
    cells = parent_pairs[0]
    far_on = far[1] >= 0
    cells_on = cells[1] >= 0
    index_a = far_row(jnp.where(far_on, far[0], -1), jnp.where(cells_on, cells[0] + LEAVES, -1), -1)
    index_b = far_row(
        jnp.where(far[1] >= LEAVES, far[1] + PARENTS, far[1]),
        jnp.where(
            cells_on,
            jnp.where(
                cells[1] >= PARENTS, cells[1] + (OWN + 4 * SLOTS - PARENTS), cells[1] + LEAVES
            ),
            -1,
        ),
        -1,
    )
    index_a = index_a.reshape(1, -1)
    index_b = index_b.reshape(1, -1)
    spare = jnp.zeros((16 * 128 - FAR_BLOCKS * 128,), f32)
    lifts = far_row(far[2] * CZ, cells[2] * CZ, 0).astype(f32)
    lifts = jnp.concatenate([lifts, spare]).reshape(16, 128)
    live = far_row(far_on.astype(f32), cells_on.astype(f32), 0.0)
    live = jnp.concatenate([live, spare]).reshape(16, 128)

    middle = pl.pallas_call(
        remote_kernel,
        out_shape=[tiled, shaped(LEAVES, 128), shaped(PARENTS, 128)] + [packed] * 4,
        in_specs=[SMEM] * 3 + [VMEM] * 12,
        out_specs=[VMEM] * 7,
        scratch_shapes=[
            pltpu.SMEM((3, near_pairs.shape[2] + 4 * GROUP), i32),
            pltpu.VMEM((4 * SLOTS + 1, 8, HALF), f32),
            pltpu.VMEM((4 * SLOTS + 1, 8, HALF), f32),
            pltpu.VMEM((16 * FEATS, 128), f32),
            pltpu.VMEM((16 * FEATS, 128), f32),
        ]
        + pair_scratch(GROUP // 2),
        compiler_params=params,
        name="pairs_with_others",
    )(
        place,
        leaf_counts,
        near_pairs,
        index_a,
        index_b,
        lifts,
        live,
        bodies,
        moments,
        parents,
        *incoming,
        field,
    )
    field, leaf_terms, parent_terms = middle[:3]
    arrived = [exchange(middle[3 + way], way, True) for way in range(4)]

    field = pl.pallas_call(
        near_kernel,
        out_shape=tiled,
        in_specs=[SMEM] * 3 + [VMEM] * 2,
        out_specs=VMEM,
        scratch_shapes=[pltpu.SMEM((3, near_pairs.shape[2] + 4 * GROUP), i32)]
        + pair_scratch(GROUP),
        compiler_params=params,
        cost_estimate=pl.CostEstimate(
            flops=20_000_000_000, bytes_accessed=2_000_000, transcendentals=0
        ),
        name="own_pairs",
    )(place, leaf_counts, near_pairs, bodies, field)

    return pl.pallas_call(
        back_kernel,
        out_shape=jax.ShapeDtypeStruct((4, LEAVES * LEAF), f32),
        in_specs=[SMEM] * 4 + [VMEM] * 9,
        out_specs=VMEM,
        scratch_shapes=[
            pltpu.VMEM((LEAVES, 128), f32),
            pltpu.VMEM((PARENTS, 128), f32),
            pltpu.VMEM((LEAVES + 1, 8, HALF), f32),
            pltpu.VMEM((64, HALF), f32),
        ],
        compiler_params=params,
        name="shift_and_evaluate",
    )(
        place,
        leaf_counts,
        send_leaves,
        send_parents,
        spots,
        field,
        leaf_terms,
        parent_terms,
        jnp.asarray(DOWN),
        *arrived,
    )


def solution(mesh):
    return jax.shard_map(
        on_device,
        mesh=mesh,
        in_specs=(
            P(None, ("slab", "sub")),
            P(("slab", "sub")),
            P(("slab", "sub")),
            P(("slab", "sub"), None),
            P(("slab", "sub"), None),
            P(("slab", "sub"), None, None),
            P(("slab", "sub"), None, None),
            P(("slab", "sub"), None, None),
        ),
        out_specs=P(None, ("slab", "sub")),
        check_vma=False,
    )
```

```python
import functools
import math

import jax
import jax.numpy as jnp
import numpy as np
from jax import lax
from jax.experimental import pallas as pl
from jax.experimental.pallas import tpu as pltpu
from jax.sharding import PartitionSpec as P

CX = 2
CY = 4
CZ = 32

soft_square = 0.0025
slab_steps = (1, 0, 1, 1)
sub_steps = (0, 1, 1, -1)

LEAVES = CX * CY * CZ
PARENTS = LEAVES // 8
SLOTS = LEAVES // 4
PSLOTS = PARENTS // 2
HALF = 128
LEAF = 2 * HALF
BODY_ROWS = 8 * SLOTS
PACK_ROWS = BODY_ROWS + SLOTS + PSLOTS
GROUP = 8
bf16 = jnp.bfloat16
f32 = jnp.float32
i32 = jnp.int32

MULTI = [
    (i, j, n - i - j) for n in range(5) for i in range(n, -1, -1) for j in range(n - i, -1, -1)
]
PLACE = {alpha: at for at, alpha in enumerate(MULTI)}
TERMS = len(MULTI)
CENTRE = TERMS
LIVE = TERMS + 3
COUNT_AT = 383
FEATS = 40
OWN = LEAVES + PARENTS
ENTRIES = 640
FAR_BLOCKS = 9


def fact(alpha):
    return math.prod(math.factorial(a) for a in alpha)


def added(alpha, beta):
    return tuple(a + b for a, b in zip(alpha, beta))


def taken(alpha, beta):
    return tuple(a - b for a, b in zip(alpha, beta))


def octant(at):
    return tuple(0.5 if bit else -0.5 for bit in (at >> 2 & 1, at >> 1 & 1, at & 1))


def power(delta, alpha):
    return math.prod(d**a for d, a in zip(delta, alpha))


def shift_matrices():
    up = np.zeros((8, 128, 128), np.float32)
    down = np.zeros((8, 128, 128), np.float32)
    for at in range(8):
        delta = octant(at)
        for alpha in MULTI:
            for beta in MULTI:
                rest = taken(alpha, beta)
                if min(rest) < 0:
                    continue
                choose = math.prod(math.comb(a, b) for a, b in zip(alpha, beta))
                up[at, PLACE[beta], PLACE[alpha]] = choose * power(delta, rest)
                down[at, PLACE[alpha], PLACE[beta]] = power(delta, rest) / fact(rest)
    return up.reshape(8 * 128, 128), down.transpose(1, 0, 2).reshape(128, 8 * 128)


UP, DOWN = shift_matrices()


def row_ids(shape):
    return lax.broadcasted_iota(i32, shape, 0)


def lane_ids(shape):
    return lax.broadcasted_iota(i32, shape, 1)


def monomials(x, y, z):
    table = {(0, 0, 0): None}
    axes = (x, y, z)
    for alpha in MULTI[1:]:
        lead = max(axis for axis in range(3) if alpha[axis])
        less = tuple(a - (axis == lead) for axis, a in enumerate(alpha))
        table[alpha] = axes[lead] if table[less] is None else table[less] * axes[lead]
    return table


def split3(value):
    high = value.astype(bf16).astype(f32)
    rest = value - high
    middle = rest.astype(bf16).astype(f32)
    return high, middle, rest - middle


def spread(tile):
    row = row_ids((8, HALF))
    turned = pltpu.roll(tile, 4, 0)
    low = row < 4
    return jnp.concatenate([jnp.where(low, tile, turned), jnp.where(low, turned, tile)], 1)


def fold(field):
    row = row_ids((8, HALF))
    return jnp.where(row < 4, field[:, :HALF], pltpu.roll(field[:, HALF:], 4, 0))


def offset_rows(ox, oy, oz):
    row = row_ids((8, LEAF)) & 3
    return jnp.where(row == 1, ox, jnp.where(row == 2, oy, jnp.where(row == 3, oz, 0.0)))


def features(tile, offset, as_row, as_column, as_weight):
    wide = spread(tile)
    row = row_ids((8, LEAF))
    first = (row & 3) == 0
    low = row < 4
    weight = jnp.broadcast_to(wide[0:1], (8, LEAF))
    x = jnp.where(first, 0.0, wide + offset)
    square = x * x
    pairwise = square + pltpu.roll(square, 1, 0)
    q = pairwise + pltpu.roll(pairwise, 2, 0)
    y = jnp.where(first, q, x)
    zero = jnp.zeros((8, LEAF), f32)
    out = [x, q]
    if as_row:
        h, m, l = split3(y)
        part_a = jnp.where(row == 4, m, h)
        part_b = jnp.where(row == 0, l, jnp.where(row == 4, 1.0, m))
        part_c = jnp.where(first, 1.0, jnp.where(low, h, l))
        out.append(jnp.concatenate([part_a, part_b, part_c, zero], 0).astype(bf16))
    if as_column:
        h, m, l = split3(jnp.where(first, q + soft_square, x * -2.0))
        mixed = jnp.where(low, h, m)
        part_a = jnp.where(first, 1.0, mixed)
        part_b = jnp.where(row == 0, 1.0, jnp.where(row == 4, h, mixed))
        part_c = jnp.where(row == 0, m, jnp.where(row == 4, l, jnp.where(low, l, h)))
        out.append(jnp.concatenate([part_a, part_b, part_c, zero], 0).astype(bf16))
    if as_weight:
        heavy = jnp.where(low, y, 1.0) * weight
        out.append(jnp.concatenate(list(split3(heavy)) + [zero], 0).astype(bf16))
    return out


def field_of(sums, x, q):
    total = sums[0:8] + sums[8:16] + sums[16:24]
    row = row_ids((8, LEAF))
    first = (row & 3) == 0
    plain = pltpu.roll(total, 4, 0)
    inner = total - jnp.where(first, q - soft_square, x) * plain
    along = x * inner
    dots = along[1:2] + along[2:3] + along[3:4]
    return fold(jnp.where(row == 0, 2.0 * dots - inner, inner))


def cubes(row_part, column_part):
    square = lax.dot_general(
        row_part, column_part, (((0,), (0,)), ((), ())), preferred_element_type=f32
    )
    inverse = lax.rsqrt(square)
    return inverse * inverse * inverse


def padded(sums):
    lanes = sums.shape[1]
    if lanes == LEAF:
        return sums
    return jnp.concatenate([sums, jnp.zeros((sums.shape[0], LEAF - lanes), f32)], 1)


def pipeline(count, group, early, late):
    @pl.when(count > 0)
    def _():
        for u in range(group):
            early(0, 0, u)

        def step(k, carry):
            for slot in range(2):
                done = []
                for u in range(group):
                    done.append(late(2 * k + slot, slot, u))
                    early(2 * k + slot + 1, 1 - slot, u)
                for store in done:
                    store()
            return carry

        lax.fori_loop(0, (count + 2 * group - 1) // (2 * group), step, 0)


def placing(places):
    slab_count, sub_count = places
    slab_at = lax.axis_index("slab")
    sub_at = lax.axis_index("sub")
    numbers = [slab_at * CX, sub_at * CY]
    for way in range(4):
        reach_x = slab_at + slab_steps[way]
        reach_y = sub_at + sub_steps[way]
        numbers.append(jnp.where(reach_x >= slab_count, slab_count * CX, 0))
        high = jnp.where(reach_y >= sub_count, sub_count * CY, 0)
        numbers.append(jnp.where(reach_y < 0, -sub_count * CY, high))
    return numbers


def jump_of(place, way):
    jump_x = jnp.int32(0)
    jump_y = jnp.int32(0)
    for at in range(4):
        jump_x = jnp.where(way == at, place[2 + 2 * at], jump_x)
        jump_y = jnp.where(way == at, place[3 + 2 * at], jump_y)
    return jump_x.astype(f32), jump_y.astype(f32)


def leaf_centre(place, leaf):
    return (
        -(place[0] + leaf // (CY * CZ)).astype(f32) - 0.5,
        -(place[1] + leaf // CZ % CY).astype(f32) - 0.5,
        -(leaf % CZ).astype(f32) - 0.5,
    )


def self_loop(words, at, group, size, place, bodies, field, scratch):
    cube_refs, weight_refs, spot_refs = scratch

    def early(k, slot, u):
        leaf = words[at, k * group + u]
        x, q, rows, columns, weights = features(
            bodies[leaf], offset_rows(*leaf_centre(place, leaf & (LEAVES - 1))), True, True, True
        )
        c = cubes(rows[:, :size], columns[:, :size])
        high = c.astype(bf16)
        cube_refs[slot][u, :size, :size] = high
        cube_refs[slot][u, size : 2 * size, :size] = (c - high.astype(f32)).astype(bf16)
        weight_refs[slot][u, :, :size] = weights[:, :size]
        spot_refs[slot][u, 0] = x
        spot_refs[slot][u, 1] = q

    def late(k, slot, u):
        leaf = words[at, k * group + u]
        w = weight_refs[slot][u, :, :size]
        sums = jnp.dot(
            jnp.concatenate([w, w], 1),
            cube_refs[slot][u, : 2 * size, :size],
            preferred_element_type=f32,
        )
        result = field_of(padded(sums), spot_refs[slot][u, 0], spot_refs[slot][u, 1])
        itself = jnp.where((row_ids((8, HALF)) & 3) == 0, bodies[leaf], 0.0)
        result = result + itself * soft_square**-0.5

        def store():
            field[leaf] = result

        return store

    pipeline(words[at, COUNT_AT], group, early, late)


def pair_loop(
    words, at, group, size, place, jumping, bodies, others, field, other_field, scratch
):
    cube_refs, row_refs, column_refs, spot_refs = scratch
    turned = (((1,), (1,)), ((), ()))

    def unpack(k, u):
        word = words[at, k * group + u]
        return word & 511, word >> 9 & 511, word >> 18 & 1, (word >> 19 & 3) - 1, word >> 21 & 7

    def early(k, slot, u):
        row_leaf, column_leaf, swapped, lift, way = unpack(k, u)
        frame = jnp.where(swapped == 1, column_leaf, row_leaf) & (LEAVES - 1)
        cx, cy, cz = leaf_centre(place, frame)
        raised = (lift * CZ).astype(f32)
        swap = (swapped == 1).astype(f32)
        jump_x, jump_y = jump_of(place, way) if jumping else (0.0, 0.0)
        row_offset = offset_rows(cx, cy, cz + swap * raised)
        column_offset = offset_rows(cx + jump_x, cy + jump_y, cz + (1.0 - swap) * raised)
        xr, qr, rows, row_weights = features(bodies[row_leaf], row_offset, True, False, True)
        xc, qc, columns, column_weights = features(
            others[column_leaf], column_offset, False, True, True
        )
        c = cubes(rows[:, :size], columns)
        high = c.astype(bf16)
        cube_refs[slot][u, :size] = high
        cube_refs[slot][u, size : 2 * size] = (c - high.astype(f32)).astype(bf16)
        row_refs[slot][u, :, :size] = row_weights[:, :size]
        column_refs[slot][u] = column_weights
        spot_refs[slot][u, 0] = xr
        spot_refs[slot][u, 1] = qr
        spot_refs[slot][u, 2] = xc
        spot_refs[slot][u, 3] = qc

    def late(k, slot, u):
        row_leaf, column_leaf, _, _, _ = unpack(k, u)
        wr = row_refs[slot][u, :, :size]
        wc = column_refs[slot][u]
        column_sums = jnp.dot(
            jnp.concatenate([wr, wr], 1),
            cube_refs[slot][u, : 2 * size],
            preferred_element_type=f32,
        )
        row_sums = lax.dot_general(
            wc, cube_refs[slot][u, :size], turned, preferred_element_type=f32
        ) + lax.dot_general(
            wc, cube_refs[slot][u, size : 2 * size], turned, preferred_element_type=f32
        )
        row_field = field_of(padded(row_sums), spot_refs[slot][u, 0], spot_refs[slot][u, 1])
        column_field = field_of(column_sums, spot_refs[slot][u, 2], spot_refs[slot][u, 3])

        def store():
            field[row_leaf] = field[row_leaf] + row_field
            other_field[column_leaf] = other_field[column_leaf] + column_field

        return store

    pipeline(words[at, COUNT_AT], group, early, late)


def pair_scratch(group):
    return (
        [pltpu.VMEM((group, 2 * LEAF, LEAF), bf16)] * 2
        + [pltpu.VMEM((group, 32, LEAF), bf16)] * 2
        + [pltpu.VMEM((group, 32, LEAF), bf16)] * 2
        + [pltpu.VMEM((group, 4, 8, LEAF), f32)] * 2
    )


def paired(scratch):
    return [scratch[0:2], scratch[2:4], scratch[4:6], scratch[6:8]]


def front_kernel(
    places, send, send_p, counts, count_row, pairs, spots, masses, up, bodies, moments, parents, words, *outs
):
    place = placing(places)
    row = row_ids((8, HALF))

    def tile_step(g, carry):
        count = jnp.zeros((8, HALF), i32)
        for u in range(8):
            leaf = 8 * g + u
            start = pl.multiple_of(leaf * LEAF, LEAF)
            low = spots[:, pl.ds(start, HALF)]
            high = spots[:, pl.ds(start + HALF, HALF)]
            blank = jnp.zeros((1, HALF), f32)
            bodies[pl.ds(pl.multiple_of(8 * leaf, 8), 8), :] = jnp.concatenate(
                [blank, low, blank, high], 0
            )
            count = jnp.where(row == u, counts[leaf], count)
        lane = lane_ids((8, HALF))
        for half in range(2):
            mass = masses[pl.ds(16 * g + half, 8, stride=2), :]
            bodies[pl.ds(64 * g + 4 * half, 8, stride=8), :] = jnp.where(
                lane + half * HALF < count, mass, 0.0
            )
        return carry

    lax.fori_loop(0, LEAVES // 8, tile_step, 0, unroll=2)

    def group_step(g, carry):
        rows = pl.ds(pl.multiple_of(8 * g, 8), 8)
        w, px, py, pz = wide_rows(bodies, g)
        cx, cy, cz = group_centre(place, g)
        axes = (px - cx, py - cy, pz - cz)
        table = {(0, 0, 0): w}
        lane = lane_ids((8, 128))
        built = jnp.zeros((8, 128), f32)
        for alpha in MULTI:
            if alpha not in table:
                lead = max(axis for axis in range(3) if alpha[axis])
                less = tuple(a - (axis == lead) for axis, a in enumerate(alpha))
                table[alpha] = table[less] * axes[lead]
            value = table[alpha]
            total = jnp.sum(value[:, :HALF] + value[:, HALF:], axis=1, keepdims=True)
            built = jnp.where(lane == PLACE[alpha], total, built)
        built = jnp.where(lane == CENTRE, cx, built)
        built = jnp.where(lane == CENTRE + 1, cy, built)
        built = jnp.where(lane == CENTRE + 2, cz, built)
        moments[rows, :] = built
        return carry

    lax.fori_loop(0, LEAVES // 8, group_step, 0, unroll=2)
    kind = row & 3
    bx = place[0].astype(f32) + 0.5
    by = place[1].astype(f32) + 0.5
    bodies[8 * LEAVES : 8 * LEAVES + 8, :] = jnp.where(
        kind == 1, bx, jnp.where(kind == 2, by, jnp.where(kind == 3, 0.5, 0.0))
    )
    half_z = CZ // 2
    summed = jnp.zeros((PARENTS, 128), f32)
    for at in range(8):
        first = (at >> 2 & 1) * CY * CZ + (at >> 1 & 1) * CZ + (at & 1)
        piece = jnp.concatenate(
            [moments[pl.ds(first + 2 * CZ * py, half_z, stride=2), :] for py in range(CY // 2)], 0
        )
        summed = summed + jnp.dot(
            piece,
            up[128 * at : 128 * at + 128, :],
            precision=lax.Precision.HIGHEST,
            preferred_element_type=f32,
        )
    lane = lane_ids((PARENTS, 128))
    cell = row_ids((PARENTS, 128))
    summed = jnp.where(lane == CENTRE, place[0].astype(f32) + 1.0, summed)
    summed = jnp.where(
        lane == CENTRE + 1,
        place[1].astype(f32) + 1.0 + 2.0 * (cell // half_z).astype(f32),
        summed,
    )
    summed = jnp.where(lane == CENTRE + 2, 1.0 + 2.0 * (cell % half_z).astype(f32), summed)
    parents[...] = summed
    for way in range(4):

        def leaf_step(k, carry, way=way):
            leaf = send[0, way * SLOTS + k]
            outs[way][pl.ds(pl.multiple_of(8 * k, 8), 8), :] = bodies[
                pl.ds(pl.multiple_of(8 * leaf, 8), 8), :
            ]
            outs[way][pl.ds(BODY_ROWS + k, 1), :] = moments[pl.ds(leaf, 1), :]
            return carry

        lax.fori_loop(0, SLOTS, leaf_step, 0, unroll=8)

        def parent_step(k, carry, way=way):
            cell = send_p[0, way * PSLOTS + k]
            outs[way][pl.ds(BODY_ROWS + SLOTS + k, 1), :] = parents[pl.ds(cell, 1), :]
            return carry

        lax.fori_loop(0, PSLOTS, parent_step, 0, unroll=8)
    words[...] = work_lists(count_row[...], pairs[0], pairs[1], pairs[2])


def wide_rows(bodies, g):
    return [
        jnp.concatenate(
            [bodies[pl.ds(64 * g + 4 * half + at, 8, stride=8), :] for half in range(2)], 1
        )
        for at in range(4)
    ]


def group_centre(place, g):
    cx = (place[0] + g // (CY * CZ // 8)).astype(f32) + 0.5
    cy = (place[1] + g // (CZ // 8) % CY).astype(f32) + 0.5
    base_z = (8 * (g % (CZ // 8))).astype(f32) + 0.5
    return cx, cy, row_ids((8, 1)).astype(f32) + base_z


def work_lists(counts, owned, partner, image):
    wide = (LEAVES, LEAVES)
    every = jnp.broadcast_to(counts.astype(f32), (8, LEAVES)).astype(bf16)

    def count_of(index):
        hot = jnp.where(row_ids(wide) == index, 1.0, 0.0).astype(bf16)
        return jnp.dot(every, hot, preferred_element_type=f32)[:1].astype(i32)

    mine = jnp.logical_and(partner >= 0, partner < LEAVES)
    other = partner >= LEAVES
    count_a = count_of(owned)
    count_b = count_of(partner)
    swapped = count_b < count_a
    lift = (image + 1) << 19
    own_word = (
        jnp.where(swapped, partner, owned)
        | jnp.where(swapped, owned, partner) << 9
        | jnp.where(swapped, 1, 0) << 18
        | lift
        | 4 << 21
    )
    spot = jnp.maximum(partner - LEAVES, 0)
    other_word = owned | spot << 9 | lift | (spot // SLOTS) << 21
    small = jnp.minimum(count_a, count_b) <= HALF
    small_a = count_a <= HALF
    small_self = counts <= HALF
    own_empty = LEAVES << 9 | 1 << 19 | 4 << 21
    other_empty = (4 * SLOTS) << 9 | 1 << 19 | 4 << 21
    leaf = lane_ids((1, LEAVES))
    yes = jnp.ones((1, LEAVES), jnp.bool_)
    lists = [
        (own_word, mine, small, own_empty),
        (other_word, other, small_a, other_empty),
        (leaf, yes, small_self, LEAVES),
    ]
    flags = []
    for _, taken_in, short, _ in lists:
        member = jnp.where(taken_in, 1.0, 0.0)
        brief = jnp.where(short, 1.0, 0.0)
        flags += [member * brief, member * (1.0 - brief)]
    flags = jnp.concatenate(flags + [jnp.zeros((2, LEAVES), f32)], 0)
    before = jnp.where(row_ids(wide) < lane_ids(wide), 1.0, 0.0).astype(bf16)
    order = jnp.dot(flags.astype(bf16), before, preferred_element_type=f32)
    order = jnp.where(flags > 0.0, order, -1.0).astype(i32)
    number = jnp.sum(flags, axis=1, keepdims=True).astype(i32)
    lane = lane_ids((1, COUNT_AT + 1))
    rows = []
    for at in range(6):
        word, _, _, empty = lists[at // 2]
        pieces = jnp.concatenate(
            [word & 255, word >> 8 & 255, word >> 16, jnp.zeros((5, LEAVES), i32)], 0
        )
        hot = jnp.where(row_ids(wide) == order[at : at + 1], 1.0, 0.0).astype(bf16)
        found = lax.dot_general(
            pieces.astype(f32).astype(bf16),
            hot,
            (((1,), (1,)), ((), ())),
            preferred_element_type=f32,
        ).astype(i32)
        joined = found[0:1] | found[1:2] << 8 | found[2:3] << 16
        joined = jnp.concatenate([joined, jnp.zeros((1, COUNT_AT + 1 - LEAVES), i32)], 1)
        count = number[at : at + 1]
        joined = jnp.where(lane < count, joined, empty)
        rows.append(jnp.where(lane == COUNT_AT, count, joined))
    return jnp.concatenate(rows + [jnp.zeros((2, COUNT_AT + 1), i32)], 0)


def self_kernel(places, words, bodies, field, *scratch):
    place = placing(places)
    field[LEAVES] = jnp.zeros((8, HALF), f32)
    refs = (scratch[0:2], scratch[2:4], scratch[4:6])
    self_loop(words, 4, GROUP, HALF, place, bodies, field, refs)
    self_loop(words, 5, GROUP, LEAF, place, bodies, field, refs)


def near_kernel(places, words, bodies, field_in, field, *scratch):
    place = placing(places)
    field[...] = field_in[...]
    refs = paired(scratch)
    pair_loop(words, 0, GROUP, HALF, place, False, bodies, bodies, field, field, refs)
    pair_loop(words, 1, GROUP, LEAF, place, False, bodies, bodies, field, field, refs)


def derivatives(x, y, z):
    inverse = lax.rsqrt(x * x + y * y + z * z)
    square = inverse * inverse
    odd = [inverse]
    for _ in range(4):
        odd.append(odd[-1] * square)
    powers = monomials(x, y, z)
    result = {}
    for alpha in MULTI:
        degree = sum(alpha)
        total = None
        for p in range(alpha[0] // 2 + 1):
            for q in range(alpha[1] // 2 + 1):
                for s in range(alpha[2] // 2 + 1):
                    m = p + q + s
                    ways = math.prod(
                        math.factorial(a) // (2**c * math.factorial(c) * math.factorial(a - 2 * c))
                        for a, c in zip(alpha, (p, q, s))
                    )
                    sign = (-1.0) ** (degree - m)
                    double = math.prod(range(1, 2 * (degree - m), 2))
                    term = odd[degree - m] * (sign * double * ways)
                    rest = (alpha[0] - 2 * p, alpha[1] - 2 * q, alpha[2] - 2 * s)
                    if powers[rest] is not None:
                        term = term * powers[rest]
                    total = term if total is None else total + term
        result[alpha] = total
    return result


def remote_kernel(
    places,
    words,
    far,
    cells,
    bodies,
    moments,
    parents,
    in_0,
    in_1,
    in_2,
    in_3,
    field_in,
    field,
    leaf_terms,
    parent_terms,
    out_0,
    out_1,
    out_2,
    out_3,
    far_bodies,
    far_field,
    gather_a,
    gather_b,
    *scratch,
):
    place = placing(places)
    incoming = (in_0, in_1, in_2, in_3)
    outgoing = (out_0, out_1, out_2, out_3)
    field[...] = field_in[...]
    for way in range(4):
        far_bodies[way * SLOTS : (way + 1) * SLOTS] = incoming[way][:BODY_ROWS, :].reshape(
            SLOTS, 8, HALF
        )
    far_bodies[4 * SLOTS] = bodies[LEAVES]
    far_field[...] = jnp.zeros_like(far_field)
    refs = paired(scratch)
    group = GROUP // 2
    pair_loop(words, 2, group, HALF, place, True, bodies, far_bodies, field, far_field, refs)
    pair_loop(words, 3, group, LEAF, place, True, bodies, far_bodies, field, far_field, refs)
    for way in range(4):
        outgoing[way][:BODY_ROWS, :] = far_field[way * SLOTS : (way + 1) * SLOTS].reshape(
            BODY_ROWS, HALF
        )

    def moved(rows, way):
        lane = lane_ids(rows.shape)
        rows = jnp.where(lane == CENTRE, rows + place[2 + 2 * way].astype(f32), rows)
        return jnp.where(lane == CENTRE + 1, rows + place[3 + 2 * way].astype(f32), rows)

    table = [moments[...], parents[...]]
    for way in range(4):
        table.append(moved(incoming[way][BODY_ROWS : BODY_ROWS + SLOTS, :], way))
    for way in range(4):
        table.append(moved(incoming[way][BODY_ROWS + SLOTS :, :], way))
    table.append(jnp.zeros((ENTRIES - OWN - 4 * SLOTS - 4 * PSLOTS, 128), f32))
    columns = jnp.concatenate(table, 0).T[:FEATS]
    columns = jnp.concatenate(split3(columns), 0).astype(bf16)

    def one_hot(index, entries):
        return jnp.where(row_ids((entries, 128)) == index, 1.0, 0.0).astype(bf16)

    def joined(parts):
        return parts[:FEATS] + parts[FEATS : 2 * FEATS] + parts[2 * FEATS :]

    def far_block(block):
        if block < FAR_BLOCKS - 1:
            lanes = slice(128 * block, 128 * block + 128)
            a, b, z = far[0, :, lanes], far[1, :, lanes], far[2, :, lanes]
            used = b >= 0
            b = jnp.where(b >= LEAVES, b + PARENTS, b)
        else:
            blank = jnp.zeros((1, 128 - cells.shape[2]), i32)
            a = jnp.concatenate([cells[0] + LEAVES, blank], 1)
            b = jnp.concatenate([cells[1], blank - 1], 1)
            z = jnp.concatenate([cells[2], blank], 1)
            used = b >= 0
            b = jnp.where(b >= PARENTS, b + (OWN + 4 * SLOTS - PARENTS), b + LEAVES)
            b = jnp.where(used, b, -1)
        a = jnp.where(used, a, -1)
        return a, b, (z * CZ).astype(f32), jnp.where(used, 1.0, 0.0)

    gather_a[...] = jnp.zeros_like(gather_a)
    gather_b[...] = jnp.zeros_like(gather_b)
    place_of = row_ids((FEATS, 128))
    for block in range(FAR_BLOCKS):
        rows = slice(FEATS * block, FEATS * block + FEATS)
        a, b, lift, used = far_block(block)
        got_a = joined(
            jnp.dot(columns[:, :OWN], one_hot(a, OWN), preferred_element_type=f32)
        )
        got_b = joined(jnp.dot(columns, one_hot(b, ENTRIES), preferred_element_type=f32))
        gather_a[rows, :] = jnp.where(place_of == LIVE, used, got_a)
        gather_b[rows, :] = got_b + jnp.where(place_of == CENTRE + 2, lift, 0.0)
    for chunk in range(2):
        start = 8 * chunk * FEATS

        def feature(ref, at, start=start):
            return ref[pl.ds(start + at, 8, stride=FEATS), :]

        def gap(axis):
            return feature(gather_a, CENTRE + axis) - feature(gather_b, CENTRE + axis)

        live = feature(gather_a, LIVE) > 0.0
        x = jnp.where(live, gap(0), 3.0)
        y = jnp.where(live, gap(1), 3.0)
        z = jnp.where(live, gap(2), 3.0)
        tensors = derivatives(x, y, z)
        held_a = {}
        held_b = {}
        for alpha in MULTI:
            held_a[alpha] = feature(gather_a, PLACE[alpha]) * (-1.0 / fact(alpha))
            held_b[alpha] = feature(gather_b, PLACE[alpha]) * (
                -((-1.0) ** sum(alpha)) / fact(alpha)
            )
        for beta in MULTI:
            to_a = None
            to_b = None
            for alpha in MULTI:
                if sum(alpha) + sum(beta) > 4:
                    continue
                tensor = tensors[added(alpha, beta)]
                term_a = held_b[alpha] * tensor
                term_b = held_a[alpha] * tensor
                to_a = term_a if to_a is None else to_a + term_a
                to_b = term_b if to_b is None else to_b + term_b
            if sum(beta) % 2:
                to_b = -to_b
            gather_a[pl.ds(start + PLACE[beta], 8, stride=FEATS), :] = to_a
            gather_b[pl.ds(start + PLACE[beta], 8, stride=FEATS), :] = to_b
    sums_a = jnp.zeros((3 * FEATS, OWN), f32)
    sums_b = jnp.zeros((3 * FEATS, ENTRIES), f32)
    turned = (((1,), (1,)), ((), ()))
    for block in range(FAR_BLOCKS):
        rows = slice(FEATS * block, FEATS * block + FEATS)
        a, b, _, _ = far_block(block)
        parts_a = jnp.concatenate(split3(gather_a[rows, :]), 0).astype(bf16)
        parts_b = jnp.concatenate(split3(gather_b[rows, :]), 0).astype(bf16)
        hot_a = one_hot(a, OWN)
        hot_b = one_hot(b, ENTRIES)
        sums_a = sums_a + lax.dot_general(parts_a, hot_a, turned, preferred_element_type=f32)
        sums_b = sums_b + lax.dot_general(parts_b, hot_b, turned, preferred_element_type=f32)
    got_a = jnp.concatenate([joined(sums_a), jnp.zeros((128 - FEATS, OWN), f32)], 0)
    got_b = jnp.concatenate([joined(sums_b), jnp.zeros((128 - FEATS, ENTRIES), f32)], 0)
    keep = lane_ids((1, 128)) < TERMS
    terms_a = jnp.where(keep, got_a.T, 0.0)
    terms_b = jnp.where(keep, got_b.T, 0.0)
    leaf_terms[...] = terms_a[:LEAVES] + terms_b[:LEAVES]
    parent_terms[...] = terms_a[LEAVES:OWN] + terms_b[LEAVES:OWN]
    leaf_start = OWN
    parent_start = OWN + 4 * SLOTS
    for way in range(4):
        first = leaf_start + way * SLOTS
        outgoing[way][BODY_ROWS : BODY_ROWS + SLOTS, :] = terms_b[first : first + SLOTS]
        first = parent_start + way * PSLOTS
        outgoing[way][BODY_ROWS + SLOTS :, :] = terms_b[first : first + PSLOTS]


def back_kernel(
    places,
    counts,
    send,
    send_p,
    bodies,
    field_in,
    leaf_in,
    parent_in,
    down,
    in_0,
    in_1,
    in_2,
    in_3,
    out,
    leaf_terms,
    parent_terms,
    field,
    tiles,
):
    place = placing(places)
    incoming = (in_0, in_1, in_2, in_3)
    leaf_terms[...] = leaf_in[...]
    parent_terms[...] = parent_in[...]
    field[...] = field_in[...]
    for way in range(4):

        def leaf_step(k, carry, way=way):
            leaf = send[0, way * SLOTS + k]
            field[leaf] = field[leaf] + incoming[way][pl.ds(pl.multiple_of(8 * k, 8), 8), :]
            leaf_terms[pl.ds(leaf, 1), :] = (
                leaf_terms[pl.ds(leaf, 1), :] + incoming[way][pl.ds(BODY_ROWS + k, 1), :]
            )
            return carry

        lax.fori_loop(0, SLOTS, leaf_step, 0, unroll=8)

        def parent_step(k, carry, way=way):
            cell = send_p[0, way * PSLOTS + k]
            parent_terms[pl.ds(cell, 1), :] = (
                parent_terms[pl.ds(cell, 1), :] + incoming[way][pl.ds(BODY_ROWS + SLOTS + k, 1), :]
            )
            return carry

        lax.fori_loop(0, PSLOTS, parent_step, 0, unroll=8)
    half_z = CZ // 2
    for at in range(8):
        moved = jnp.dot(
            parent_terms[...],
            down[:, 128 * at : 128 * at + 128],
            precision=lax.Precision.HIGHEST,
            preferred_element_type=f32,
        )
        first = (at >> 2 & 1) * CY * CZ + (at >> 1 & 1) * CZ + (at & 1)
        for py in range(CY // 2):
            rows = pl.ds(first + 2 * CZ * py, half_z, stride=2)
            leaf_terms[rows, :] = leaf_terms[rows, :] + moved[half_z * py : half_z * py + half_z]

    def group_step(g, carry):
        rows = pl.ds(pl.multiple_of(8 * g, 8), 8)
        cx, cy, cz = group_centre(place, g)
        _, px, py, pz = wide_rows(bodies, g)
        x, y, z = px - cx, py - cy, pz - cz
        terms = leaf_terms[rows, :]
        powers = monomials(x, y, z)
        column = {
            alpha: jnp.broadcast_to(terms[:, PLACE[alpha] : PLACE[alpha] + 1], (8, LEAF))
            for alpha in MULTI
        }
        totals = [None] * 4
        for beta in MULTI:
            scale = 1.0 / fact(beta)
            base = powers[beta]
            if base is not None and scale != 1.0:
                base = base * scale
            kinds = [beta] + (
                [added(beta, unit) for unit in ((1, 0, 0), (0, 1, 0), (0, 0, 1))]
                if sum(beta) < 4
                else []
            )
            for at, kind in enumerate(kinds):
                term = column[kind] if base is None else column[kind] * base
                totals[at] = term if totals[at] is None else totals[at] + term
        values = [totals[0], -totals[1], -totals[2], -totals[3]]
        for at, value in enumerate(values):
            tiles[pl.ds(at, 8, stride=8), :] = value[:, :HALF]
            tiles[pl.ds(4 + at, 8, stride=8), :] = value[:, HALF:]
        row = row_ids((8, HALF))
        body = lane_ids((8, HALF)) + jnp.where(row < 4, 0, HALF)
        for u in range(8):
            leaf = 8 * g + u
            tile = tiles[8 * u : 8 * u + 8, :] + field[leaf]
            tile = jnp.where(body < counts[leaf], tile, 0.0)
            start = pl.multiple_of(leaf * LEAF, LEAF)
            out[:, pl.ds(start, HALF)] = tile[:4]
            out[:, pl.ds(start + HALF, HALF)] = tile[4:]
        return carry

    lax.fori_loop(0, LEAVES // 8, group_step, 0)


VMEM = pl.BlockSpec(memory_space=pltpu.VMEM)
SMEM = pl.BlockSpec(memory_space=pltpu.SMEM)
params = pltpu.CompilerParams(vmem_limit_bytes=20 * 1024 * 1024)
packed = jax.ShapeDtypeStruct((PACK_ROWS, 128), f32)
tiled = jax.ShapeDtypeStruct((LEAVES + 1, 8, HALF), f32)
heavy = pl.CostEstimate(flops=20_000_000_000, bytes_accessed=2_000_000, transcendentals=0)


def shaped(*dims):
    return jax.ShapeDtypeStruct(dims, f32)


def on_device(
    positions, masses, leaf_counts, send_leaves, send_parents, near_pairs, far_pairs, parent_pairs
):
    slab_count = lax.axis_size("slab")
    sub_count = lax.axis_size("sub")
    places = (slab_count, sub_count)

    def rows_first(lists):
        return jnp.transpose(lists, (1, 0, 2))

    sent = pl.pallas_call(
        functools.partial(front_kernel, places),
        out_shape=[shaped(8 * LEAVES + 8, HALF), shaped(LEAVES, 128), shaped(PARENTS, 128)]
        + [jax.ShapeDtypeStruct((8, COUNT_AT + 1), i32)]
        + [packed] * 4,
        in_specs=[SMEM] * 3 + [VMEM] * 5,
        out_specs=[VMEM] * 8,
        compiler_params=params,
        name="moments_and_packing",
    )(
        send_leaves,
        send_parents,
        leaf_counts,
        leaf_counts.reshape(1, LEAVES),
        rows_first(near_pairs),
        positions,
        masses.reshape(2 * LEAVES, HALF),
        jnp.asarray(UP),
    )
    bodies = sent[0].reshape(LEAVES + 1, 8, HALF)
    moments, parents, words = sent[1:4]

    def exchange(value, way, back):
        pairs = []
        for s in range(slab_count):
            for u in range(sub_count):
                here = s * sub_count + u
                there = (s + slab_steps[way]) % slab_count * sub_count + (
                    u + sub_steps[way]
                ) % sub_count
                pairs.append((here, there) if back else (there, here))
        return lax.ppermute(value, ("slab", "sub"), pairs)

    incoming = [exchange(sent[4 + way], way, False) for way in range(4)]

    field = pl.pallas_call(
        functools.partial(self_kernel, places),
        out_shape=tiled,
        in_specs=[SMEM, VMEM],
        out_specs=VMEM,
        scratch_shapes=[pltpu.VMEM((GROUP, 2 * LEAF, LEAF), bf16)] * 2
        + [pltpu.VMEM((GROUP, 32, LEAF), bf16)] * 2
        + [pltpu.VMEM((GROUP, 2, 8, LEAF), f32)] * 2,
        compiler_params=params,
        cost_estimate=heavy,
        name="self_pairs",
    )(words, bodies)

    middle = pl.pallas_call(
        functools.partial(remote_kernel, places),
        out_shape=[tiled, shaped(LEAVES, 128), shaped(PARENTS, 128)] + [packed] * 4,
        in_specs=[SMEM] + [VMEM] * 10,
        out_specs=[VMEM] * 7,
        scratch_shapes=[
            pltpu.VMEM((4 * SLOTS + 1, 8, HALF), f32),
            pltpu.VMEM((4 * SLOTS + 1, 8, HALF), f32),
            pltpu.VMEM((16 * FEATS, 128), f32),
            pltpu.VMEM((16 * FEATS, 128), f32),
        ]
        + pair_scratch(GROUP // 2),
        compiler_params=params,
        name="pairs_with_others",
    )(
        words,
        rows_first(far_pairs),
        rows_first(parent_pairs),
        bodies,
        moments,
        parents,
        *incoming,
        field,
    )
    field, leaf_terms, parent_terms = middle[:3]
    arrived = [exchange(middle[3 + way], way, True) for way in range(4)]

    field = pl.pallas_call(
        functools.partial(near_kernel, places),
        out_shape=tiled,
        in_specs=[SMEM] + [VMEM] * 2,
        out_specs=VMEM,
        scratch_shapes=pair_scratch(GROUP),
        compiler_params=params,
        cost_estimate=heavy,
        name="own_pairs",
    )(words, bodies, field)

    return pl.pallas_call(
        functools.partial(back_kernel, places),
        out_shape=jax.ShapeDtypeStruct((4, LEAVES * LEAF), f32),
        in_specs=[SMEM] * 3 + [VMEM] * 9,
        out_specs=VMEM,
        scratch_shapes=[
            pltpu.VMEM((LEAVES, 128), f32),
            pltpu.VMEM((PARENTS, 128), f32),
            pltpu.VMEM((LEAVES + 1, 8, HALF), f32),
            pltpu.VMEM((64, HALF), f32),
        ],
        compiler_params=params,
        name="shift_and_evaluate",
    )(
        leaf_counts,
        send_leaves,
        send_parents,
        sent[0],
        field,
        leaf_terms,
        parent_terms,
        jnp.asarray(DOWN),
        *arrived,
    )


def solution(mesh):
    return jax.shard_map(
        on_device,
        mesh=mesh,
        in_specs=(
            P(None, ("slab", "sub")),
            P(("slab", "sub")),
            P(("slab", "sub")),
            P(("slab", "sub"), None),
            P(("slab", "sub"), None),
            P(("slab", "sub"), None, None),
            P(("slab", "sub"), None, None),
            P(("slab", "sub"), None, None),
        ),
        out_specs=P(None, ("slab", "sub")),
        check_vma=False,
    )
```

```python
import functools
import math

import jax
import jax.numpy as jnp
import numpy as np
from jax import lax
from jax.experimental import pallas as pl
from jax.experimental.pallas import tpu as pltpu
from jax.sharding import PartitionSpec as P

CX = 2
CY = 4
CZ = 32

soft_square = 0.0025
slab_steps = (1, 0, 1, 1)
sub_steps = (0, 1, 1, -1)

LEAVES = CX * CY * CZ
PARENTS = LEAVES // 8
SLOTS = LEAVES // 4
PSLOTS = PARENTS // 2
HALF = 128
LEAF = 2 * HALF
BODY_ROWS = 8 * SLOTS
PACK_ROWS = BODY_ROWS + SLOTS + PSLOTS
GROUP = 8
bf16 = jnp.bfloat16
f32 = jnp.float32
i32 = jnp.int32

MULTI = [
    (i, j, n - i - j) for n in range(5) for i in range(n, -1, -1) for j in range(n - i, -1, -1)
]
PLACE = {alpha: at for at, alpha in enumerate(MULTI)}
TERMS = len(MULTI)
CENTRE = TERMS
LIVE = TERMS + 3
SIZES = (256, 192, 160, 128, 96)
EVERY_SIZE = tuple((size, at) for at, size in enumerate(SIZES))
SOME_SIZES = ((256, 0), (192, 2), (128, 4))
LIST = 384
STEPS_AT = LIST - 8
FEATS = 40
OWN = LEAVES + PARENTS
ENTRIES = 640
FAR_BLOCKS = 9


def fact(alpha):
    return math.prod(math.factorial(a) for a in alpha)


def added(alpha, beta):
    return tuple(a + b for a, b in zip(alpha, beta))


def taken(alpha, beta):
    return tuple(a - b for a, b in zip(alpha, beta))


def octant(at):
    return tuple(0.5 if bit else -0.5 for bit in (at >> 2 & 1, at >> 1 & 1, at & 1))


def power(delta, alpha):
    return math.prod(d**a for d, a in zip(delta, alpha))


def shift_matrices():
    up = np.zeros((8, 128, 128), np.float32)
    down = np.zeros((8, 128, 128), np.float32)
    for at in range(8):
        delta = octant(at)
        for alpha in MULTI:
            for beta in MULTI:
                rest = taken(alpha, beta)
                if min(rest) < 0:
                    continue
                choose = math.prod(math.comb(a, b) for a, b in zip(alpha, beta))
                up[at, PLACE[beta], PLACE[alpha]] = choose * power(delta, rest)
                down[at, PLACE[alpha], PLACE[beta]] = power(delta, rest) / fact(rest)
    return up.reshape(8 * 128, 128), down.transpose(1, 0, 2).reshape(128, 8 * 128)


UP, DOWN = shift_matrices()


def row_ids(shape):
    return lax.broadcasted_iota(i32, shape, 0)


def lane_ids(shape):
    return lax.broadcasted_iota(i32, shape, 1)


def monomials(x, y, z):
    table = {(0, 0, 0): None}
    axes = (x, y, z)
    for alpha in MULTI[1:]:
        lead = max(axis for axis in range(3) if alpha[axis])
        less = tuple(a - (axis == lead) for axis, a in enumerate(alpha))
        table[alpha] = axes[lead] if table[less] is None else table[less] * axes[lead]
    return table


def split3(value):
    high = value.astype(bf16).astype(f32)
    rest = value - high
    middle = rest.astype(bf16).astype(f32)
    return high, middle, rest - middle


def spread(tile):
    row = row_ids((8, HALF))
    turned = pltpu.roll(tile, 4, 0)
    low = row < 4
    return jnp.concatenate([jnp.where(low, tile, turned), jnp.where(low, turned, tile)], 1)


def fold(field):
    row = row_ids((8, HALF))
    return jnp.where(row < 4, field[:, :HALF], pltpu.roll(field[:, HALF:], 4, 0))


def offset_rows(ox, oy, oz):
    row = row_ids((8, LEAF)) & 3
    return jnp.where(row == 1, ox, jnp.where(row == 2, oy, jnp.where(row == 3, oz, 0.0)))


def features(tile, offset, as_row, as_column, as_weight):
    wide = spread(tile)
    row = row_ids((8, LEAF))
    first = (row & 3) == 0
    low = row < 4
    weight = jnp.broadcast_to(wide[0:1], (8, LEAF))
    x = jnp.where(first, 0.0, wide + offset)
    square = x * x
    pairwise = square + pltpu.roll(square, 1, 0)
    q = pairwise + pltpu.roll(pairwise, 2, 0)
    y = jnp.where(first, q, x)
    zero = jnp.zeros((8, LEAF), f32)
    out = [x, q]
    if as_row:
        h, m, l = split3(y)
        part_a = jnp.where(row == 4, m, h)
        part_b = jnp.where(row == 0, l, jnp.where(row == 4, 1.0, m))
        part_c = jnp.where(first, 1.0, jnp.where(low, h, l))
        out.append(jnp.concatenate([part_a, part_b, part_c, zero], 0).astype(bf16))
    if as_column:
        h, m, l = split3(jnp.where(first, q + soft_square, x * -2.0))
        mixed = jnp.where(low, h, m)
        part_a = jnp.where(first, 1.0, mixed)
        part_b = jnp.where(row == 0, 1.0, jnp.where(row == 4, h, mixed))
        part_c = jnp.where(row == 0, m, jnp.where(row == 4, l, jnp.where(low, l, h)))
        out.append(jnp.concatenate([part_a, part_b, part_c, zero], 0).astype(bf16))
    if as_weight:
        heavy = jnp.where(low, y, 1.0) * weight
        out.append(jnp.concatenate(list(split3(heavy)) + [zero], 0).astype(bf16))
    return out


def field_of(sums, x, q):
    total = sums[0:8] + sums[8:16] + sums[16:24]
    row = row_ids((8, LEAF))
    first = (row & 3) == 0
    plain = pltpu.roll(total, 4, 0)
    inner = total - jnp.where(first, q - soft_square, x) * plain
    along = x * inner
    dots = along[1:2] + along[2:3] + along[3:4]
    return fold(jnp.where(row == 0, 2.0 * dots - inner, inner))


def cubes(row_part, column_part):
    square = lax.dot_general(
        row_part, column_part, (((0,), (0,)), ((), ())), preferred_element_type=f32
    )
    inverse = lax.rsqrt(square)
    return inverse * inverse * inverse


def padded(sums):
    lanes = sums.shape[1]
    if lanes == LEAF:
        return sums
    return jnp.concatenate([sums, jnp.zeros((sums.shape[0], LEAF - lanes), f32)], 1)


def pipeline(words, at, group, plan, early, late):
    @pl.when(words[at, STEPS_AT + len(SIZES) - 1] > 0)
    def _():
        for u in range(group):
            early(SIZES[0], 0, 0, u)

    begin = jnp.int32(0)
    for size, last in plan:

        def step(k, carry, size=size):
            for slot in range(2):
                done = []
                for u in range(group):
                    done.append(late(size, 2 * k + slot, slot, u))
                    early(size, 2 * k + slot + 1, 1 - slot, u)
                for store in done:
                    store()
            return carry

        end = words[at, STEPS_AT + last]
        lax.fori_loop(begin, end, step, 0)
        begin = end


def placing(places):
    slab_count, sub_count = places
    slab_at = lax.axis_index("slab")
    sub_at = lax.axis_index("sub")
    numbers = [slab_at * CX, sub_at * CY]
    for way in range(4):
        reach_x = slab_at + slab_steps[way]
        reach_y = sub_at + sub_steps[way]
        numbers.append(jnp.where(reach_x >= slab_count, slab_count * CX, 0))
        high = jnp.where(reach_y >= sub_count, sub_count * CY, 0)
        numbers.append(jnp.where(reach_y < 0, -sub_count * CY, high))
    return numbers


def jump_of(place, way):
    jump_x = jnp.int32(0)
    jump_y = jnp.int32(0)
    for at in range(4):
        jump_x = jnp.where(way == at, place[2 + 2 * at], jump_x)
        jump_y = jnp.where(way == at, place[3 + 2 * at], jump_y)
    return jump_x.astype(f32), jump_y.astype(f32)


def leaf_centre(place, leaf):
    return (
        -(place[0] + leaf // (CY * CZ)).astype(f32) - 0.5,
        -(place[1] + leaf // CZ % CY).astype(f32) - 0.5,
        -(leaf % CZ).astype(f32) - 0.5,
    )


def halves(c):
    high = c.astype(bf16)
    return high, (c - high.astype(f32)).astype(bf16)


def self_loop(words, at, group, plan, place, bodies, field, scratch):
    high_refs, low_refs, weight_refs, spot_refs = scratch

    def early(size, k, slot, u):
        leaf = words[at, k * group + u]
        x, q, rows, columns, weights = features(
            bodies[leaf], offset_rows(*leaf_centre(place, leaf & (LEAVES - 1))), True, True, True
        )
        wide = LEAF if size > HALF else HALF
        high, low = halves(cubes(rows[:, :size], columns[:, :wide]))
        high_refs[slot][u, :size, :wide] = high
        low_refs[slot][u, :size, :wide] = low
        weight_refs[slot][u] = weights
        spot_refs[slot][u, 0] = x
        spot_refs[slot][u, 1] = q

    def late(size, k, slot, u):
        leaf = words[at, k * group + u]
        wide = LEAF if size > HALF else HALF
        w = weight_refs[slot][u, :, :size]
        sums = jnp.dot(
            w, high_refs[slot][u, :size, :wide], preferred_element_type=f32
        ) + jnp.dot(w, low_refs[slot][u, :size, :wide], preferred_element_type=f32)
        result = field_of(padded(sums), spot_refs[slot][u, 0], spot_refs[slot][u, 1])
        itself = jnp.where((row_ids((8, HALF)) & 3) == 0, bodies[leaf], 0.0)
        result = result + itself * soft_square**-0.5

        def store():
            field[leaf] = result

        return store

    pipeline(words, at, group, plan, early, late)


def pair_loop(
    words, at, group, plan, place, jumping, bodies, others, field, other_field, scratch
):
    high_refs, low_refs, row_refs, column_refs, spot_refs = scratch
    turned = (((1,), (1,)), ((), ()))

    def unpack(k, u):
        word = words[at, k * group + u]
        return word & 511, word >> 9 & 511, word >> 18 & 1, (word >> 19 & 3) - 1, word >> 21 & 7

    def early(size, k, slot, u):
        row_leaf, column_leaf, swapped, lift, way = unpack(k, u)
        frame = jnp.where(swapped == 1, column_leaf, row_leaf) & (LEAVES - 1)
        cx, cy, cz = leaf_centre(place, frame)
        raised = (lift * CZ).astype(f32)
        swap = (swapped == 1).astype(f32)
        jump_x, jump_y = jump_of(place, way) if jumping else (0.0, 0.0)
        row_offset = offset_rows(cx, cy, cz + swap * raised)
        column_offset = offset_rows(cx + jump_x, cy + jump_y, cz + (1.0 - swap) * raised)
        xr, qr, rows, row_weights = features(bodies[row_leaf], row_offset, True, False, True)
        xc, qc, columns, column_weights = features(
            others[column_leaf], column_offset, False, True, True
        )
        high, low = halves(cubes(rows[:, :size], columns))
        high_refs[slot][u, :size] = high
        low_refs[slot][u, :size] = low
        row_refs[slot][u] = row_weights
        column_refs[slot][u] = column_weights
        spot_refs[slot][u, 0] = xr
        spot_refs[slot][u, 1] = qr
        spot_refs[slot][u, 2] = xc
        spot_refs[slot][u, 3] = qc

    def late(size, k, slot, u):
        row_leaf, column_leaf, _, _, _ = unpack(k, u)
        wr = row_refs[slot][u, :, :size]
        wc = column_refs[slot][u]
        high = high_refs[slot][u, :size]
        low = low_refs[slot][u, :size]
        column_sums = jnp.dot(wr, high, preferred_element_type=f32) + jnp.dot(
            wr, low, preferred_element_type=f32
        )
        row_sums = lax.dot_general(wc, high, turned, preferred_element_type=f32) + lax.dot_general(
            wc, low, turned, preferred_element_type=f32
        )
        row_field = field_of(padded(row_sums), spot_refs[slot][u, 0], spot_refs[slot][u, 1])
        column_field = field_of(column_sums, spot_refs[slot][u, 2], spot_refs[slot][u, 3])

        def store():
            field[row_leaf] = field[row_leaf] + row_field
            other_field[column_leaf] = other_field[column_leaf] + column_field

        return store

    pipeline(words, at, group, plan, early, late)


def pair_scratch(group):
    return (
        [pltpu.VMEM((group, LEAF, LEAF), bf16)] * 4
        + [pltpu.VMEM((group, 32, LEAF), bf16)] * 4
        + [pltpu.VMEM((group, 4, 8, LEAF), f32)] * 2
    )


def paired(scratch):
    return [scratch[at : at + 2] for at in range(0, len(scratch), 2)]


def front_kernel(places, *refs):
    stored, made, held, sems = refs[:7], refs[7:15], refs[15:23], refs[23]
    bodies, moments, parents, words = made[:4]
    outs = made[4:]
    sources = (stored[0], stored[1], stored[2], *stored[2:])
    copies = [
        pltpu.make_async_copy(source, target, sems.at[at])
        for at, (source, target) in enumerate(zip(sources, held))
    ]
    for copy in copies:
        copy.start()
    for copy in copies:
        copy.wait()
    send, send_p, counts, count_row, pairs, spots, masses, up = held
    place = placing(places)
    row = row_ids((8, HALF))

    def tile_step(g, carry):
        count = jnp.zeros((8, HALF), i32)
        for u in range(8):
            leaf = 8 * g + u
            start = pl.multiple_of(leaf * LEAF, LEAF)
            low = spots[:, pl.ds(start, HALF)]
            high = spots[:, pl.ds(start + HALF, HALF)]
            blank = jnp.zeros((1, HALF), f32)
            bodies[pl.ds(pl.multiple_of(8 * leaf, 8), 8), :] = jnp.concatenate(
                [blank, low, blank, high], 0
            )
            count = jnp.where(row == u, counts[0, leaf], count)
        lane = lane_ids((8, HALF))
        for half in range(2):
            mass = masses[pl.ds(16 * g + half, 8, stride=2), :]
            bodies[pl.ds(64 * g + 4 * half, 8, stride=8), :] = jnp.where(
                lane + half * HALF < count, mass, 0.0
            )
        return carry

    lax.fori_loop(0, LEAVES // 8, tile_step, 0, unroll=4)

    def group_step(g, carry):
        rows = pl.ds(pl.multiple_of(8 * g, 8), 8)
        w, px, py, pz = wide_rows(bodies, g)
        cx, cy, cz = group_centre(place, g)
        axes = (px - cx, py - cy, pz - cz)
        table = {(0, 0, 0): w}
        lane = lane_ids((8, 128))
        built = jnp.zeros((8, 128), f32)
        for alpha in MULTI:
            if alpha not in table:
                lead = max(axis for axis in range(3) if alpha[axis])
                less = tuple(a - (axis == lead) for axis, a in enumerate(alpha))
                table[alpha] = table[less] * axes[lead]
            value = table[alpha]
            total = jnp.sum(value[:, :HALF] + value[:, HALF:], axis=1, keepdims=True)
            built = jnp.where(lane == PLACE[alpha], total, built)
        built = jnp.where(lane == CENTRE, cx, built)
        built = jnp.where(lane == CENTRE + 1, cy, built)
        built = jnp.where(lane == CENTRE + 2, cz, built)
        moments[rows, :] = built
        return carry

    lax.fori_loop(0, LEAVES // 8, group_step, 0, unroll=4)
    kind = row & 3
    bx = place[0].astype(f32) + 0.5
    by = place[1].astype(f32) + 0.5
    bodies[8 * LEAVES : 8 * LEAVES + 8, :] = jnp.where(
        kind == 1, bx, jnp.where(kind == 2, by, jnp.where(kind == 3, 0.5, 0.0))
    )
    half_z = CZ // 2
    summed = jnp.zeros((PARENTS, 128), f32)
    for at in range(8):
        first = (at >> 2 & 1) * CY * CZ + (at >> 1 & 1) * CZ + (at & 1)
        piece = jnp.concatenate(
            [moments[pl.ds(first + 2 * CZ * py, half_z, stride=2), :] for py in range(CY // 2)], 0
        )
        summed = summed + jnp.dot(
            piece,
            up[128 * at : 128 * at + 128, :],
            precision=lax.Precision.HIGHEST,
            preferred_element_type=f32,
        )
    lane = lane_ids((PARENTS, 128))
    cell = row_ids((PARENTS, 128))
    summed = jnp.where(lane == CENTRE, place[0].astype(f32) + 1.0, summed)
    summed = jnp.where(
        lane == CENTRE + 1,
        place[1].astype(f32) + 1.0 + 2.0 * (cell // half_z).astype(f32),
        summed,
    )
    summed = jnp.where(lane == CENTRE + 2, 1.0 + 2.0 * (cell % half_z).astype(f32), summed)
    parents[...] = summed
    for way in range(4):

        def leaf_step(k, carry, way=way):
            leaf = send[0, way * SLOTS + k]
            outs[way][pl.ds(pl.multiple_of(8 * k, 8), 8), :] = bodies[
                pl.ds(pl.multiple_of(8 * leaf, 8), 8), :
            ]
            outs[way][pl.ds(BODY_ROWS + k, 1), :] = moments[pl.ds(leaf, 1), :]
            return carry

        lax.fori_loop(0, SLOTS, leaf_step, 0, unroll=8)

        def parent_step(k, carry, way=way):
            cell = send_p[0, way * PSLOTS + k]
            outs[way][pl.ds(BODY_ROWS + SLOTS + k, 1), :] = parents[pl.ds(cell, 1), :]
            return carry

        lax.fori_loop(0, PSLOTS, parent_step, 0, unroll=8)
    words[...] = work_lists(count_row[...], pairs[0], pairs[1], pairs[2])


def wide_rows(bodies, g):
    return [
        jnp.concatenate(
            [bodies[pl.ds(64 * g + 4 * half + at, 8, stride=8), :] for half in range(2)], 1
        )
        for at in range(4)
    ]


def group_centre(place, g):
    cx = (place[0] + g // (CY * CZ // 8)).astype(f32) + 0.5
    cy = (place[1] + g // (CZ // 8) % CY).astype(f32) + 0.5
    base_z = (8 * (g % (CZ // 8))).astype(f32) + 0.5
    return cx, cy, row_ids((8, 1)).astype(f32) + base_z


def work_lists(counts, owned, partner, image):
    wide = (LEAVES, LEAVES)
    every = jnp.broadcast_to(counts.astype(f32), (8, LEAVES)).astype(bf16)

    def count_of(index):
        hot = jnp.where(row_ids(wide) == index, 1.0, 0.0).astype(bf16)
        return jnp.dot(every, hot, preferred_element_type=f32)[:1].astype(i32)

    mine = jnp.logical_and(partner >= 0, partner < LEAVES)
    other = partner >= LEAVES
    count_a = count_of(owned)
    count_b = count_of(partner)
    swapped = count_b < count_a
    lift = (image + 1) << 19
    own_word = (
        jnp.where(swapped, partner, owned)
        | jnp.where(swapped, owned, partner) << 9
        | jnp.where(swapped, 1, 0) << 18
        | lift
        | 4 << 21
    )
    spot = jnp.maximum(partner - LEAVES, 0)
    other_word = owned | spot << 9 | lift | (spot // SLOTS) << 21
    own_empty = LEAVES << 9 | 1 << 19 | 4 << 21
    other_empty = (4 * SLOTS) << 9 | 1 << 19 | 4 << 21
    yes = jnp.ones((1, LEAVES), jnp.bool_)
    lists = [
        (own_word, mine, jnp.minimum(count_a, count_b), own_empty, 2 * GROUP),
        (other_word, other, count_a, other_empty, GROUP),
        (lane_ids((1, LEAVES)), yes, counts, LEAVES, 2 * GROUP),
    ]
    flags = []
    for _, member, need, _, _ in lists:
        for at, size in enumerate(SIZES):
            fits = need <= size
            if at + 1 < len(SIZES):
                fits = jnp.logical_and(fits, need > SIZES[at + 1])
            flags.append(jnp.where(jnp.logical_and(member, fits), 1.0, 0.0))
    flags = jnp.concatenate(flags + [jnp.zeros((16 - len(flags), LEAVES), f32)], 0)
    before = jnp.where(row_ids(wide) < lane_ids(wide), 1.0, 0.0).astype(bf16)
    order = jnp.dot(flags.astype(bf16), before, preferred_element_type=f32)
    number = jnp.sum(flags, axis=1, keepdims=True)
    lane = lane_ids((1, LIST))
    rows = []
    for at, (word, member, _, empty, unit) in enumerate(lists):
        spot = jnp.zeros((1, LEAVES), f32)
        total = jnp.zeros((1, 1), f32)
        ends = []
        for row in range(len(SIZES) * at, len(SIZES) * (at + 1)):
            spot = spot + flags[row : row + 1] * (order[row : row + 1] + total)
            total = total + number[row : row + 1]
            ends.append((total.astype(i32) + (unit - 1)) // unit)
        spot = jnp.where(member, spot, -1.0).astype(i32)
        pieces = jnp.concatenate(
            [word & 255, word >> 8 & 255, word >> 16, jnp.zeros((5, LEAVES), i32)], 0
        )
        hot = jnp.where(row_ids(wide) == spot, 1.0, 0.0).astype(bf16)
        found = lax.dot_general(
            pieces.astype(f32).astype(bf16),
            hot,
            (((1,), (1,)), ((), ())),
            preferred_element_type=f32,
        ).astype(i32)
        joined = found[0:1] | found[1:2] << 8 | found[2:3] << 16
        joined = jnp.concatenate([joined, jnp.zeros((1, LIST - LEAVES), i32)], 1)
        joined = jnp.where(lane < total.astype(i32), joined, empty)
        for size_at, end in enumerate(ends):
            joined = jnp.where(lane == STEPS_AT + size_at, end, joined)
        rows.append(joined)
    return jnp.concatenate(rows + [jnp.zeros((5, LIST), i32)], 0)


def self_kernel(places, words, bodies, field, *scratch):
    place = placing(places)
    field[LEAVES] = jnp.zeros((8, HALF), f32)
    self_loop(words, 2, GROUP, EVERY_SIZE, place, bodies, field, paired(scratch))


def near_kernel(places, words, bodies, field_in, field, *scratch):
    place = placing(places)
    field[...] = field_in[...]
    refs = paired(scratch)
    pair_loop(words, 0, GROUP, EVERY_SIZE, place, False, bodies, bodies, field, field, refs)


def derivatives(x, y, z):
    inverse = lax.rsqrt(x * x + y * y + z * z)
    square = inverse * inverse
    odd = [inverse]
    for _ in range(4):
        odd.append(odd[-1] * square)
    powers = monomials(x, y, z)
    result = {}
    for alpha in MULTI:
        degree = sum(alpha)
        total = None
        for p in range(alpha[0] // 2 + 1):
            for q in range(alpha[1] // 2 + 1):
                for s in range(alpha[2] // 2 + 1):
                    m = p + q + s
                    ways = math.prod(
                        math.factorial(a) // (2**c * math.factorial(c) * math.factorial(a - 2 * c))
                        for a, c in zip(alpha, (p, q, s))
                    )
                    sign = (-1.0) ** (degree - m)
                    double = math.prod(range(1, 2 * (degree - m), 2))
                    term = odd[degree - m] * (sign * double * ways)
                    rest = (alpha[0] - 2 * p, alpha[1] - 2 * q, alpha[2] - 2 * s)
                    if powers[rest] is not None:
                        term = term * powers[rest]
                    total = term if total is None else total + term
        result[alpha] = total
    return result


def remote_kernel(
    places,
    words,
    far,
    cells,
    bodies,
    moments,
    parents,
    in_0,
    in_1,
    in_2,
    in_3,
    field_in,
    field,
    leaf_terms,
    parent_terms,
    out_0,
    out_1,
    out_2,
    out_3,
    far_bodies,
    far_field,
    gather_a,
    gather_b,
    *scratch,
):
    place = placing(places)
    incoming = (in_0, in_1, in_2, in_3)
    outgoing = (out_0, out_1, out_2, out_3)
    field[...] = field_in[...]
    for way in range(4):
        far_bodies[way * SLOTS : (way + 1) * SLOTS] = incoming[way][:BODY_ROWS, :].reshape(
            SLOTS, 8, HALF
        )
    far_bodies[4 * SLOTS] = bodies[LEAVES]
    far_field[...] = jnp.zeros_like(far_field)
    refs = paired(scratch)
    pair_loop(
        words, 1, GROUP // 2, SOME_SIZES, place, True, bodies, far_bodies, field, far_field, refs
    )
    for way in range(4):
        outgoing[way][:BODY_ROWS, :] = far_field[way * SLOTS : (way + 1) * SLOTS].reshape(
            BODY_ROWS, HALF
        )

    def moved(rows, way):
        lane = lane_ids(rows.shape)
        rows = jnp.where(lane == CENTRE, rows + place[2 + 2 * way].astype(f32), rows)
        return jnp.where(lane == CENTRE + 1, rows + place[3 + 2 * way].astype(f32), rows)

    table = [moments[...], parents[...]]
    for way in range(4):
        table.append(moved(incoming[way][BODY_ROWS : BODY_ROWS + SLOTS, :], way))
    for way in range(4):
        table.append(moved(incoming[way][BODY_ROWS + SLOTS :, :], way))
    table.append(jnp.zeros((ENTRIES - OWN - 4 * SLOTS - 4 * PSLOTS, 128), f32))
    columns = jnp.concatenate(table, 0).T[:FEATS]
    columns = jnp.concatenate(split3(columns), 0).astype(bf16)

    def one_hot(index, entries):
        return jnp.where(row_ids((entries, 128)) == index, 1.0, 0.0).astype(bf16)

    def joined(parts):
        return parts[:FEATS] + parts[FEATS : 2 * FEATS] + parts[2 * FEATS :]

    def far_block(block):
        if block < FAR_BLOCKS - 1:
            lanes = slice(128 * block, 128 * block + 128)
            a, b, z = far[0, :, lanes], far[1, :, lanes], far[2, :, lanes]
            used = b >= 0
            b = jnp.where(b >= LEAVES, b + PARENTS, b)
        else:
            blank = jnp.zeros((1, 128 - cells.shape[2]), i32)
            a = jnp.concatenate([cells[0] + LEAVES, blank], 1)
            b = jnp.concatenate([cells[1], blank - 1], 1)
            z = jnp.concatenate([cells[2], blank], 1)
            used = b >= 0
            b = jnp.where(b >= PARENTS, b + (OWN + 4 * SLOTS - PARENTS), b + LEAVES)
            b = jnp.where(used, b, -1)
        a = jnp.where(used, a, -1)
        return a, b, (z * CZ).astype(f32), jnp.where(used, 1.0, 0.0)

    gather_a[...] = jnp.zeros_like(gather_a)
    gather_b[...] = jnp.zeros_like(gather_b)
    place_of = row_ids((FEATS, 128))
    for block in range(FAR_BLOCKS):
        rows = slice(FEATS * block, FEATS * block + FEATS)
        a, b, lift, used = far_block(block)
        got_a = joined(
            jnp.dot(columns[:, :OWN], one_hot(a, OWN), preferred_element_type=f32)
        )
        got_b = joined(jnp.dot(columns, one_hot(b, ENTRIES), preferred_element_type=f32))
        gather_a[rows, :] = jnp.where(place_of == LIVE, used, got_a)
        gather_b[rows, :] = got_b + jnp.where(place_of == CENTRE + 2, lift, 0.0)
    for chunk in range(2):
        start = 8 * chunk * FEATS

        def feature(ref, at, start=start):
            return ref[pl.ds(start + at, 8, stride=FEATS), :]

        def gap(axis):
            return feature(gather_a, CENTRE + axis) - feature(gather_b, CENTRE + axis)

        live = feature(gather_a, LIVE) > 0.0
        x = jnp.where(live, gap(0), 3.0)
        y = jnp.where(live, gap(1), 3.0)
        z = jnp.where(live, gap(2), 3.0)
        tensors = derivatives(x, y, z)
        held_a = {}
        held_b = {}
        for alpha in MULTI:
            held_a[alpha] = feature(gather_a, PLACE[alpha]) * (-1.0 / fact(alpha))
            held_b[alpha] = feature(gather_b, PLACE[alpha]) * (
                -((-1.0) ** sum(alpha)) / fact(alpha)
            )
        for beta in MULTI:
            to_a = None
            to_b = None
            for alpha in MULTI:
                if sum(alpha) + sum(beta) > 4:
                    continue
                tensor = tensors[added(alpha, beta)]
                term_a = held_b[alpha] * tensor
                term_b = held_a[alpha] * tensor
                to_a = term_a if to_a is None else to_a + term_a
                to_b = term_b if to_b is None else to_b + term_b
            if sum(beta) % 2:
                to_b = -to_b
            gather_a[pl.ds(start + PLACE[beta], 8, stride=FEATS), :] = to_a
            gather_b[pl.ds(start + PLACE[beta], 8, stride=FEATS), :] = to_b
    sums_a = jnp.zeros((3 * FEATS, OWN), f32)
    sums_b = jnp.zeros((3 * FEATS, ENTRIES), f32)
    turned = (((1,), (1,)), ((), ()))
    for block in range(FAR_BLOCKS):
        rows = slice(FEATS * block, FEATS * block + FEATS)
        a, b, _, _ = far_block(block)
        parts_a = jnp.concatenate(split3(gather_a[rows, :]), 0).astype(bf16)
        parts_b = jnp.concatenate(split3(gather_b[rows, :]), 0).astype(bf16)
        hot_a = one_hot(a, OWN)
        hot_b = one_hot(b, ENTRIES)
        sums_a = sums_a + lax.dot_general(parts_a, hot_a, turned, preferred_element_type=f32)
        sums_b = sums_b + lax.dot_general(parts_b, hot_b, turned, preferred_element_type=f32)
    got_a = jnp.concatenate([joined(sums_a), jnp.zeros((128 - FEATS, OWN), f32)], 0)
    got_b = jnp.concatenate([joined(sums_b), jnp.zeros((128 - FEATS, ENTRIES), f32)], 0)
    keep = lane_ids((1, 128)) < TERMS
    terms_a = jnp.where(keep, got_a.T, 0.0)
    terms_b = jnp.where(keep, got_b.T, 0.0)
    leaf_terms[...] = terms_a[:LEAVES] + terms_b[:LEAVES]
    parent_terms[...] = terms_a[LEAVES:OWN] + terms_b[LEAVES:OWN]
    leaf_start = OWN
    parent_start = OWN + 4 * SLOTS
    for way in range(4):
        first = leaf_start + way * SLOTS
        outgoing[way][BODY_ROWS : BODY_ROWS + SLOTS, :] = terms_b[first : first + SLOTS]
        first = parent_start + way * PSLOTS
        outgoing[way][BODY_ROWS + SLOTS :, :] = terms_b[first : first + PSLOTS]


def back_kernel(
    places,
    counts,
    send,
    send_p,
    bodies,
    field_in,
    leaf_in,
    parent_in,
    down,
    in_0,
    in_1,
    in_2,
    in_3,
    out,
    leaf_terms,
    parent_terms,
    field,
    tiles,
):
    place = placing(places)
    incoming = (in_0, in_1, in_2, in_3)
    leaf_terms[...] = leaf_in[...]
    parent_terms[...] = parent_in[...]
    field[...] = field_in[...]
    for way in range(4):

        def leaf_step(k, carry, way=way):
            leaf = send[0, way * SLOTS + k]
            field[leaf] = field[leaf] + incoming[way][pl.ds(pl.multiple_of(8 * k, 8), 8), :]
            leaf_terms[pl.ds(leaf, 1), :] = (
                leaf_terms[pl.ds(leaf, 1), :] + incoming[way][pl.ds(BODY_ROWS + k, 1), :]
            )
            return carry

        lax.fori_loop(0, SLOTS, leaf_step, 0, unroll=8)

        def parent_step(k, carry, way=way):
            cell = send_p[0, way * PSLOTS + k]
            parent_terms[pl.ds(cell, 1), :] = (
                parent_terms[pl.ds(cell, 1), :] + incoming[way][pl.ds(BODY_ROWS + SLOTS + k, 1), :]
            )
            return carry

        lax.fori_loop(0, PSLOTS, parent_step, 0, unroll=8)
    half_z = CZ // 2
    for at in range(8):
        moved = jnp.dot(
            parent_terms[...],
            down[:, 128 * at : 128 * at + 128],
            precision=lax.Precision.HIGHEST,
            preferred_element_type=f32,
        )
        first = (at >> 2 & 1) * CY * CZ + (at >> 1 & 1) * CZ + (at & 1)
        for py in range(CY // 2):
            rows = pl.ds(first + 2 * CZ * py, half_z, stride=2)
            leaf_terms[rows, :] = leaf_terms[rows, :] + moved[half_z * py : half_z * py + half_z]

    lane = lane_ids((8, 128))
    inverse_factorials = jnp.zeros((8, 128), f32)
    for alpha in MULTI:
        inverse_factorials = jnp.where(lane == PLACE[alpha], 1.0 / fact(alpha), inverse_factorials)

    def group_step(g, carry):
        rows = pl.ds(pl.multiple_of(8 * g, 8), 8)
        cx, cy, cz = group_centre(place, g)
        _, px, py, pz = wide_rows(bodies, g)
        x, y, z = px - cx, py - cy, pz - cz
        terms = leaf_terms[rows, :] * inverse_factorials

        def coefficient(*alpha):
            at = PLACE[alpha]
            return jnp.broadcast_to(terms[:, at : at + 1], (8, LEAF))

        def nested(values, t):
            total, slope = values[-1], None
            for value in values[-2::-1]:
                slope = total if slope is None else slope * t + total
                total = total * t + value
            return total, slope

        def plain(values, t):
            total = values[-1]
            for value in values[-2::-1]:
                total = total * t + value
            return total

        by_x = []
        by_x_y = []
        by_x_z = []
        for i in range(5):
            in_z = [
                nested([coefficient(i, j, k) for k in range(5 - i - j)], z) for j in range(5 - i)
            ]
            value, slope = nested([pair[0] for pair in in_z], y)
            by_x.append(value)
            if i < 4:
                by_x_y.append(slope)
                by_x_z.append(plain([pair[1] for pair in in_z[:-1]], y))
        value, slope = nested(by_x, x)
        values = [value, -slope, -plain(by_x_y, x), -plain(by_x_z, x)]
        for at, value in enumerate(values):
            tiles[pl.ds(64 * g + at, 8, stride=8), :] = value[:, :HALF]
            tiles[pl.ds(64 * g + 4 + at, 8, stride=8), :] = value[:, HALF:]
        row = row_ids((8, HALF))
        body = lane_ids((8, HALF)) + jnp.where(row < 4, 0, HALF)
        for u in range(8):
            leaf = 8 * g + u
            tile = tiles[pl.ds(pl.multiple_of(8 * leaf, 8), 8), :] + field[leaf]
            tile = jnp.where(body < counts[leaf], tile, 0.0)
            start = pl.multiple_of(leaf * LEAF, LEAF)
            out[:, pl.ds(start, HALF)] = tile[:4]
            out[:, pl.ds(start + HALF, HALF)] = tile[4:]
        return carry

    lax.fori_loop(0, LEAVES // 8, group_step, 0, unroll=2)


VMEM = pl.BlockSpec(memory_space=pltpu.VMEM)
SMEM = pl.BlockSpec(memory_space=pltpu.SMEM)
HBM = pl.BlockSpec(memory_space=pltpu.HBM)
params = pltpu.CompilerParams(vmem_limit_bytes=20 * 1024 * 1024)
packed = jax.ShapeDtypeStruct((PACK_ROWS, 128), f32)
tiled = jax.ShapeDtypeStruct((LEAVES + 1, 8, HALF), f32)
heavy = pl.CostEstimate(flops=20_000_000_000, bytes_accessed=2_000_000, transcendentals=0)


def shaped(*dims):
    return jax.ShapeDtypeStruct(dims, f32)


def on_device(
    positions, masses, leaf_counts, send_leaves, send_parents, near_pairs, far_pairs, parent_pairs
):
    slab_count = lax.axis_size("slab")
    sub_count = lax.axis_size("sub")
    places = (slab_count, sub_count)

    def rows_first(lists):
        return jnp.transpose(lists, (1, 0, 2))

    sent = pl.pallas_call(
        functools.partial(front_kernel, places),
        out_shape=[shaped(8 * LEAVES + 8, HALF), shaped(LEAVES, 128), shaped(PARENTS, 128)]
        + [jax.ShapeDtypeStruct((8, LIST), i32)]
        + [packed] * 4,
        in_specs=[HBM] * 7,
        out_specs=[VMEM] * 8,
        scratch_shapes=[
            pltpu.SMEM(send_leaves.shape, i32),
            pltpu.SMEM(send_parents.shape, i32),
            pltpu.SMEM((1, LEAVES), i32),
            pltpu.VMEM((1, LEAVES), i32),
            pltpu.VMEM((3, 1, near_pairs.shape[2]), i32),
            pltpu.VMEM(positions.shape, f32),
            pltpu.VMEM((2 * LEAVES, HALF), f32),
            pltpu.VMEM(UP.shape, f32),
            pltpu.SemaphoreType.DMA((8,)),
        ],
        compiler_params=params,
        name="moments_and_packing",
    )(
        send_leaves,
        send_parents,
        leaf_counts.reshape(1, LEAVES),
        rows_first(near_pairs),
        positions,
        masses.reshape(2 * LEAVES, HALF),
        jnp.asarray(UP),
    )
    bodies = sent[0].reshape(LEAVES + 1, 8, HALF)
    moments, parents, words = sent[1:4]

    def exchange(value, way, back):
        pairs = []
        for s in range(slab_count):
            for u in range(sub_count):
                here = s * sub_count + u
                there = (s + slab_steps[way]) % slab_count * sub_count + (
                    u + sub_steps[way]
                ) % sub_count
                pairs.append((here, there) if back else (there, here))
        return lax.ppermute(value, ("slab", "sub"), pairs)

    incoming = [exchange(sent[4 + way], way, False) for way in range(4)]

    field = pl.pallas_call(
        functools.partial(self_kernel, places),
        out_shape=tiled,
        in_specs=[SMEM, VMEM],
        out_specs=VMEM,
        scratch_shapes=[pltpu.VMEM((GROUP, LEAF, LEAF), bf16)] * 4
        + [pltpu.VMEM((GROUP, 32, LEAF), bf16)] * 2
        + [pltpu.VMEM((GROUP, 2, 8, LEAF), f32)] * 2,
        compiler_params=params,
        cost_estimate=heavy,
        name="self_pairs",
    )(words, bodies)

    middle = pl.pallas_call(
        functools.partial(remote_kernel, places),
        out_shape=[tiled, shaped(LEAVES, 128), shaped(PARENTS, 128)] + [packed] * 4,
        in_specs=[SMEM] + [VMEM] * 10,
        out_specs=[VMEM] * 7,
        scratch_shapes=[
            pltpu.VMEM((4 * SLOTS + 1, 8, HALF), f32),
            pltpu.VMEM((4 * SLOTS + 1, 8, HALF), f32),
            pltpu.VMEM((16 * FEATS, 128), f32),
            pltpu.VMEM((16 * FEATS, 128), f32),
        ]
        + pair_scratch(GROUP // 2),
        compiler_params=params,
        name="pairs_with_others",
    )(
        words,
        rows_first(far_pairs),
        rows_first(parent_pairs),
        bodies,
        moments,
        parents,
        *incoming,
        field,
    )
    field, leaf_terms, parent_terms = middle[:3]
    arrived = [exchange(middle[3 + way], way, True) for way in range(4)]

    field = pl.pallas_call(
        functools.partial(near_kernel, places),
        out_shape=tiled,
        in_specs=[SMEM] + [VMEM] * 2,
        out_specs=VMEM,
        scratch_shapes=pair_scratch(GROUP),
        compiler_params=params,
        cost_estimate=heavy,
        name="own_pairs",
    )(words, bodies, field)

    return pl.pallas_call(
        functools.partial(back_kernel, places),
        out_shape=jax.ShapeDtypeStruct((4, LEAVES * LEAF), f32),
        in_specs=[SMEM] * 3 + [VMEM] * 9,
        out_specs=VMEM,
        scratch_shapes=[
            pltpu.VMEM((LEAVES, 128), f32),
            pltpu.VMEM((PARENTS, 128), f32),
            pltpu.VMEM((LEAVES + 1, 8, HALF), f32),
            pltpu.VMEM((8 * LEAVES, HALF), f32),
        ],
        compiler_params=params,
        name="shift_and_evaluate",
    )(
        leaf_counts,
        send_leaves,
        send_parents,
        sent[0],
        field,
        leaf_terms,
        parent_terms,
        jnp.asarray(DOWN),
        *arrived,
    )


def solution(mesh):
    return jax.shard_map(
        on_device,
        mesh=mesh,
        in_specs=(
            P(None, ("slab", "sub")),
            P(("slab", "sub")),
            P(("slab", "sub")),
            P(("slab", "sub"), None),
            P(("slab", "sub"), None),
            P(("slab", "sub"), None, None),
            P(("slab", "sub"), None, None),
            P(("slab", "sub"), None, None),
        ),
        out_specs=P(None, ("slab", "sub")),
        check_vma=False,
    )
```

```python
import functools
import math

import jax
import jax.numpy as jnp
import numpy as np
from jax import lax
from jax.experimental import pallas as pl
from jax.experimental.pallas import tpu as pltpu
from jax.sharding import PartitionSpec as P

CX = 2
CY = 4
CZ = 32

soft_square = 0.0025
slab_steps = (1, 0, 1, 1)
sub_steps = (0, 1, 1, -1)

LEAVES = CX * CY * CZ
PARENTS = LEAVES // 8
SLOTS = LEAVES // 4
PSLOTS = PARENTS // 2
HALF = 128
LEAF = 2 * HALF
BODY_ROWS = 8 * SLOTS
PACK_ROWS = BODY_ROWS + SLOTS + PSLOTS
GROUP = 8
bf16 = jnp.bfloat16
f32 = jnp.float32
i32 = jnp.int32

MULTI = [
    (i, j, n - i - j) for n in range(5) for i in range(n, -1, -1) for j in range(n - i, -1, -1)
]
PLACE = {alpha: at for at, alpha in enumerate(MULTI)}
TERMS = len(MULTI)
CENTRE = TERMS
LIVE = TERMS + 3
SIZES = (256, 192, 160, 128, 96)
EVERY_SIZE = tuple((size, at) for at, size in enumerate(SIZES))
SOME_SIZES = ((256, 0), (192, 2), (128, 4))
LIST = 384
STEPS_AT = LIST - 8
FEATS = 40
OWN = LEAVES + PARENTS
ENTRIES = 640
FAR_BLOCKS = 9


def fact(alpha):
    return math.prod(math.factorial(a) for a in alpha)


def added(alpha, beta):
    return tuple(a + b for a, b in zip(alpha, beta))


def taken(alpha, beta):
    return tuple(a - b for a, b in zip(alpha, beta))


def octant(at):
    return tuple(0.5 if bit else -0.5 for bit in (at >> 2 & 1, at >> 1 & 1, at & 1))


def power(delta, alpha):
    return math.prod(d**a for d, a in zip(delta, alpha))


def shift_matrices():
    up = np.zeros((8, 128, 128), np.float32)
    down = np.zeros((8, 128, 128), np.float32)
    for at in range(8):
        delta = octant(at)
        for alpha in MULTI:
            for beta in MULTI:
                rest = taken(alpha, beta)
                if min(rest) < 0:
                    continue
                choose = math.prod(math.comb(a, b) for a, b in zip(alpha, beta))
                up[at, PLACE[beta], PLACE[alpha]] = choose * power(delta, rest)
                down[at, PLACE[alpha], PLACE[beta]] = power(delta, rest) / fact(rest)
    return up.reshape(8 * 128, 128), down.transpose(1, 0, 2).reshape(128, 8 * 128)


UP, DOWN = shift_matrices()


def row_ids(shape):
    return lax.broadcasted_iota(i32, shape, 0)


def lane_ids(shape):
    return lax.broadcasted_iota(i32, shape, 1)


def monomials(x, y, z):
    table = {(0, 0, 0): None}
    axes = (x, y, z)
    for alpha in MULTI[1:]:
        lead = max(axis for axis in range(3) if alpha[axis])
        less = tuple(a - (axis == lead) for axis, a in enumerate(alpha))
        table[alpha] = axes[lead] if table[less] is None else table[less] * axes[lead]
    return table


def split3(value):
    high = value.astype(bf16).astype(f32)
    rest = value - high
    middle = rest.astype(bf16).astype(f32)
    return high, middle, rest - middle


def spread(tile):
    row = row_ids((8, HALF))
    turned = pltpu.roll(tile, 4, 0)
    low = row < 4
    return jnp.concatenate([jnp.where(low, tile, turned), jnp.where(low, turned, tile)], 1)


def fold(field):
    row = row_ids((8, HALF))
    return jnp.where(row < 4, field[:, :HALF], pltpu.roll(field[:, HALF:], 4, 0))


def offset_rows(ox, oy, oz):
    row = row_ids((8, LEAF)) & 3
    return jnp.where(row == 1, ox, jnp.where(row == 2, oy, jnp.where(row == 3, oz, 0.0)))


def features(tile, offset, as_row, as_column, as_weight):
    wide = spread(tile)
    row = row_ids((8, LEAF))
    first = (row & 3) == 0
    low = row < 4
    weight = jnp.broadcast_to(wide[0:1], (8, LEAF))
    x = jnp.where(first, 0.0, wide + offset)
    square = x * x
    pairwise = square + pltpu.roll(square, 1, 0)
    q = pairwise + pltpu.roll(pairwise, 2, 0)
    y = jnp.where(first, q, x)
    zero = jnp.zeros((8, LEAF), f32)
    out = [x, q]
    if as_row:
        h, m, l = split3(y)
        part_a = jnp.where(row == 4, m, h)
        part_b = jnp.where(row == 0, l, jnp.where(row == 4, 1.0, m))
        part_c = jnp.where(first, 1.0, jnp.where(low, h, l))
        out.append(jnp.concatenate([part_a, part_b, part_c, zero], 0).astype(bf16))
    if as_column:
        h, m, l = split3(jnp.where(first, q + soft_square, x * -2.0))
        mixed = jnp.where(low, h, m)
        part_a = jnp.where(first, 1.0, mixed)
        part_b = jnp.where(row == 0, 1.0, jnp.where(row == 4, h, mixed))
        part_c = jnp.where(row == 0, m, jnp.where(row == 4, l, jnp.where(low, l, h)))
        out.append(jnp.concatenate([part_a, part_b, part_c, zero], 0).astype(bf16))
    if as_weight:
        heavy = jnp.where(low, y, 1.0) * weight
        out.append(jnp.concatenate(list(split3(heavy)) + [zero], 0).astype(bf16))
    return out


def field_of(sums, x, q):
    total = sums[0:8] + sums[8:16] + sums[16:24]
    row = row_ids((8, LEAF))
    first = (row & 3) == 0
    plain = pltpu.roll(total, 4, 0)
    inner = total - jnp.where(first, q - soft_square, x) * plain
    along = x * inner
    dots = along[1:2] + along[2:3] + along[3:4]
    return fold(jnp.where(row == 0, 2.0 * dots - inner, inner))


def cubes(row_part, column_part):
    square = lax.dot_general(
        row_part, column_part, (((0,), (0,)), ((), ())), preferred_element_type=f32
    )
    inverse = lax.rsqrt(square)
    return inverse * inverse * inverse


def padded(sums):
    lanes = sums.shape[1]
    if lanes == LEAF:
        return sums
    return jnp.concatenate([sums, jnp.zeros((sums.shape[0], LEAF - lanes), f32)], 1)


def pipeline(words, at, group, plan, early, late):
    @pl.when(words[at, STEPS_AT + len(SIZES) - 1] > 0)
    def _():
        for u in range(group):
            early(SIZES[0], 0, 0, u)

    begin = jnp.int32(0)
    for size, last in plan:

        def step(k, carry, size=size):
            for slot in range(2):
                done = []
                for u in range(group):
                    done.append(late(size, 2 * k + slot, slot, u))
                    early(size, 2 * k + slot + 1, 1 - slot, u)
                for store in done:
                    store()
            return carry

        end = words[at, STEPS_AT + last]
        lax.fori_loop(begin, end, step, 0)
        begin = end


def placing(places):
    slab_count, sub_count = places
    slab_at = lax.axis_index("slab")
    sub_at = lax.axis_index("sub")
    numbers = [slab_at * CX, sub_at * CY]
    for way in range(4):
        reach_x = slab_at + slab_steps[way]
        reach_y = sub_at + sub_steps[way]
        numbers.append(jnp.where(reach_x >= slab_count, slab_count * CX, 0))
        high = jnp.where(reach_y >= sub_count, sub_count * CY, 0)
        numbers.append(jnp.where(reach_y < 0, -sub_count * CY, high))
    return numbers


def jump_of(place, way):
    jump_x = jnp.int32(0)
    jump_y = jnp.int32(0)
    for at in range(4):
        jump_x = jnp.where(way == at, place[2 + 2 * at], jump_x)
        jump_y = jnp.where(way == at, place[3 + 2 * at], jump_y)
    return jump_x.astype(f32), jump_y.astype(f32)


def leaf_centre(place, leaf):
    return (
        -(place[0] + leaf // (CY * CZ)).astype(f32) - 0.5,
        -(place[1] + leaf // CZ % CY).astype(f32) - 0.5,
        -(leaf % CZ).astype(f32) - 0.5,
    )


def halves(c):
    high = c.astype(bf16)
    return high, (c - high.astype(f32)).astype(bf16)


def self_loop(words, at, group, plan, place, bodies, field, scratch):
    high_refs, low_refs, weight_refs, spot_refs = scratch

    def early(size, k, slot, u):
        leaf = words[at, k * group + u]
        x, q, rows, columns, weights = features(
            bodies[leaf], offset_rows(*leaf_centre(place, leaf & (LEAVES - 1))), True, True, True
        )
        wide = LEAF if size > HALF else HALF
        high, low = halves(cubes(rows[:, :size], columns[:, :wide]))
        high_refs[slot][u, :size, :wide] = high
        low_refs[slot][u, :size, :wide] = low
        weight_refs[slot][u] = weights
        spot_refs[slot][u, 0] = x
        spot_refs[slot][u, 1] = q

    def late(size, k, slot, u):
        leaf = words[at, k * group + u]
        wide = LEAF if size > HALF else HALF
        w = weight_refs[slot][u, :, :size]
        sums = jnp.dot(
            w, high_refs[slot][u, :size, :wide], preferred_element_type=f32
        ) + jnp.dot(w, low_refs[slot][u, :size, :wide], preferred_element_type=f32)
        result = field_of(padded(sums), spot_refs[slot][u, 0], spot_refs[slot][u, 1])
        itself = jnp.where((row_ids((8, HALF)) & 3) == 0, bodies[leaf], 0.0)
        result = result + itself * soft_square**-0.5

        def store():
            field[leaf] = result

        return store

    pipeline(words, at, group, plan, early, late)


def pair_loop(
    words, at, group, plan, place, jumping, bodies, others, field, other_field, scratch
):
    high_refs, low_refs, across_refs, row_refs, column_refs, spot_refs = scratch
    turned = (((1,), (1,)), ((), ()))

    def unpack(k, u):
        word = words[at, k * group + u]
        return word & 511, word >> 9 & 511, word >> 18 & 1, (word >> 19 & 3) - 1, word >> 21 & 7

    def early(size, k, slot, u):
        row_leaf, column_leaf, swapped, lift, way = unpack(k, u)
        frame = jnp.where(swapped == 1, column_leaf, row_leaf) & (LEAVES - 1)
        cx, cy, cz = leaf_centre(place, frame)
        raised = (lift * CZ).astype(f32)
        swap = (swapped == 1).astype(f32)
        jump_x, jump_y = jump_of(place, way) if jumping else (0.0, 0.0)
        row_offset = offset_rows(cx, cy, cz + swap * raised)
        column_offset = offset_rows(cx + jump_x, cy + jump_y, cz + (1.0 - swap) * raised)
        xr, qr, rows, row_weights = features(bodies[row_leaf], row_offset, True, False, True)
        xc, qc, columns, column_weights = features(
            others[column_leaf], column_offset, False, True, True
        )
        high, low = halves(cubes(rows[:, :size], columns))
        high_refs[slot][u, :size] = high
        low_refs[slot][u, :size] = low
        if size == LEAF:
            across_refs[slot][u] = high.T
        row_refs[slot][u] = row_weights
        column_refs[slot][u] = column_weights
        spot_refs[slot][u, 0] = xr
        spot_refs[slot][u, 1] = qr
        spot_refs[slot][u, 2] = xc
        spot_refs[slot][u, 3] = qc

    def late(size, k, slot, u):
        row_leaf, column_leaf, _, _, _ = unpack(k, u)
        wr = row_refs[slot][u, :, :size]
        wc = column_refs[slot][u]
        high = high_refs[slot][u, :size]
        low = low_refs[slot][u, :size]
        column_sums = jnp.dot(wr, high, preferred_element_type=f32) + jnp.dot(
            wr, low, preferred_element_type=f32
        )
        row_sums = lax.dot_general(wc, low, turned, preferred_element_type=f32)
        if size == LEAF:
            row_sums += jnp.dot(wc, across_refs[slot][u], preferred_element_type=f32)
        else:
            row_sums += lax.dot_general(wc, high, turned, preferred_element_type=f32)
        row_field = field_of(padded(row_sums), spot_refs[slot][u, 0], spot_refs[slot][u, 1])
        column_field = field_of(column_sums, spot_refs[slot][u, 2], spot_refs[slot][u, 3])

        def store():
            field[row_leaf] = field[row_leaf] + row_field
            other_field[column_leaf] = other_field[column_leaf] + column_field

        return store

    pipeline(words, at, group, plan, early, late)


def pair_scratch(group):
    return (
        [pltpu.VMEM((group, LEAF, LEAF), bf16)] * 6
        + [pltpu.VMEM((group, 32, LEAF), bf16)] * 4
        + [pltpu.VMEM((group, 4, 8, LEAF), f32)] * 2
    )


def paired(scratch):
    return [scratch[at : at + 2] for at in range(0, len(scratch), 2)]


def front_kernel(places, *refs):
    stored, made, held, sems = refs[:7], refs[7:15], refs[15:23], refs[23]
    bodies, moments, parents, words = made[:4]
    outs = made[4:]
    sources = (stored[0], stored[1], stored[2], *stored[2:])
    copies = [
        pltpu.make_async_copy(source, target, sems.at[at])
        for at, (source, target) in enumerate(zip(sources, held))
    ]
    for copy in copies:
        copy.start()
    send, send_p, counts, count_row, pairs, spots, masses, up = held
    place = placing(places)
    copies[3].wait()
    copies[4].wait()
    words[...] = work_lists(count_row[...], pairs[0], pairs[1], pairs[2])
    copies[2].wait()
    copies[5].wait()
    copies[6].wait()
    row = row_ids((8, HALF))

    def tile_step(g, carry):
        count = jnp.zeros((8, HALF), i32)
        for u in range(8):
            leaf = 8 * g + u
            start = pl.multiple_of(leaf * LEAF, LEAF)
            low = spots[:, pl.ds(start, HALF)]
            high = spots[:, pl.ds(start + HALF, HALF)]
            blank = jnp.zeros((1, HALF), f32)
            bodies[pl.ds(pl.multiple_of(8 * leaf, 8), 8), :] = jnp.concatenate(
                [blank, low, blank, high], 0
            )
            count = jnp.where(row == u, counts[0, leaf], count)
        lane = lane_ids((8, HALF))
        for half in range(2):
            mass = masses[pl.ds(16 * g + half, 8, stride=2), :]
            bodies[pl.ds(64 * g + 4 * half, 8, stride=8), :] = jnp.where(
                lane + half * HALF < count, mass, 0.0
            )
        return carry

    lax.fori_loop(0, LEAVES // 8, tile_step, 0, unroll=4)

    def group_step(g, carry):
        rows = pl.ds(pl.multiple_of(8 * g, 8), 8)
        w, px, py, pz = wide_rows(bodies, g)
        cx, cy, cz = group_centre(place, g)
        axes = (px - cx, py - cy, pz - cz)
        table = {(0, 0, 0): w}
        lane = lane_ids((8, 128))
        built = jnp.zeros((8, 128), f32)
        for alpha in MULTI:
            if alpha not in table:
                lead = max(axis for axis in range(3) if alpha[axis])
                less = tuple(a - (axis == lead) for axis, a in enumerate(alpha))
                table[alpha] = table[less] * axes[lead]
            value = table[alpha]
            total = jnp.sum(value[:, :HALF] + value[:, HALF:], axis=1, keepdims=True)
            built = jnp.where(lane == PLACE[alpha], total, built)
        built = jnp.where(lane == CENTRE, cx, built)
        built = jnp.where(lane == CENTRE + 1, cy, built)
        built = jnp.where(lane == CENTRE + 2, cz, built)
        moments[rows, :] = built
        return carry

    lax.fori_loop(0, LEAVES // 8, group_step, 0, unroll=4)
    kind = row & 3
    bx = place[0].astype(f32) + 0.5
    by = place[1].astype(f32) + 0.5
    bodies[8 * LEAVES : 8 * LEAVES + 8, :] = jnp.where(
        kind == 1, bx, jnp.where(kind == 2, by, jnp.where(kind == 3, 0.5, 0.0))
    )
    copies[7].wait()
    half_z = CZ // 2
    summed = jnp.zeros((PARENTS, 128), f32)
    for at in range(8):
        first = (at >> 2 & 1) * CY * CZ + (at >> 1 & 1) * CZ + (at & 1)
        piece = jnp.concatenate(
            [moments[pl.ds(first + 2 * CZ * py, half_z, stride=2), :] for py in range(CY // 2)], 0
        )
        summed = summed + jnp.dot(
            piece,
            up[128 * at : 128 * at + 128, :],
            precision=lax.Precision.HIGHEST,
            preferred_element_type=f32,
        )
    lane = lane_ids((PARENTS, 128))
    cell = row_ids((PARENTS, 128))
    summed = jnp.where(lane == CENTRE, place[0].astype(f32) + 1.0, summed)
    summed = jnp.where(
        lane == CENTRE + 1,
        place[1].astype(f32) + 1.0 + 2.0 * (cell // half_z).astype(f32),
        summed,
    )
    summed = jnp.where(lane == CENTRE + 2, 1.0 + 2.0 * (cell % half_z).astype(f32), summed)
    parents[...] = summed
    copies[0].wait()
    copies[1].wait()
    for way in range(4):

        def leaf_step(k, carry, way=way):
            leaf = send[0, way * SLOTS + k]
            outs[way][pl.ds(pl.multiple_of(8 * k, 8), 8), :] = bodies[
                pl.ds(pl.multiple_of(8 * leaf, 8), 8), :
            ]
            outs[way][pl.ds(BODY_ROWS + k, 1), :] = moments[pl.ds(leaf, 1), :]
            return carry

        lax.fori_loop(0, SLOTS, leaf_step, 0, unroll=8)

        def parent_step(k, carry, way=way):
            cell = send_p[0, way * PSLOTS + k]
            outs[way][pl.ds(BODY_ROWS + SLOTS + k, 1), :] = parents[pl.ds(cell, 1), :]
            return carry

        lax.fori_loop(0, PSLOTS, parent_step, 0, unroll=8)


def wide_rows(bodies, g):
    return [
        jnp.concatenate(
            [bodies[pl.ds(64 * g + 4 * half + at, 8, stride=8), :] for half in range(2)], 1
        )
        for at in range(4)
    ]


def group_centre(place, g):
    cx = (place[0] + g // (CY * CZ // 8)).astype(f32) + 0.5
    cy = (place[1] + g // (CZ // 8) % CY).astype(f32) + 0.5
    base_z = (8 * (g % (CZ // 8))).astype(f32) + 0.5
    return cx, cy, row_ids((8, 1)).astype(f32) + base_z


def work_lists(counts, owned, partner, image):
    wide = (LEAVES, LEAVES)
    every = jnp.broadcast_to(counts.astype(f32), (8, LEAVES)).astype(bf16)

    def count_of(index):
        hot = jnp.where(row_ids(wide) == index, 1.0, 0.0).astype(bf16)
        return jnp.dot(every, hot, preferred_element_type=f32)[:1].astype(i32)

    mine = jnp.logical_and(partner >= 0, partner < LEAVES)
    other = partner >= LEAVES
    count_a = count_of(owned)
    count_b = count_of(partner)
    swapped = count_b < count_a
    lift = (image + 1) << 19
    own_word = (
        jnp.where(swapped, partner, owned)
        | jnp.where(swapped, owned, partner) << 9
        | jnp.where(swapped, 1, 0) << 18
        | lift
        | 4 << 21
    )
    spot = jnp.maximum(partner - LEAVES, 0)
    other_word = owned | spot << 9 | lift | (spot // SLOTS) << 21
    own_empty = LEAVES << 9 | 1 << 19 | 4 << 21
    other_empty = (4 * SLOTS) << 9 | 1 << 19 | 4 << 21
    yes = jnp.ones((1, LEAVES), jnp.bool_)
    lists = [
        (own_word, mine, jnp.minimum(count_a, count_b), own_empty, 2 * GROUP),
        (other_word, other, count_a, other_empty, GROUP),
        (lane_ids((1, LEAVES)), yes, counts, LEAVES, 2 * GROUP),
    ]
    flags = []
    for _, member, need, _, _ in lists:
        for at, size in enumerate(SIZES):
            fits = need <= size
            if at + 1 < len(SIZES):
                fits = jnp.logical_and(fits, need > SIZES[at + 1])
            flags.append(jnp.where(jnp.logical_and(member, fits), 1.0, 0.0))
    flags = jnp.concatenate(flags + [jnp.zeros((16 - len(flags), LEAVES), f32)], 0)
    before = jnp.where(row_ids(wide) < lane_ids(wide), 1.0, 0.0).astype(bf16)
    order = jnp.dot(flags.astype(bf16), before, preferred_element_type=f32)
    number = jnp.sum(flags, axis=1, keepdims=True)
    lane = lane_ids((1, LIST))
    rows = []
    for at, (word, member, _, empty, unit) in enumerate(lists):
        spot = jnp.zeros((1, LEAVES), f32)
        total = jnp.zeros((1, 1), f32)
        ends = []
        for row in range(len(SIZES) * at, len(SIZES) * (at + 1)):
            spot = spot + flags[row : row + 1] * (order[row : row + 1] + total)
            total = total + number[row : row + 1]
            ends.append((total.astype(i32) + (unit - 1)) // unit)
        spot = jnp.where(member, spot, -1.0).astype(i32)
        pieces = jnp.concatenate(
            [word & 255, word >> 8 & 255, word >> 16, jnp.zeros((5, LEAVES), i32)], 0
        )
        hot = jnp.where(row_ids(wide) == spot, 1.0, 0.0).astype(bf16)
        found = lax.dot_general(
            pieces.astype(f32).astype(bf16),
            hot,
            (((1,), (1,)), ((), ())),
            preferred_element_type=f32,
        ).astype(i32)
        joined = found[0:1] | found[1:2] << 8 | found[2:3] << 16
        joined = jnp.concatenate([joined, jnp.zeros((1, LIST - LEAVES), i32)], 1)
        joined = jnp.where(lane < total.astype(i32), joined, empty)
        for size_at, end in enumerate(ends):
            joined = jnp.where(lane == STEPS_AT + size_at, end, joined)
        rows.append(joined)
    return jnp.concatenate(rows + [jnp.zeros((5, LIST), i32)], 0)


def self_kernel(places, words, bodies, field, *scratch):
    place = placing(places)
    field[LEAVES] = jnp.zeros((8, HALF), f32)
    self_loop(words, 2, GROUP, EVERY_SIZE, place, bodies, field, paired(scratch))


def near_kernel(places, words, bodies, field_in, field, *scratch):
    place = placing(places)
    refs = paired(scratch)
    pair_loop(words, 0, GROUP, EVERY_SIZE, place, False, bodies, bodies, field, field, refs)


def derivatives(x, y, z):
    inverse = lax.rsqrt(x * x + y * y + z * z)
    square = inverse * inverse
    odd = [inverse]
    for _ in range(4):
        odd.append(odd[-1] * square)
    powers = monomials(x, y, z)
    result = {}
    for alpha in MULTI:
        degree = sum(alpha)
        total = None
        for p in range(alpha[0] // 2 + 1):
            for q in range(alpha[1] // 2 + 1):
                for s in range(alpha[2] // 2 + 1):
                    m = p + q + s
                    ways = math.prod(
                        math.factorial(a) // (2**c * math.factorial(c) * math.factorial(a - 2 * c))
                        for a, c in zip(alpha, (p, q, s))
                    )
                    sign = (-1.0) ** (degree - m)
                    double = math.prod(range(1, 2 * (degree - m), 2))
                    term = odd[degree - m] * (sign * double * ways)
                    rest = (alpha[0] - 2 * p, alpha[1] - 2 * q, alpha[2] - 2 * s)
                    if powers[rest] is not None:
                        term = term * powers[rest]
                    total = term if total is None else total + term
        result[alpha] = total
    return result


def remote_kernel(
    places,
    words,
    far,
    cells,
    bodies,
    moments,
    parents,
    in_0,
    in_1,
    in_2,
    in_3,
    field_in,
    field,
    leaf_terms,
    parent_terms,
    out_0,
    out_1,
    out_2,
    out_3,
    far_bodies,
    far_field,
    gather_a,
    gather_b,
    *scratch,
):
    place = placing(places)
    incoming = (in_0, in_1, in_2, in_3)
    outgoing = (out_0, out_1, out_2, out_3)
    for way in range(4):
        far_bodies[way * SLOTS : (way + 1) * SLOTS] = incoming[way][:BODY_ROWS, :].reshape(
            SLOTS, 8, HALF
        )
    far_bodies[4 * SLOTS] = bodies[LEAVES]
    far_field[...] = jnp.zeros_like(far_field)
    refs = paired(scratch)
    pair_loop(
        words, 1, GROUP // 2, SOME_SIZES, place, True, bodies, far_bodies, field, far_field, refs
    )
    for way in range(4):
        outgoing[way][:BODY_ROWS, :] = far_field[way * SLOTS : (way + 1) * SLOTS].reshape(
            BODY_ROWS, HALF
        )

    def moved(rows, way):
        lane = lane_ids(rows.shape)
        rows = jnp.where(lane == CENTRE, rows + place[2 + 2 * way].astype(f32), rows)
        return jnp.where(lane == CENTRE + 1, rows + place[3 + 2 * way].astype(f32), rows)

    table = [moments[...], parents[...]]
    for way in range(4):
        table.append(moved(incoming[way][BODY_ROWS : BODY_ROWS + SLOTS, :], way))
    for way in range(4):
        table.append(moved(incoming[way][BODY_ROWS + SLOTS :, :], way))
    table.append(jnp.zeros((ENTRIES - OWN - 4 * SLOTS - 4 * PSLOTS, 128), f32))
    columns = jnp.concatenate(table, 0).T[:FEATS]
    columns = jnp.concatenate(split3(columns), 0).astype(bf16)

    def one_hot(index, entries):
        return jnp.where(row_ids((entries, 128)) == index, 1.0, 0.0).astype(bf16)

    def joined(parts):
        return parts[:FEATS] + parts[FEATS : 2 * FEATS] + parts[2 * FEATS :]

    def far_block(block):
        if block < FAR_BLOCKS - 1:
            lanes = slice(128 * block, 128 * block + 128)
            a, b, z = far[0, :, lanes], far[1, :, lanes], far[2, :, lanes]
            used = b >= 0
            b = jnp.where(b >= LEAVES, b + PARENTS, b)
        else:
            blank = jnp.zeros((1, 128 - cells.shape[2]), i32)
            a = jnp.concatenate([cells[0] + LEAVES, blank], 1)
            b = jnp.concatenate([cells[1], blank - 1], 1)
            z = jnp.concatenate([cells[2], blank], 1)
            used = b >= 0
            b = jnp.where(b >= PARENTS, b + (OWN + 4 * SLOTS - PARENTS), b + LEAVES)
            b = jnp.where(used, b, -1)
        a = jnp.where(used, a, -1)
        return a, b, (z * CZ).astype(f32), jnp.where(used, 1.0, 0.0)

    gather_a[...] = jnp.zeros_like(gather_a)
    gather_b[...] = jnp.zeros_like(gather_b)
    place_of = row_ids((FEATS, 128))
    for block in range(FAR_BLOCKS):
        rows = slice(FEATS * block, FEATS * block + FEATS)
        a, b, lift, used = far_block(block)
        got_a = joined(
            jnp.dot(columns[:, :OWN], one_hot(a, OWN), preferred_element_type=f32)
        )
        got_b = joined(jnp.dot(columns, one_hot(b, ENTRIES), preferred_element_type=f32))
        gather_a[rows, :] = jnp.where(place_of == LIVE, used, got_a)
        gather_b[rows, :] = got_b + jnp.where(place_of == CENTRE + 2, lift, 0.0)
    for chunk in range(2):
        start = 8 * chunk * FEATS

        def feature(ref, at, start=start):
            return ref[pl.ds(start + at, 8, stride=FEATS), :]

        def gap(axis):
            return feature(gather_a, CENTRE + axis) - feature(gather_b, CENTRE + axis)

        live = feature(gather_a, LIVE) > 0.0
        x = jnp.where(live, gap(0), 3.0)
        y = jnp.where(live, gap(1), 3.0)
        z = jnp.where(live, gap(2), 3.0)
        tensors = derivatives(x, y, z)
        held_a = {}
        held_b = {}
        for alpha in MULTI:
            held_a[alpha] = feature(gather_a, PLACE[alpha]) * (-1.0 / fact(alpha))
            held_b[alpha] = feature(gather_b, PLACE[alpha]) * (
                -((-1.0) ** sum(alpha)) / fact(alpha)
            )
        for beta in MULTI:
            to_a = None
            to_b = None
            for alpha in MULTI:
                if sum(alpha) + sum(beta) > 4:
                    continue
                tensor = tensors[added(alpha, beta)]
                term_a = held_b[alpha] * tensor
                term_b = held_a[alpha] * tensor
                to_a = term_a if to_a is None else to_a + term_a
                to_b = term_b if to_b is None else to_b + term_b
            if sum(beta) % 2:
                to_b = -to_b
            gather_a[pl.ds(start + PLACE[beta], 8, stride=FEATS), :] = to_a
            gather_b[pl.ds(start + PLACE[beta], 8, stride=FEATS), :] = to_b
    sums_a = jnp.zeros((3 * FEATS, OWN), f32)
    sums_b = jnp.zeros((3 * FEATS, ENTRIES), f32)
    turned = (((1,), (1,)), ((), ()))
    for block in range(FAR_BLOCKS):
        rows = slice(FEATS * block, FEATS * block + FEATS)
        a, b, _, _ = far_block(block)
        parts_a = jnp.concatenate(split3(gather_a[rows, :]), 0).astype(bf16)
        parts_b = jnp.concatenate(split3(gather_b[rows, :]), 0).astype(bf16)
        hot_a = one_hot(a, OWN)
        hot_b = one_hot(b, ENTRIES)
        sums_a = sums_a + lax.dot_general(parts_a, hot_a, turned, preferred_element_type=f32)
        sums_b = sums_b + lax.dot_general(parts_b, hot_b, turned, preferred_element_type=f32)
    got_a = jnp.concatenate([joined(sums_a), jnp.zeros((128 - FEATS, OWN), f32)], 0)
    got_b = jnp.concatenate([joined(sums_b), jnp.zeros((128 - FEATS, ENTRIES), f32)], 0)
    keep = lane_ids((1, 128)) < TERMS
    terms_a = jnp.where(keep, got_a.T, 0.0)
    terms_b = jnp.where(keep, got_b.T, 0.0)
    leaf_terms[...] = terms_a[:LEAVES] + terms_b[:LEAVES]
    parent_terms[...] = terms_a[LEAVES:OWN] + terms_b[LEAVES:OWN]
    leaf_start = OWN
    parent_start = OWN + 4 * SLOTS
    for way in range(4):
        first = leaf_start + way * SLOTS
        outgoing[way][BODY_ROWS : BODY_ROWS + SLOTS, :] = terms_b[first : first + SLOTS]
        first = parent_start + way * PSLOTS
        outgoing[way][BODY_ROWS + SLOTS :, :] = terms_b[first : first + PSLOTS]


def back_kernel(
    places,
    counts,
    send,
    send_p,
    bodies,
    field_in,
    leaf_in,
    parent_in,
    down,
    in_0,
    in_1,
    in_2,
    in_3,
    out,
    field,
    leaf_terms,
    parent_terms,
    tiles,
):
    place = placing(places)
    incoming = (in_0, in_1, in_2, in_3)
    leaf_terms[...] = leaf_in[...]
    parent_terms[...] = parent_in[...]
    for way in range(4):

        def leaf_step(k, carry, way=way):
            leaf = send[0, way * SLOTS + k]
            field[leaf] = field[leaf] + incoming[way][pl.ds(pl.multiple_of(8 * k, 8), 8), :]
            leaf_terms[pl.ds(leaf, 1), :] = (
                leaf_terms[pl.ds(leaf, 1), :] + incoming[way][pl.ds(BODY_ROWS + k, 1), :]
            )
            return carry

        lax.fori_loop(0, SLOTS, leaf_step, 0, unroll=8)

        def parent_step(k, carry, way=way):
            cell = send_p[0, way * PSLOTS + k]
            parent_terms[pl.ds(cell, 1), :] = (
                parent_terms[pl.ds(cell, 1), :] + incoming[way][pl.ds(BODY_ROWS + SLOTS + k, 1), :]
            )
            return carry

        lax.fori_loop(0, PSLOTS, parent_step, 0, unroll=8)
    half_z = CZ // 2
    for at in range(8):
        moved = jnp.dot(
            parent_terms[...],
            down[:, 128 * at : 128 * at + 128],
            precision=lax.Precision.HIGHEST,
            preferred_element_type=f32,
        )
        first = (at >> 2 & 1) * CY * CZ + (at >> 1 & 1) * CZ + (at & 1)
        for py in range(CY // 2):
            rows = pl.ds(first + 2 * CZ * py, half_z, stride=2)
            leaf_terms[rows, :] = leaf_terms[rows, :] + moved[half_z * py : half_z * py + half_z]

    lane = lane_ids((8, 128))
    inverse_factorials = jnp.zeros((8, 128), f32)
    for alpha in MULTI:
        inverse_factorials = jnp.where(lane == PLACE[alpha], 1.0 / fact(alpha), inverse_factorials)

    def group_step(g, carry):
        rows = pl.ds(pl.multiple_of(8 * g, 8), 8)
        cx, cy, cz = group_centre(place, g)
        _, px, py, pz = wide_rows(bodies, g)
        x, y, z = px - cx, py - cy, pz - cz
        terms = leaf_terms[rows, :] * inverse_factorials

        def coefficient(*alpha):
            at = PLACE[alpha]
            return jnp.broadcast_to(terms[:, at : at + 1], (8, LEAF))

        def nested(values, t):
            total, slope = values[-1], None
            for value in values[-2::-1]:
                slope = total if slope is None else slope * t + total
                total = total * t + value
            return total, slope

        def plain(values, t):
            total = values[-1]
            for value in values[-2::-1]:
                total = total * t + value
            return total

        by_x = []
        by_x_y = []
        by_x_z = []
        for i in range(5):
            in_z = [
                nested([coefficient(i, j, k) for k in range(5 - i - j)], z) for j in range(5 - i)
            ]
            value, slope = nested([pair[0] for pair in in_z], y)
            by_x.append(value)
            if i < 4:
                by_x_y.append(slope)
                by_x_z.append(plain([pair[1] for pair in in_z[:-1]], y))
        value, slope = nested(by_x, x)
        values = [value, -slope, -plain(by_x_y, x), -plain(by_x_z, x)]
        for at, value in enumerate(values):
            tiles[pl.ds(64 * g + at, 8, stride=8), :] = value[:, :HALF]
            tiles[pl.ds(64 * g + 4 + at, 8, stride=8), :] = value[:, HALF:]
        row = row_ids((8, HALF))
        body = lane_ids((8, HALF)) + jnp.where(row < 4, 0, HALF)
        for u in range(8):
            leaf = 8 * g + u
            tile = tiles[pl.ds(pl.multiple_of(8 * leaf, 8), 8), :] + field[leaf]
            tile = jnp.where(body < counts[leaf], tile, 0.0)
            start = pl.multiple_of(leaf * LEAF, LEAF)
            out[:, pl.ds(start, HALF)] = tile[:4]
            out[:, pl.ds(start + HALF, HALF)] = tile[4:]
        return carry

    lax.fori_loop(0, LEAVES // 8, group_step, 0, unroll=4)


VMEM = pl.BlockSpec(memory_space=pltpu.VMEM)
SMEM = pl.BlockSpec(memory_space=pltpu.SMEM)
HBM = pl.BlockSpec(memory_space=pltpu.HBM)
params = pltpu.CompilerParams(vmem_limit_bytes=20 * 1024 * 1024)
packed = jax.ShapeDtypeStruct((PACK_ROWS, 128), f32)
tiled = jax.ShapeDtypeStruct((LEAVES + 1, 8, HALF), f32)
heavy = pl.CostEstimate(flops=20_000_000_000, bytes_accessed=2_000_000, transcendentals=0)


def shaped(*dims):
    return jax.ShapeDtypeStruct(dims, f32)


def on_device(
    positions, masses, leaf_counts, send_leaves, send_parents, near_pairs, far_pairs, parent_pairs
):
    slab_count = lax.axis_size("slab")
    sub_count = lax.axis_size("sub")
    places = (slab_count, sub_count)

    def rows_first(lists):
        return jnp.transpose(lists, (1, 0, 2))

    sent = pl.pallas_call(
        functools.partial(front_kernel, places),
        out_shape=[shaped(8 * LEAVES + 8, HALF), shaped(LEAVES, 128), shaped(PARENTS, 128)]
        + [jax.ShapeDtypeStruct((8, LIST), i32)]
        + [packed] * 4,
        in_specs=[HBM] * 7,
        out_specs=[VMEM] * 8,
        scratch_shapes=[
            pltpu.SMEM(send_leaves.shape, i32),
            pltpu.SMEM(send_parents.shape, i32),
            pltpu.SMEM((1, LEAVES), i32),
            pltpu.VMEM((1, LEAVES), i32),
            pltpu.VMEM((3, 1, near_pairs.shape[2]), i32),
            pltpu.VMEM(positions.shape, f32),
            pltpu.VMEM((2 * LEAVES, HALF), f32),
            pltpu.VMEM(UP.shape, f32),
            pltpu.SemaphoreType.DMA((8,)),
        ],
        compiler_params=params,
        name="moments_and_packing",
    )(
        *(
            pltpu.with_memory_space_constraint(value, pltpu.HBM)
            for value in (
                send_leaves,
                send_parents,
                leaf_counts.reshape(1, LEAVES),
                rows_first(near_pairs),
                positions,
                masses.reshape(2 * LEAVES, HALF),
                jnp.asarray(UP),
            )
        )
    )
    bodies = sent[0].reshape(LEAVES + 1, 8, HALF)
    moments, parents, words = sent[1:4]

    def exchange(value, way, back):
        pairs = []
        for s in range(slab_count):
            for u in range(sub_count):
                here = s * sub_count + u
                there = (s + slab_steps[way]) % slab_count * sub_count + (
                    u + sub_steps[way]
                ) % sub_count
                pairs.append((here, there) if back else (there, here))
        return lax.ppermute(value, ("slab", "sub"), pairs)

    incoming = [exchange(sent[4 + way], way, False) for way in range(4)]

    field = pl.pallas_call(
        functools.partial(self_kernel, places),
        out_shape=tiled,
        in_specs=[SMEM, VMEM],
        out_specs=VMEM,
        scratch_shapes=[pltpu.VMEM((GROUP, LEAF, LEAF), bf16)] * 4
        + [pltpu.VMEM((GROUP, 32, LEAF), bf16)] * 2
        + [pltpu.VMEM((GROUP, 2, 8, LEAF), f32)] * 2,
        compiler_params=params,
        cost_estimate=heavy,
        name="self_pairs",
    )(words, bodies)

    middle = pl.pallas_call(
        functools.partial(remote_kernel, places),
        out_shape=[tiled, shaped(LEAVES, 128), shaped(PARENTS, 128)] + [packed] * 4,
        in_specs=[SMEM] + [VMEM] * 10,
        out_specs=[VMEM] * 7,
        scratch_shapes=[
            pltpu.VMEM((4 * SLOTS + 1, 8, HALF), f32),
            pltpu.VMEM((4 * SLOTS + 1, 8, HALF), f32),
            pltpu.VMEM((16 * FEATS, 128), f32),
            pltpu.VMEM((16 * FEATS, 128), f32),
        ]
        + pair_scratch(GROUP // 2),
        compiler_params=params,
        input_output_aliases={10: 0},
        name="pairs_with_others",
    )(
        words,
        rows_first(far_pairs),
        rows_first(parent_pairs),
        bodies,
        moments,
        parents,
        *incoming,
        field,
    )
    field, leaf_terms, parent_terms = middle[:3]
    arrived = [exchange(middle[3 + way], way, True) for way in range(4)]

    field = pl.pallas_call(
        functools.partial(near_kernel, places),
        out_shape=tiled,
        in_specs=[SMEM] + [VMEM] * 2,
        out_specs=VMEM,
        scratch_shapes=pair_scratch(GROUP),
        compiler_params=params,
        cost_estimate=heavy,
        input_output_aliases={2: 0},
        name="own_pairs",
    )(words, bodies, field)

    return pl.pallas_call(
        functools.partial(back_kernel, places),
        out_shape=[shaped(4, LEAVES * LEAF), tiled],
        in_specs=[SMEM] * 3 + [VMEM] * 9,
        out_specs=[VMEM] * 2,
        input_output_aliases={4: 1},
        scratch_shapes=[
            pltpu.VMEM((LEAVES, 128), f32),
            pltpu.VMEM((PARENTS, 128), f32),
            pltpu.VMEM((8 * LEAVES, HALF), f32),
        ],
        compiler_params=params,
        name="shift_and_evaluate",
    )(
        leaf_counts,
        send_leaves,
        send_parents,
        sent[0],
        field,
        leaf_terms,
        parent_terms,
        jnp.asarray(DOWN),
        *arrived,
    )[0]


def solution(mesh):
    return jax.shard_map(
        on_device,
        mesh=mesh,
        in_specs=(
            P(None, ("slab", "sub")),
            P(("slab", "sub")),
            P(("slab", "sub")),
            P(("slab", "sub"), None),
            P(("slab", "sub"), None),
            P(("slab", "sub"), None, None),
            P(("slab", "sub"), None, None),
            P(("slab", "sub"), None, None),
        ),
        out_specs=P(None, ("slab", "sub")),
        check_vma=False,
    )
```

```python
import functools
import math

import jax
import jax.numpy as jnp
import ml_dtypes
import numpy as np
from jax import lax
from jax.experimental import pallas as pl
from jax.experimental.pallas import tpu as pltpu
from jax.sharding import PartitionSpec as P

CX = 2
CY = 4
CZ = 32

soft_square = 0.0025
slab_steps = (1, 0, 1, 1)
sub_steps = (0, 1, 1, -1)

LEAVES = CX * CY * CZ
PARENTS = LEAVES // 8
SLOTS = LEAVES // 4
PSLOTS = PARENTS // 2
HALF = 128
LEAF = 2 * HALF
BODY_ROWS = 8 * SLOTS
CELL_ROWS = SLOTS // 2
PACK_ROWS = BODY_ROWS + CELL_ROWS
GROUP = 8
bf16 = jnp.bfloat16
f32 = jnp.float32
i32 = jnp.int32

MULTI = [
    (i, j, n - i - j) for n in range(5) for i in range(n, -1, -1) for j in range(n - i, -1, -1)
]
PLACE = {alpha: at for at, alpha in enumerate(MULTI)}
TERMS = len(MULTI)
CENTRE = TERMS
LIVE = TERMS + 3
SIZES = (256, 192, 160, 128, 96)
EVERY_SIZE = tuple((size, at) for at, size in enumerate(SIZES))
SOME_SIZES = ((256, 0), (192, 2), (128, 4))
LIST = 384
STEPS_AT = LIST - 8
FEATS = 40
OWN = LEAVES + PARENTS
ENTRIES = 640
FAR_BLOCKS = 5


def fact(alpha):
    return math.prod(math.factorial(a) for a in alpha)


def added(alpha, beta):
    return tuple(a + b for a, b in zip(alpha, beta))


def taken(alpha, beta):
    return tuple(a - b for a, b in zip(alpha, beta))


def octant(at):
    return tuple(0.5 if bit else -0.5 for bit in (at >> 2 & 1, at >> 1 & 1, at & 1))


def power(delta, alpha):
    return math.prod(d**a for d, a in zip(delta, alpha))


def shift_matrices():
    up = np.zeros((8, 128, 128), np.float32)
    down = np.zeros((8, 128, 128), np.float32)
    for at in range(8):
        delta = octant(at)
        for alpha in MULTI:
            for beta in MULTI:
                rest = taken(alpha, beta)
                if min(rest) < 0:
                    continue
                choose = math.prod(math.comb(a, b) for a, b in zip(alpha, beta))
                up[at, PLACE[beta], PLACE[alpha]] = choose * power(delta, rest)
                down[at, PLACE[alpha], PLACE[beta]] = power(delta, rest) / fact(rest)
    return up.reshape(8 * 128, 128), down.transpose(1, 0, 2).reshape(128, 8 * 128)


UP, DOWN = shift_matrices()


def row_ids(shape):
    return lax.broadcasted_iota(i32, shape, 0)


def lane_ids(shape):
    return lax.broadcasted_iota(i32, shape, 1)


def monomials(x, y, z):
    table = {(0, 0, 0): None}
    axes = (x, y, z)
    for alpha in MULTI[1:]:
        lead = max(axis for axis in range(3) if alpha[axis])
        less = tuple(a - (axis == lead) for axis, a in enumerate(alpha))
        table[alpha] = axes[lead] if table[less] is None else table[less] * axes[lead]
    return table


def split3(value):
    high = value.astype(bf16).astype(f32)
    rest = value - high
    middle = rest.astype(bf16).astype(f32)
    return high, middle, rest - middle


def soft_parts():
    rest = np.float32(soft_square)
    parts = []
    for _ in range(3):
        part = np.float32(rest.astype(ml_dtypes.bfloat16))
        parts.append(float(part))
        rest = np.float32(rest - part)
    return parts


SOFT = soft_parts()


def spread(tile):
    row = row_ids((8, HALF))
    turned = pltpu.roll(tile, 4, 0)
    low = row < 4
    return jnp.concatenate([jnp.where(low, tile, turned), jnp.where(low, turned, tile)], 1)


def fold(field):
    row = row_ids((8, HALF))
    return jnp.where(row < 4, field[:, :HALF], pltpu.roll(field[:, HALF:], 4, 0))


def offset_rows(ox, oy, oz):
    row = row_ids((8, LEAF)) & 3
    return jnp.where(row == 1, ox, jnp.where(row == 2, oy, jnp.where(row == 3, oz, 0.0)))


def features(tile, offset, as_row, as_column, as_weight):
    wide = spread(tile)
    row = row_ids((8, LEAF))
    first = (row & 3) == 0
    low = row < 4
    weight = jnp.broadcast_to(wide[0:1], (8, LEAF))
    x = jnp.where(first, 0.0, wide + offset)
    square = x * x
    pairwise = square + pltpu.roll(square, 1, 0)
    q = pairwise + pltpu.roll(pairwise, 2, 0)
    y = jnp.where(first, q, x)
    zero = jnp.zeros((8, LEAF), f32)
    out = [x, q]
    if as_row or as_column or as_weight:
        h, m, l = split3(y)
    if as_row:
        part_a = jnp.where(row == 4, m, h)
        part_b = jnp.where(row == 0, l, jnp.where(row == 4, 1.0, m))
        part_c = jnp.where(first, 1.0, jnp.where(low, h, l))
        part_d = jnp.where(row < 3, 1.0, 0.0)
        out.append(jnp.concatenate([part_a, part_b, part_c, part_d], 0).astype(bf16))
    if as_column:
        scale = jnp.where(first, 1.0, -2.0)
        h2, m2, l2 = h * scale, m * scale, l * scale
        mixed = jnp.where(low, h2, m2)
        part_a = jnp.where(first, 1.0, mixed)
        part_b = jnp.where(row == 0, 1.0, jnp.where(row == 4, h, mixed))
        part_c = jnp.where(row == 0, m, jnp.where(row == 4, l, jnp.where(low, l2, h2)))
        part_d = jnp.where(
            row == 0, SOFT[0], jnp.where(row == 1, SOFT[1], jnp.where(row == 2, SOFT[2], 0.0))
        )
        out.append(jnp.concatenate([part_a, part_b, part_c, part_d], 0).astype(bf16))
    if as_weight:
        heavy = jnp.where(low, y, 1.0) * weight
        out.append(jnp.concatenate(list(split3(heavy)) + [zero], 0).astype(bf16))
    return out


def field_of(sums, x, q):
    total = sums[0:8] + sums[8:16] + sums[16:24]
    row = row_ids((8, LEAF))
    first = (row & 3) == 0
    plain = pltpu.roll(total, 4, 0)
    inner = total - jnp.where(first, q - soft_square, x) * plain
    along = x * inner
    dots = along[1:2] + along[2:3] + along[3:4]
    return fold(jnp.where(row == 0, 2.0 * dots - inner, inner))


def cubes(row_part, column_part):
    square = lax.dot_general(
        row_part, column_part, (((0,), (0,)), ((), ())), preferred_element_type=f32
    )
    inverse = lax.rsqrt(square)
    return inverse * inverse * inverse


def padded(sums):
    lanes = sums.shape[1]
    if lanes == LEAF:
        return sums
    return jnp.concatenate([sums, jnp.zeros((sums.shape[0], LEAF - lanes), f32)], 1)


def pipeline(words, at, group, plan, early, late):
    @pl.when(words[at, STEPS_AT + len(SIZES) - 1] > 0)
    def _():
        for u in range(group):
            early(SIZES[0], 0, 0, u)

    begin = jnp.int32(0)
    for size, last in plan:

        def step(k, carry, size=size):
            for slot in range(2):
                done = []
                for u in range(group):
                    done.append(late(size, 2 * k + slot, slot, u))
                    early(size, 2 * k + slot + 1, 1 - slot, u)
                for store in done:
                    store()
            return carry

        end = words[at, STEPS_AT + last]
        lax.fori_loop(begin, end, step, 0)
        begin = end


def placing(places):
    slab_count, sub_count = places
    slab_at = lax.axis_index("slab")
    sub_at = lax.axis_index("sub")
    numbers = [slab_at * CX, sub_at * CY]
    for way in range(4):
        reach_x = slab_at + slab_steps[way]
        reach_y = sub_at + sub_steps[way]
        numbers.append(jnp.where(reach_x >= slab_count, slab_count * CX, 0))
        high = jnp.where(reach_y >= sub_count, sub_count * CY, 0)
        numbers.append(jnp.where(reach_y < 0, -sub_count * CY, high))
    return numbers


def jump_of(place, way):
    jump_x = jnp.int32(0)
    jump_y = jnp.int32(0)
    for at in range(4):
        jump_x = jnp.where(way == at, place[2 + 2 * at], jump_x)
        jump_y = jnp.where(way == at, place[3 + 2 * at], jump_y)
    return jump_x.astype(f32), jump_y.astype(f32)


def leaf_centre(place, leaf):
    return (
        -(place[0] + leaf // (CY * CZ)).astype(f32) - 0.5,
        -(place[1] + leaf // CZ % CY).astype(f32) - 0.5,
        -(leaf % CZ).astype(f32) - 0.5,
    )


def tall(part):
    rows = part.shape[0]
    if rows == LEAF:
        return part
    return jnp.concatenate([part, jnp.zeros((LEAF - rows, LEAF), bf16)], 0)


def halves(c):
    high = c.astype(bf16)
    return high, (c - high.astype(f32)).astype(bf16)


def self_loop(words, at, group, plan, place, bodies, field, scratch):
    high_refs, low_refs, weight_refs, spot_refs = scratch

    def early(size, k, slot, u):
        leaf = words[at, k * group + u]
        x, q, rows, columns, weights = features(
            bodies[leaf], offset_rows(*leaf_centre(place, leaf & (LEAVES - 1))), True, True, True
        )
        wide = LEAF if size > HALF else HALF
        high, low = halves(cubes(rows[:, :size], columns[:, :wide]))
        high_refs[slot][u, :size, :wide] = high
        low_refs[slot][u, :size, :wide] = low
        weight_refs[slot][u] = weights
        spot_refs[slot][u, 0] = x
        spot_refs[slot][u, 1] = q

    def late(size, k, slot, u):
        leaf = words[at, k * group + u]
        wide = LEAF if size > HALF else HALF
        w = weight_refs[slot][u, :, :size]
        sums = jnp.dot(
            w, high_refs[slot][u, :size, :wide], preferred_element_type=f32
        ) + jnp.dot(w, low_refs[slot][u, :size, :wide], preferred_element_type=f32)
        result = field_of(padded(sums), spot_refs[slot][u, 0], spot_refs[slot][u, 1])
        itself = jnp.where((row_ids((8, HALF)) & 3) == 0, bodies[leaf], 0.0)
        result = result + itself * soft_square**-0.5

        def store():
            field[leaf] = result

        return store

    pipeline(words, at, group, plan, early, late)


def pair_loop(
    words, at, group, plan, place, jumping, bodies, others, field, other_field, scratch
):
    high_refs, low_refs, across_refs, row_refs, column_refs, spot_refs = scratch
    turned = (((1,), (1,)), ((), ()))

    def unpack(k, u):
        word = words[at, k * group + u]
        return word & 511, word >> 9 & 511, word >> 18 & 1, (word >> 19 & 3) - 1, word >> 21 & 7

    def early(size, k, slot, u):
        row_leaf, column_leaf, swapped, lift, way = unpack(k, u)
        frame = jnp.where(swapped == 1, column_leaf, row_leaf) & (LEAVES - 1)
        cx, cy, cz = leaf_centre(place, frame)
        raised = (lift * CZ).astype(f32)
        swap = (swapped == 1).astype(f32)
        jump_x, jump_y = jump_of(place, way) if jumping else (0.0, 0.0)
        row_offset = offset_rows(cx, cy, cz + swap * raised)
        column_offset = offset_rows(cx + jump_x, cy + jump_y, cz + (1.0 - swap) * raised)
        xr, qr, rows, row_weights = features(bodies[row_leaf], row_offset, True, False, True)
        xc, qc, columns, column_weights = features(
            others[column_leaf], column_offset, False, True, True
        )
        high, low = halves(cubes(rows[:, :size], columns))
        high_refs[slot][u, :size] = high
        low_refs[slot][u, :size] = low
        if size > HALF:
            across_refs[slot][u] = tall(high).T
        row_refs[slot][u] = row_weights
        column_refs[slot][u] = column_weights
        spot_refs[slot][u, 0] = xr
        spot_refs[slot][u, 1] = qr
        spot_refs[slot][u, 2] = xc
        spot_refs[slot][u, 3] = qc

    def late(size, k, slot, u):
        row_leaf, column_leaf, _, _, _ = unpack(k, u)
        wr = row_refs[slot][u, :, :size]
        wc = column_refs[slot][u]
        high = high_refs[slot][u, :size]
        low = low_refs[slot][u, :size]
        column_sums = jnp.dot(wr, high, preferred_element_type=f32) + jnp.dot(
            wr, low, preferred_element_type=f32
        )
        row_sums = lax.dot_general(wc, low, turned, preferred_element_type=f32)
        if size > HALF:
            row_sums = padded(row_sums) + jnp.dot(
                wc, across_refs[slot][u], preferred_element_type=f32
            )
        else:
            row_sums += lax.dot_general(wc, high, turned, preferred_element_type=f32)
        row_field = field_of(padded(row_sums), spot_refs[slot][u, 0], spot_refs[slot][u, 1])
        column_field = field_of(column_sums, spot_refs[slot][u, 2], spot_refs[slot][u, 3])

        def store():
            field[row_leaf] = field[row_leaf] + row_field
            other_field[column_leaf] = other_field[column_leaf] + column_field

        return store

    pipeline(words, at, group, plan, early, late)


def pair_scratch(group):
    return (
        [pltpu.VMEM((group, LEAF, LEAF), bf16)] * 6
        + [pltpu.VMEM((group, 32, LEAF), bf16)] * 4
        + [pltpu.VMEM((group, 4, 8, LEAF), f32)] * 2
    )


def paired(scratch):
    return [scratch[at : at + 2] for at in range(0, len(scratch), 2)]


def front_kernel(places, *refs):
    stored, made, held, sems, chosen = refs[:7], refs[7:15], refs[15:23], refs[23], refs[24]
    bodies, moments, parents, words = made[:4]
    outs = made[4:]
    sources = (stored[0], stored[1], stored[2], *stored[2:])
    copies = [
        pltpu.make_async_copy(source, target, sems.at[at])
        for at, (source, target) in enumerate(zip(sources, held))
    ]
    for copy in copies:
        copy.start()
    send, send_p, counts, count_row, pairs, spots, masses, up = held
    place = placing(places)
    copies[3].wait()
    copies[4].wait()
    words[...] = work_lists(count_row[...], pairs[0], pairs[1], pairs[2])
    copies[2].wait()
    copies[5].wait()
    copies[6].wait()
    row = row_ids((8, HALF))

    def tile(g):
        count = jnp.zeros((8, HALF), i32)
        for u in range(8):
            leaf = 8 * g + u
            start = pl.multiple_of(leaf * LEAF, LEAF)
            low = spots[:, pl.ds(start, HALF)]
            high = spots[:, pl.ds(start + HALF, HALF)]
            blank = jnp.zeros((1, HALF), f32)
            bodies[pl.ds(pl.multiple_of(8 * leaf, 8), 8), :] = jnp.concatenate(
                [blank, low, blank, high], 0
            )
            count = jnp.where(row == u, counts[0, leaf], count)
        lane = lane_ids((8, HALF))
        for half in range(2):
            mass = masses[pl.ds(16 * g + half, 8, stride=2), :]
            bodies[pl.ds(64 * g + 4 * half, 8, stride=8), :] = jnp.where(
                lane + half * HALF < count, mass, 0.0
            )

    def cell_moments(g, parts):
        w, px, py, pz = parts
        cx, cy, cz = group_centre(place, g)
        axes = (px - cx, py - cy, pz - cz)
        table = {(0, 0, 0): w}
        lane = lane_ids((8, 128))
        built = jnp.zeros((8, 128), f32)
        for alpha in MULTI:
            if alpha not in table:
                lead = max(axis for axis in range(3) if alpha[axis])
                less = tuple(a - (axis == lead) for axis, a in enumerate(alpha))
                table[alpha] = table[less] * axes[lead]
            value = table[alpha]
            total = jnp.sum(value[:, :HALF] + value[:, HALF:], axis=1, keepdims=True)
            built = jnp.where(lane == PLACE[alpha], total, built)
        built = jnp.where(lane == CENTRE, cx, built)
        built = jnp.where(lane == CENTRE + 1, cy, built)
        built = jnp.where(lane == CENTRE + 2, cz, built)
        moments[pl.ds(pl.multiple_of(8 * g, 8), 8), :] = built

    batch = 4
    for u in range(batch):
        tile(u)

    def group_step(k, carry):
        groups = [batch * k + u for u in range(batch)]
        parts = [wide_rows(bodies, g) for g in groups]
        following = jnp.minimum(batch * (k + 1), LEAVES // 8 - batch)
        for u in range(batch):
            tile(following + u)
        for g, part in zip(groups, parts):
            cell_moments(g, part)
        return carry

    lax.fori_loop(0, LEAVES // 8 // batch, group_step, 0)
    kind = row & 3
    bx = place[0].astype(f32) + 0.5
    by = place[1].astype(f32) + 0.5
    bodies[8 * LEAVES : 8 * LEAVES + 8, :] = jnp.where(
        kind == 1, bx, jnp.where(kind == 2, by, jnp.where(kind == 3, 0.5, 0.0))
    )
    copies[7].wait()
    half_z = CZ // 2
    summed = jnp.zeros((PARENTS, 128), f32)
    for at in range(8):
        first = (at >> 2 & 1) * CY * CZ + (at >> 1 & 1) * CZ + (at & 1)
        piece = jnp.concatenate(
            [moments[pl.ds(first + 2 * CZ * py, half_z, stride=2), :] for py in range(CY // 2)], 0
        )
        summed = summed + jnp.dot(
            piece,
            up[128 * at : 128 * at + 128, :],
            precision=lax.Precision.HIGHEST,
            preferred_element_type=f32,
        )
    lane = lane_ids((PARENTS, 128))
    cell = row_ids((PARENTS, 128))
    summed = jnp.where(lane == CENTRE, place[0].astype(f32) + 1.0, summed)
    summed = jnp.where(
        lane == CENTRE + 1,
        place[1].astype(f32) + 1.0 + 2.0 * (cell // half_z).astype(f32),
        summed,
    )
    summed = jnp.where(lane == CENTRE + 2, 1.0 + 2.0 * (cell % half_z).astype(f32), summed)
    parents[...] = summed
    copies[0].wait()
    copies[1].wait()
    for way in range(4):

        def leaf_step(k, carry, way=way):
            leaf = send[0, way * SLOTS + k]
            outs[way][pl.ds(pl.multiple_of(8 * k, 8), 8), :] = bodies[
                pl.ds(pl.multiple_of(8 * leaf, 8), 8), :
            ]
            chosen[pl.ds(way * (SLOTS + PSLOTS) + k, 1), :] = moments[pl.ds(leaf, 1), :]
            return carry

        lax.fori_loop(0, SLOTS, leaf_step, 0, unroll=8)
        for k in range(PSLOTS):
            cell = send_p[0, way * PSLOTS + k]
            chosen[pl.ds(way * (SLOTS + PSLOTS) + SLOTS + k, 1), :] = parents[pl.ds(cell, 1), :]
        first = way * (SLOTS + PSLOTS)
        outs[way][BODY_ROWS:, :] = three_to_a_row(
            chosen[first : first + SLOTS, :], chosen[first + SLOTS : first + SLOTS + PSLOTS, :]
        )


def three_to_a_row(leaves, parents):
    rest = jnp.zeros((CELL_ROWS - parents.shape[0], 128), f32)
    return (
        leaves[:CELL_ROWS]
        + pltpu.roll(leaves[CELL_ROWS:], FEATS, 1)
        + pltpu.roll(jnp.concatenate([parents, rest], 0), 2 * FEATS, 1)
    )


def one_to_a_row(rows):
    keep = lane_ids(rows.shape) < FEATS
    parts = [rows, pltpu.roll(rows, 128 - FEATS, 1), pltpu.roll(rows, 128 - 2 * FEATS, 1)]
    parts = [jnp.where(keep, part, 0.0) for part in parts]
    return jnp.concatenate(parts[:2], 0), parts[2][:PSLOTS]


def wide_rows(bodies, g):
    return [
        jnp.concatenate(
            [bodies[pl.ds(64 * g + 4 * half + at, 8, stride=8), :] for half in range(2)], 1
        )
        for at in range(4)
    ]


def group_centre(place, g):
    cx = (place[0] + g // (CY * CZ // 8)).astype(f32) + 0.5
    cy = (place[1] + g // (CZ // 8) % CY).astype(f32) + 0.5
    base_z = (8 * (g % (CZ // 8))).astype(f32) + 0.5
    return cx, cy, row_ids((8, 1)).astype(f32) + base_z


def work_lists(counts, owned, partner, image):
    wide = (LEAVES, LEAVES)
    every = jnp.broadcast_to(counts.astype(f32), (8, LEAVES)).astype(bf16)

    def count_of(index):
        hot = jnp.where(row_ids(wide) == index, 1.0, 0.0).astype(bf16)
        return jnp.dot(every, hot, preferred_element_type=f32)[:1].astype(i32)

    mine = jnp.logical_and(partner >= 0, partner < LEAVES)
    other = partner >= LEAVES
    count_a = count_of(owned)
    count_b = count_of(partner)
    swapped = count_b < count_a
    lift = (image + 1) << 19
    own_word = (
        jnp.where(swapped, partner, owned)
        | jnp.where(swapped, owned, partner) << 9
        | jnp.where(swapped, 1, 0) << 18
        | lift
        | 4 << 21
    )
    spot = jnp.maximum(partner - LEAVES, 0)
    other_word = owned | spot << 9 | lift | (spot // SLOTS) << 21
    own_empty = LEAVES << 9 | 1 << 19 | 4 << 21
    other_empty = (4 * SLOTS) << 9 | 1 << 19 | 4 << 21
    yes = jnp.ones((1, LEAVES), jnp.bool_)
    lists = [
        (own_word, mine, jnp.minimum(count_a, count_b), own_empty, 2 * GROUP),
        (other_word, other, count_a, other_empty, GROUP),
        (lane_ids((1, LEAVES)), yes, counts, LEAVES, 2 * GROUP),
    ]
    flags = []
    for _, member, need, _, _ in lists:
        for at, size in enumerate(SIZES):
            fits = need <= size
            if at + 1 < len(SIZES):
                fits = jnp.logical_and(fits, need > SIZES[at + 1])
            flags.append(jnp.where(jnp.logical_and(member, fits), 1.0, 0.0))
    flags = jnp.concatenate(flags + [jnp.zeros((16 - len(flags), LEAVES), f32)], 0)
    before = jnp.where(row_ids(wide) < lane_ids(wide), 1.0, 0.0).astype(bf16)
    order = jnp.dot(flags.astype(bf16), before, preferred_element_type=f32)
    number = jnp.sum(flags, axis=1, keepdims=True)
    lane = lane_ids((1, LIST))
    rows = []
    for at, (word, member, _, empty, unit) in enumerate(lists):
        spot = jnp.zeros((1, LEAVES), f32)
        total = jnp.zeros((1, 1), f32)
        ends = []
        for row in range(len(SIZES) * at, len(SIZES) * (at + 1)):
            spot = spot + flags[row : row + 1] * (order[row : row + 1] + total)
            total = total + number[row : row + 1]
            ends.append((total.astype(i32) + (unit - 1)) // unit)
        spot = jnp.where(member, spot, -1.0).astype(i32)
        pieces = jnp.concatenate(
            [word & 255, word >> 8 & 255, word >> 16, jnp.zeros((5, LEAVES), i32)], 0
        )
        hot = jnp.where(row_ids(wide) == spot, 1.0, 0.0).astype(bf16)
        found = lax.dot_general(
            pieces.astype(f32).astype(bf16),
            hot,
            (((1,), (1,)), ((), ())),
            preferred_element_type=f32,
        ).astype(i32)
        joined = found[0:1] | found[1:2] << 8 | found[2:3] << 16
        joined = jnp.concatenate([joined, jnp.zeros((1, LIST - LEAVES), i32)], 1)
        joined = jnp.where(lane < total.astype(i32), joined, empty)
        for size_at, end in enumerate(ends):
            joined = jnp.where(lane == STEPS_AT + size_at, end, joined)
        rows.append(joined)
    return jnp.concatenate(rows + [jnp.zeros((5, LIST), i32)], 0)


def self_kernel(places, words, bodies, field, *scratch):
    place = placing(places)
    field[LEAVES] = jnp.zeros((8, HALF), f32)
    self_loop(words, 2, GROUP, EVERY_SIZE, place, bodies, field, paired(scratch))


def near_kernel(places, words, bodies, field_in, field, *scratch):
    place = placing(places)
    refs = paired(scratch)
    pair_loop(words, 0, GROUP, EVERY_SIZE, place, False, bodies, bodies, field, field, refs)


def derivatives(x, y, z):
    inverse = lax.rsqrt(x * x + y * y + z * z)
    square = inverse * inverse
    odd = [inverse]
    for _ in range(4):
        odd.append(odd[-1] * square)
    powers = monomials(x, y, z)
    result = {}
    for alpha in MULTI:
        degree = sum(alpha)
        total = None
        for p in range(alpha[0] // 2 + 1):
            for q in range(alpha[1] // 2 + 1):
                for s in range(alpha[2] // 2 + 1):
                    m = p + q + s
                    ways = math.prod(
                        math.factorial(a) // (2**c * math.factorial(c) * math.factorial(a - 2 * c))
                        for a, c in zip(alpha, (p, q, s))
                    )
                    sign = (-1.0) ** (degree - m)
                    double = math.prod(range(1, 2 * (degree - m), 2))
                    term = odd[degree - m] * (sign * double * ways)
                    rest = (alpha[0] - 2 * p, alpha[1] - 2 * q, alpha[2] - 2 * s)
                    if powers[rest] is not None:
                        term = term * powers[rest]
                    total = term if total is None else total + term
        result[alpha] = total
    return result


def remote_kernel(
    places,
    words,
    far,
    cells,
    bodies,
    moments,
    parents,
    in_0,
    in_1,
    in_2,
    in_3,
    field_in,
    field,
    leaf_terms,
    parent_terms,
    out_0,
    out_1,
    out_2,
    out_3,
    far_bodies,
    far_field,
    gather_a,
    gather_b,
    *scratch,
):
    place = placing(places)
    incoming = (in_0, in_1, in_2, in_3)
    outgoing = (out_0, out_1, out_2, out_3)
    for way in range(4):
        far_bodies[way * SLOTS : (way + 1) * SLOTS] = incoming[way][:BODY_ROWS, :].reshape(
            SLOTS, 8, HALF
        )
    far_bodies[4 * SLOTS] = bodies[LEAVES]
    far_field[...] = jnp.zeros_like(far_field)
    refs = paired(scratch)
    pair_loop(
        words, 1, GROUP // 2, SOME_SIZES, place, True, bodies, far_bodies, field, far_field, refs
    )
    for way in range(4):
        outgoing[way][:BODY_ROWS, :] = far_field[way * SLOTS : (way + 1) * SLOTS].reshape(
            BODY_ROWS, HALF
        )

    def moved(rows, way):
        lane = lane_ids(rows.shape)
        rows = jnp.where(lane == CENTRE, rows + place[2 + 2 * way].astype(f32), rows)
        return jnp.where(lane == CENTRE + 1, rows + place[3 + 2 * way].astype(f32), rows)

    arrived = [one_to_a_row(incoming[way][BODY_ROWS:, :]) for way in range(4)]
    table = [moments[...], parents[...]]
    for way in range(4):
        table.append(moved(arrived[way][0], way))
    for way in range(4):
        table.append(moved(arrived[way][1], way))
    table.append(jnp.zeros((ENTRIES - OWN - 4 * SLOTS - 4 * PSLOTS, 128), f32))
    columns = jnp.concatenate(table, 0).T[:FEATS]
    columns = jnp.concatenate(split3(columns), 0).astype(bf16)

    def one_hot(index, entries):
        return jnp.where(row_ids((entries, index.shape[1])) == index, 1.0, 0.0).astype(bf16)

    def joined(parts):
        return parts[:FEATS] + parts[FEATS : 2 * FEATS] + parts[2 * FEATS :]

    def far_block(block):
        if block < FAR_BLOCKS - 1:
            lanes = slice(LEAF * block, LEAF * block + LEAF)
            a, b, z = far[0, :, lanes], far[1, :, lanes], far[2, :, lanes]
            used = b >= 0
            b = jnp.where(b >= LEAVES, b + PARENTS, b)
        else:
            blank = jnp.zeros((1, 128 - cells.shape[2]), i32)
            a = jnp.concatenate([cells[0] + LEAVES, blank], 1)
            b = jnp.concatenate([cells[1], blank - 1], 1)
            z = jnp.concatenate([cells[2], blank], 1)
            used = b >= 0
            b = jnp.where(b >= PARENTS, b + (OWN + 4 * SLOTS - PARENTS), b + LEAVES)
            b = jnp.where(used, b, -1)
        a = jnp.where(used, a, -1)
        return a, b, (z * CZ).astype(f32), jnp.where(used, 1.0, 0.0)

    def far_rows(block):
        parts = range(2 * block, 2 * block + (2 if block < FAR_BLOCKS - 1 else 1))
        return [slice(FEATS * part, FEATS * part + FEATS) for part in parts]

    gather_a[...] = jnp.zeros_like(gather_a)
    gather_b[...] = jnp.zeros_like(gather_b)
    for block in range(FAR_BLOCKS):
        a, b, lift, used = far_block(block)
        place_of = row_ids((FEATS, a.shape[1]))
        got_a = joined(jnp.dot(columns[:, :OWN], one_hot(a, OWN), preferred_element_type=f32))
        got_b = joined(jnp.dot(columns, one_hot(b, ENTRIES), preferred_element_type=f32))
        got_a = jnp.where(place_of == LIVE, used, got_a)
        got_b = got_b + jnp.where(place_of == CENTRE + 2, lift, 0.0)
        for part, rows in enumerate(far_rows(block)):
            gather_a[rows, :] = got_a[:, 128 * part : 128 * part + 128]
            gather_b[rows, :] = got_b[:, 128 * part : 128 * part + 128]
    for chunk in range(2):
        start = 8 * chunk * FEATS

        def feature(ref, at, start=start):
            return ref[pl.ds(start + at, 8, stride=FEATS), :]

        def gap(axis):
            return feature(gather_a, CENTRE + axis) - feature(gather_b, CENTRE + axis)

        live = feature(gather_a, LIVE) > 0.0
        x = jnp.where(live, gap(0), 3.0)
        y = jnp.where(live, gap(1), 3.0)
        z = jnp.where(live, gap(2), 3.0)
        tensors = derivatives(x, y, z)
        held_a = {}
        held_b = {}
        for alpha in MULTI:
            held_a[alpha] = feature(gather_a, PLACE[alpha]) * (-1.0 / fact(alpha))
            held_b[alpha] = feature(gather_b, PLACE[alpha]) * (
                -((-1.0) ** sum(alpha)) / fact(alpha)
            )
        for beta in MULTI:
            to_a = None
            to_b = None
            for alpha in MULTI:
                if sum(alpha) + sum(beta) > 4:
                    continue
                tensor = tensors[added(alpha, beta)]
                term_a = held_b[alpha] * tensor
                term_b = held_a[alpha] * tensor
                to_a = term_a if to_a is None else to_a + term_a
                to_b = term_b if to_b is None else to_b + term_b
            if sum(beta) % 2:
                to_b = -to_b
            gather_a[pl.ds(start + PLACE[beta], 8, stride=FEATS), :] = to_a
            gather_b[pl.ds(start + PLACE[beta], 8, stride=FEATS), :] = to_b
    sums_a = jnp.zeros((3 * FEATS, OWN), f32)
    sums_b = jnp.zeros((3 * FEATS, ENTRIES), f32)
    turned = (((1,), (1,)), ((), ()))
    for block in range(FAR_BLOCKS):
        a, b, _, _ = far_block(block)
        rows = far_rows(block)
        got_a = jnp.concatenate([gather_a[part, :] for part in rows], 1)
        got_b = jnp.concatenate([gather_b[part, :] for part in rows], 1)
        parts_a = jnp.concatenate(split3(got_a), 0).astype(bf16)
        parts_b = jnp.concatenate(split3(got_b), 0).astype(bf16)
        hot_a = one_hot(a, OWN)
        hot_b = one_hot(b, ENTRIES)
        sums_a = sums_a + lax.dot_general(parts_a, hot_a, turned, preferred_element_type=f32)
        sums_b = sums_b + lax.dot_general(parts_b, hot_b, turned, preferred_element_type=f32)
    got_a = jnp.concatenate([joined(sums_a), jnp.zeros((128 - FEATS, OWN), f32)], 0)
    got_b = jnp.concatenate([joined(sums_b), jnp.zeros((128 - FEATS, ENTRIES), f32)], 0)
    keep = lane_ids((1, 128)) < TERMS
    terms_a = jnp.where(keep, got_a.T, 0.0)
    terms_b = jnp.where(keep, got_b.T, 0.0)
    leaf_terms[...] = terms_a[:LEAVES] + terms_b[:LEAVES]
    parent_terms[...] = terms_a[LEAVES:OWN] + terms_b[LEAVES:OWN]
    leaf_start = OWN
    parent_start = OWN + 4 * SLOTS
    for way in range(4):
        leaf_first = leaf_start + way * SLOTS
        parent_first = parent_start + way * PSLOTS
        outgoing[way][BODY_ROWS:, :] = three_to_a_row(
            terms_b[leaf_first : leaf_first + SLOTS],
            terms_b[parent_first : parent_first + PSLOTS],
        )


def back_kernel(
    places,
    counts,
    send,
    send_p,
    bodies,
    field_in,
    leaf_in,
    parent_in,
    down,
    in_0,
    in_1,
    in_2,
    in_3,
    result,
    field,
    leaf_terms,
    parent_terms,
    tiles,
    arrived,
    out,
    sems,
):
    place = placing(places)
    incoming = (in_0, in_1, in_2, in_3)
    leaf_terms[...] = leaf_in[...]
    parent_terms[...] = parent_in[...]
    for way in range(4):
        leaf_rows, parent_rows = one_to_a_row(incoming[way][BODY_ROWS:, :])
        arrived[:SLOTS, :] = leaf_rows
        arrived[SLOTS:, :] = parent_rows

        def leaf_step(g, carry, way=way):
            at = [16 * g + u for u in range(16)]
            leaves = [send[0, way * SLOTS + k] for k in at]
            bodies_now = [
                field[leaf] + incoming[way][pl.ds(pl.multiple_of(8 * k, 8), 8), :]
                for k, leaf in zip(at, leaves)
            ]
            terms_now = [
                leaf_terms[pl.ds(leaf, 1), :] + arrived[pl.ds(k, 1), :]
                for k, leaf in zip(at, leaves)
            ]
            for leaf, value, terms in zip(leaves, bodies_now, terms_now):
                field[leaf] = value
                leaf_terms[pl.ds(leaf, 1), :] = terms
            return carry

        lax.fori_loop(0, SLOTS // 16, leaf_step, 0)
        chosen = [send_p[0, way * PSLOTS + k] for k in range(PSLOTS)]
        terms_now = [
            parent_terms[pl.ds(cell, 1), :] + arrived[pl.ds(SLOTS + k, 1), :]
            for k, cell in enumerate(chosen)
        ]
        for cell, terms in zip(chosen, terms_now):
            parent_terms[pl.ds(cell, 1), :] = terms
    half_z = CZ // 2
    for at in range(8):
        moved = jnp.dot(
            parent_terms[...],
            down[:, 128 * at : 128 * at + 128],
            precision=lax.Precision.HIGHEST,
            preferred_element_type=f32,
        )
        first = (at >> 2 & 1) * CY * CZ + (at >> 1 & 1) * CZ + (at & 1)
        for py in range(CY // 2):
            rows = pl.ds(first + 2 * CZ * py, half_z, stride=2)
            leaf_terms[rows, :] = leaf_terms[rows, :] + moved[half_z * py : half_z * py + half_z]

    lane = lane_ids((8, 128))
    inverse_factorials = jnp.zeros((8, 128), f32)
    for alpha in MULTI:
        inverse_factorials = jnp.where(lane == PLACE[alpha], 1.0 / fact(alpha), inverse_factorials)

    def group_step(g, carry):
        rows = pl.ds(pl.multiple_of(8 * g, 8), 8)
        cx, cy, cz = group_centre(place, g)
        _, px, py, pz = wide_rows(bodies, g)
        x, y, z = px - cx, py - cy, pz - cz
        terms = leaf_terms[rows, :] * inverse_factorials

        def coefficient(*alpha):
            at = PLACE[alpha]
            return jnp.broadcast_to(terms[:, at : at + 1], (8, LEAF))

        def nested(values, t):
            total, slope = values[-1], None
            for value in values[-2::-1]:
                slope = total if slope is None else slope * t + total
                total = total * t + value
            return total, slope

        def plain(values, t):
            total = values[-1]
            for value in values[-2::-1]:
                total = total * t + value
            return total

        by_x = []
        by_x_y = []
        by_x_z = []
        for i in range(5):
            in_z = [
                nested([coefficient(i, j, k) for k in range(5 - i - j)], z) for j in range(5 - i)
            ]
            value, slope = nested([pair[0] for pair in in_z], y)
            by_x.append(value)
            if i < 4:
                by_x_y.append(slope)
                by_x_z.append(plain([pair[1] for pair in in_z[:-1]], y))
        value, slope = nested(by_x, x)
        values = [value, -slope, -plain(by_x_y, x), -plain(by_x_z, x)]
        for at, value in enumerate(values):
            tiles[pl.ds(64 * g + at, 8, stride=8), :] = value[:, :HALF]
            tiles[pl.ds(64 * g + 4 + at, 8, stride=8), :] = value[:, HALF:]
        row = row_ids((8, HALF))
        body = lane_ids((8, HALF)) + jnp.where(row < 4, 0, HALF)
        for u in range(8):
            leaf = 8 * g + u
            tile = tiles[pl.ds(pl.multiple_of(8 * leaf, 8), 8), :] + field[leaf]
            tile = jnp.where(body < counts[leaf], tile, 0.0)
            start = pl.multiple_of(leaf * LEAF, LEAF)
            out[:, pl.ds(start, HALF)] = tile[:4]
            out[:, pl.ds(start + HALF, HALF)] = tile[4:]
        return carry

    copies = []
    for part in range(4):
        groups = LEAVES // 32
        lax.fori_loop(groups * part, groups * (part + 1), group_step, 0, unroll=4)
        lanes = pl.ds(8 * LEAF * groups * part, 8 * LEAF * groups)
        copies.append(
            pltpu.make_async_copy(out.at[:, lanes], result.at[:, lanes], sems.at[part])
        )
        copies[-1].start()
    for copy in copies:
        copy.wait()


VMEM = pl.BlockSpec(memory_space=pltpu.VMEM)
SMEM = pl.BlockSpec(memory_space=pltpu.SMEM)
HBM = pl.BlockSpec(memory_space=pltpu.HBM)
params = pltpu.CompilerParams(vmem_limit_bytes=20 * 1024 * 1024)
packed = jax.ShapeDtypeStruct((PACK_ROWS, 128), f32)
tiled = jax.ShapeDtypeStruct((LEAVES + 1, 8, HALF), f32)
heavy = pl.CostEstimate(flops=20_000_000_000, bytes_accessed=2_000_000, transcendentals=0)


def shaped(*dims):
    return jax.ShapeDtypeStruct(dims, f32)


def on_device(
    positions, masses, leaf_counts, send_leaves, send_parents, near_pairs, far_pairs, parent_pairs
):
    slab_count = lax.axis_size("slab")
    sub_count = lax.axis_size("sub")
    places = (slab_count, sub_count)

    def rows_first(lists):
        return jnp.transpose(lists, (1, 0, 2))

    sent = pl.pallas_call(
        functools.partial(front_kernel, places),
        out_shape=[shaped(8 * LEAVES + 8, HALF), shaped(LEAVES, 128), shaped(PARENTS, 128)]
        + [jax.ShapeDtypeStruct((8, LIST), i32)]
        + [packed] * 4,
        in_specs=[HBM] * 7,
        out_specs=[VMEM] * 8,
        scratch_shapes=[
            pltpu.SMEM(send_leaves.shape, i32),
            pltpu.SMEM(send_parents.shape, i32),
            pltpu.SMEM((1, LEAVES), i32),
            pltpu.VMEM((1, LEAVES), i32),
            pltpu.VMEM((3, 1, near_pairs.shape[2]), i32),
            pltpu.VMEM(positions.shape, f32),
            pltpu.VMEM((2 * LEAVES, HALF), f32),
            pltpu.VMEM(UP.shape, f32),
            pltpu.SemaphoreType.DMA((8,)),
            pltpu.VMEM((4 * (SLOTS + PSLOTS), 128), f32),
        ],
        compiler_params=params,
        name="moments_and_packing",
    )(
        *(
            pltpu.with_memory_space_constraint(value, pltpu.HBM)
            for value in (
                send_leaves,
                send_parents,
                leaf_counts.reshape(1, LEAVES),
                rows_first(near_pairs),
                positions,
                masses.reshape(2 * LEAVES, HALF),
                jnp.asarray(UP),
            )
        )
    )
    bodies = sent[0].reshape(LEAVES + 1, 8, HALF)
    moments, parents, words = sent[1:4]

    def exchange(value, way, back):
        pairs = []
        for s in range(slab_count):
            for u in range(sub_count):
                here = s * sub_count + u
                there = (s + slab_steps[way]) % slab_count * sub_count + (
                    u + sub_steps[way]
                ) % sub_count
                pairs.append((here, there) if back else (there, here))
        return lax.ppermute(value, ("slab", "sub"), pairs)

    incoming = [exchange(sent[4 + way], way, False) for way in range(4)]

    field = pl.pallas_call(
        functools.partial(self_kernel, places),
        out_shape=tiled,
        in_specs=[SMEM, VMEM],
        out_specs=VMEM,
        scratch_shapes=[pltpu.VMEM((GROUP, LEAF, LEAF), bf16)] * 4
        + [pltpu.VMEM((GROUP, 32, LEAF), bf16)] * 2
        + [pltpu.VMEM((GROUP, 2, 8, LEAF), f32)] * 2,
        compiler_params=params,
        cost_estimate=heavy,
        name="self_pairs",
    )(words, bodies)

    middle = pl.pallas_call(
        functools.partial(remote_kernel, places),
        out_shape=[tiled, shaped(LEAVES, 128), shaped(PARENTS, 128)] + [packed] * 4,
        in_specs=[SMEM] + [VMEM] * 10,
        out_specs=[VMEM] * 7,
        scratch_shapes=[
            pltpu.VMEM((4 * SLOTS + 1, 8, HALF), f32),
            pltpu.VMEM((4 * SLOTS + 1, 8, HALF), f32),
            pltpu.VMEM((16 * FEATS, 128), f32),
            pltpu.VMEM((16 * FEATS, 128), f32),
        ]
        + pair_scratch(GROUP // 2),
        compiler_params=params,
        input_output_aliases={10: 0},
        name="pairs_with_others",
    )(
        words,
        rows_first(far_pairs),
        rows_first(parent_pairs),
        bodies,
        moments,
        parents,
        *incoming,
        field,
    )
    field, leaf_terms, parent_terms = middle[:3]
    arrived = [exchange(middle[3 + way], way, True) for way in range(4)]

    field = pl.pallas_call(
        functools.partial(near_kernel, places),
        out_shape=tiled,
        in_specs=[SMEM] + [VMEM] * 2,
        out_specs=VMEM,
        scratch_shapes=pair_scratch(GROUP),
        compiler_params=params,
        cost_estimate=heavy,
        input_output_aliases={2: 0},
        name="own_pairs",
    )(words, bodies, field)

    return pl.pallas_call(
        functools.partial(back_kernel, places),
        out_shape=[shaped(4, LEAVES * LEAF), tiled],
        in_specs=[SMEM] * 3 + [VMEM] * 9,
        out_specs=[HBM, VMEM],
        input_output_aliases={4: 1},
        scratch_shapes=[
            pltpu.VMEM((LEAVES, 128), f32),
            pltpu.VMEM((PARENTS, 128), f32),
            pltpu.VMEM((8 * LEAVES, HALF), f32),
            pltpu.VMEM((SLOTS + PSLOTS, 128), f32),
            pltpu.VMEM((4, LEAVES * LEAF), f32),
            pltpu.SemaphoreType.DMA((4,)),
        ],
        compiler_params=params,
        name="shift_and_evaluate",
    )(
        leaf_counts,
        send_leaves,
        send_parents,
        sent[0],
        field,
        leaf_terms,
        parent_terms,
        jnp.asarray(DOWN),
        *arrived,
    )[0]


def solution(mesh):
    return jax.shard_map(
        on_device,
        mesh=mesh,
        in_specs=(
            P(None, ("slab", "sub")),
            P(("slab", "sub")),
            P(("slab", "sub")),
            P(("slab", "sub"), None),
            P(("slab", "sub"), None),
            P(("slab", "sub"), None, None),
            P(("slab", "sub"), None, None),
            P(("slab", "sub"), None, None),
        ),
        out_specs=P(None, ("slab", "sub")),
        check_vma=False,
    )
```

```python
import functools
import math

import jax
import jax.numpy as jnp
import ml_dtypes
import numpy as np
from jax import lax
from jax.experimental import pallas as pl
from jax.experimental.pallas import tpu as pltpu
from jax.sharding import PartitionSpec as P

CX = 2
CY = 4
CZ = 32

soft_square = 0.0025
slab_steps = (1, 0, 1, 1)
sub_steps = (0, 1, 1, -1)

LEAVES = CX * CY * CZ
PARENTS = LEAVES // 8
SLOTS = LEAVES // 4
PSLOTS = PARENTS // 2
HALF = 128
LEAF = 2 * HALF
BODY_ROWS = 8 * SLOTS
CELL_ROWS = SLOTS // 2
PACK_ROWS = BODY_ROWS + CELL_ROWS
GROUP = 8
bf16 = jnp.bfloat16
f32 = jnp.float32
i32 = jnp.int32

MULTI = [
    (i, j, n - i - j) for n in range(5) for i in range(n, -1, -1) for j in range(n - i, -1, -1)
]
PLACE = {alpha: at for at, alpha in enumerate(MULTI)}
TERMS = len(MULTI)
CENTRE = TERMS
LIVE = TERMS + 3
SIZES = (256, 192, 160, 128, 96)
EVERY_SIZE = tuple((size, at) for at, size in enumerate(SIZES))
SOME_SIZES = ((256, 0), (192, 2), (128, 4))
LIST = 384
STEPS_AT = LIST - 8
FEATS = 40
OWN = LEAVES + PARENTS
ENTRIES = 640
FAR_BLOCKS = 5


def fact(alpha):
    return math.prod(math.factorial(a) for a in alpha)


def added(alpha, beta):
    return tuple(a + b for a, b in zip(alpha, beta))


def taken(alpha, beta):
    return tuple(a - b for a, b in zip(alpha, beta))


def octant(at):
    return tuple(0.5 if bit else -0.5 for bit in (at >> 2 & 1, at >> 1 & 1, at & 1))


def power(delta, alpha):
    return math.prod(d**a for d, a in zip(delta, alpha))


def shift_matrices():
    up = np.zeros((8, 128, 128), np.float32)
    down = np.zeros((8, 128, 128), np.float32)
    for at in range(8):
        delta = octant(at)
        for alpha in MULTI:
            for beta in MULTI:
                rest = taken(alpha, beta)
                if min(rest) < 0:
                    continue
                choose = math.prod(math.comb(a, b) for a, b in zip(alpha, beta))
                up[at, PLACE[beta], PLACE[alpha]] = choose * power(delta, rest)
                down[at, PLACE[alpha], PLACE[beta]] = power(delta, rest) / fact(rest)
    up = up[:, :FEATS].reshape(8 * FEATS, 128)
    return up, down[:, :FEATS].transpose(1, 0, 2).reshape(FEATS, 8 * 128)


UP, DOWN = shift_matrices()


def row_ids(shape):
    return lax.broadcasted_iota(i32, shape, 0)


def lane_ids(shape):
    return lax.broadcasted_iota(i32, shape, 1)


def monomials(x, y, z):
    table = {(0, 0, 0): None}
    axes = (x, y, z)
    for alpha in MULTI[1:]:
        lead = max(axis for axis in range(3) if alpha[axis])
        less = tuple(a - (axis == lead) for axis, a in enumerate(alpha))
        table[alpha] = axes[lead] if table[less] is None else table[less] * axes[lead]
    return table


def split3(value):
    high = value.astype(bf16).astype(f32)
    rest = value - high
    middle = rest.astype(bf16).astype(f32)
    return high, middle, rest - middle


def soft_parts():
    rest = np.float32(soft_square)
    parts = []
    for _ in range(3):
        part = np.float32(rest.astype(ml_dtypes.bfloat16))
        parts.append(float(part))
        rest = np.float32(rest - part)
    return parts


SOFT = soft_parts()


def spread(tile):
    row = row_ids((8, HALF))
    turned = pltpu.roll(tile, 4, 0)
    low = row < 4
    return jnp.concatenate([jnp.where(low, tile, turned), jnp.where(low, turned, tile)], 1)


def fold(field):
    row = row_ids((8, HALF))
    return jnp.where(row < 4, field[:, :HALF], pltpu.roll(field[:, HALF:], 4, 0))


def offset_rows(ox, oy, oz):
    row = row_ids((8, LEAF)) & 3
    return jnp.where(row == 1, ox, jnp.where(row == 2, oy, jnp.where(row == 3, oz, 0.0)))


def features(tile, offset, as_row, as_column, as_weight):
    wide = spread(tile)
    row = row_ids((8, LEAF))
    first = (row & 3) == 0
    low = row < 4
    weight = jnp.broadcast_to(wide[0:1], (8, LEAF))
    x = jnp.where(first, 0.0, wide + offset)
    square = x * x
    pairwise = square + pltpu.roll(square, 1, 0)
    q = pairwise + pltpu.roll(pairwise, 2, 0)
    y = jnp.where(first, q, x)
    zero = jnp.zeros((8, LEAF), f32)
    out = [x, q]
    if as_row or as_column or as_weight:
        h, m, l = split3(y)
    if as_row:
        part_a = jnp.where(row == 4, m, h)
        part_b = jnp.where(row == 0, l, jnp.where(row == 4, 1.0, m))
        part_c = jnp.where(first, 1.0, jnp.where(low, h, l))
        part_d = jnp.where(row < 3, 1.0, 0.0)
        out.append(jnp.concatenate([part_a, part_b, part_c, part_d], 0).astype(bf16))
    if as_column:
        scale = jnp.where(first, 1.0, -2.0)
        h2, m2, l2 = h * scale, m * scale, l * scale
        mixed = jnp.where(low, h2, m2)
        part_a = jnp.where(first, 1.0, mixed)
        part_b = jnp.where(row == 0, 1.0, jnp.where(row == 4, h, mixed))
        part_c = jnp.where(row == 0, m, jnp.where(row == 4, l, jnp.where(low, l2, h2)))
        part_d = jnp.where(
            row == 0, SOFT[0], jnp.where(row == 1, SOFT[1], jnp.where(row == 2, SOFT[2], 0.0))
        )
        out.append(jnp.concatenate([part_a, part_b, part_c, part_d], 0).astype(bf16))
    if as_weight:
        heavy = jnp.where(low, y, 1.0) * weight
        out.append(jnp.concatenate(list(split3(heavy)) + [zero], 0).astype(bf16))
    return out


def field_of(sums, x, q):
    total = sums[0:8] + sums[8:16] + sums[16:24]
    row = row_ids((8, LEAF))
    first = (row & 3) == 0
    plain = pltpu.roll(total, 4, 0)
    inner = total - jnp.where(first, q - soft_square, x) * plain
    along = x * inner
    dots = along[1:2] + along[2:3] + along[3:4]
    return fold(jnp.where(row == 0, 2.0 * dots - inner, inner))


def cubes(row_part, column_part):
    square = lax.dot_general(
        row_part, column_part, (((0,), (0,)), ((), ())), preferred_element_type=f32
    )
    inverse = lax.rsqrt(square)
    return inverse * inverse * inverse


def padded(sums):
    lanes = sums.shape[1]
    if lanes == LEAF:
        return sums
    return jnp.concatenate([sums, jnp.zeros((sums.shape[0], LEAF - lanes), f32)], 1)


def pipeline(words, at, group, plan, early, late):
    @pl.when(words[at, STEPS_AT + len(SIZES) - 1] > 0)
    def _():
        for u in range(group):
            early(SIZES[0], 0, 0, u)

    begin = jnp.int32(0)
    for size, last in plan:

        def step(k, carry, size=size):
            for slot in range(2):
                done = []
                for u in range(group):
                    done.append(late(size, 2 * k + slot, slot, u))
                    early(size, 2 * k + slot + 1, 1 - slot, u)
                for store in done:
                    store()
            return carry

        end = words[at, STEPS_AT + last]
        lax.fori_loop(begin, end, step, 0)
        begin = end


def placing(places):
    slab_count, sub_count = places
    slab_at = lax.axis_index("slab")
    sub_at = lax.axis_index("sub")
    numbers = [slab_at * CX, sub_at * CY]
    for way in range(4):
        reach_x = slab_at + slab_steps[way]
        reach_y = sub_at + sub_steps[way]
        numbers.append(jnp.where(reach_x >= slab_count, slab_count * CX, 0))
        high = jnp.where(reach_y >= sub_count, sub_count * CY, 0)
        numbers.append(jnp.where(reach_y < 0, -sub_count * CY, high))
    return numbers


def jump_of(place, way):
    jump_x = jnp.int32(0)
    jump_y = jnp.int32(0)
    for at in range(4):
        jump_x = jnp.where(way == at, place[2 + 2 * at], jump_x)
        jump_y = jnp.where(way == at, place[3 + 2 * at], jump_y)
    return jump_x.astype(f32), jump_y.astype(f32)


def leaf_centre(place, leaf):
    return (
        -(place[0] + leaf // (CY * CZ)).astype(f32) - 0.5,
        -(place[1] + leaf // CZ % CY).astype(f32) - 0.5,
        -(leaf % CZ).astype(f32) - 0.5,
    )


def tall(part):
    rows = part.shape[0]
    if rows == LEAF:
        return part
    return jnp.concatenate([part, jnp.zeros((LEAF - rows, LEAF), bf16)], 0)


def halves(c):
    high = c.astype(bf16)
    return high, (c - high.astype(f32)).astype(bf16)


def self_loop(words, at, group, plan, place, bodies, field, scratch):
    high_refs, low_refs, weight_refs, spot_refs = scratch

    def early(size, k, slot, u):
        leaf = words[at, k * group + u]
        x, q, rows, columns, weights = features(
            bodies[leaf], offset_rows(*leaf_centre(place, leaf & (LEAVES - 1))), True, True, True
        )
        wide = LEAF if size > HALF else HALF
        high, low = halves(cubes(rows[:, :size], columns[:, :wide]))
        high_refs[slot][u, :size, :wide] = high
        low_refs[slot][u, :size, :wide] = low
        weight_refs[slot][u] = weights
        spot_refs[slot][u, 0] = x
        spot_refs[slot][u, 1] = q

    def late(size, k, slot, u):
        leaf = words[at, k * group + u]
        wide = LEAF if size > HALF else HALF
        w = weight_refs[slot][u, :, :size]
        sums = jnp.dot(
            w, high_refs[slot][u, :size, :wide], preferred_element_type=f32
        ) + jnp.dot(w, low_refs[slot][u, :size, :wide], preferred_element_type=f32)
        result = field_of(padded(sums), spot_refs[slot][u, 0], spot_refs[slot][u, 1])
        itself = jnp.where((row_ids((8, HALF)) & 3) == 0, bodies[leaf], 0.0)
        result = result + itself * soft_square**-0.5

        def store():
            field[leaf] = result

        return store

    pipeline(words, at, group, plan, early, late)


def pair_loop(
    words, at, group, plan, place, jumping, bodies, others, field, other_field, scratch
):
    high_refs, low_refs, across_refs, row_refs, column_refs, spot_refs = scratch
    turned = (((1,), (1,)), ((), ()))

    def unpack(k, u):
        word = words[at, k * group + u]
        return word & 511, word >> 9 & 511, word >> 18 & 1, (word >> 19 & 3) - 1, word >> 21 & 7

    def early(size, k, slot, u):
        row_leaf, column_leaf, swapped, lift, way = unpack(k, u)
        frame = jnp.where(swapped == 1, column_leaf, row_leaf) & (LEAVES - 1)
        cx, cy, cz = leaf_centre(place, frame)
        raised = (lift * CZ).astype(f32)
        swap = (swapped == 1).astype(f32)
        jump_x, jump_y = jump_of(place, way) if jumping else (0.0, 0.0)
        row_offset = offset_rows(cx, cy, cz + swap * raised)
        column_offset = offset_rows(cx + jump_x, cy + jump_y, cz + (1.0 - swap) * raised)
        xr, qr, rows, row_weights = features(bodies[row_leaf], row_offset, True, False, True)
        xc, qc, columns, column_weights = features(
            others[column_leaf], column_offset, False, True, True
        )
        high, low = halves(cubes(rows[:, :size], columns))
        high_refs[slot][u, :size] = high
        low_refs[slot][u, :size] = low
        if size > HALF:
            across_refs[slot][u] = tall(high).T
        row_refs[slot][u] = row_weights
        column_refs[slot][u] = column_weights
        spot_refs[slot][u, 0] = xr
        spot_refs[slot][u, 1] = qr
        spot_refs[slot][u, 2] = xc
        spot_refs[slot][u, 3] = qc

    def late(size, k, slot, u):
        row_leaf, column_leaf, _, _, _ = unpack(k, u)
        wr = row_refs[slot][u, :, :size]
        wc = column_refs[slot][u]
        high = high_refs[slot][u, :size]
        low = low_refs[slot][u, :size]
        column_sums = jnp.dot(wr, high, preferred_element_type=f32) + jnp.dot(
            wr, low, preferred_element_type=f32
        )
        row_sums = lax.dot_general(wc, low, turned, preferred_element_type=f32)
        if size > HALF:
            row_sums = padded(row_sums) + jnp.dot(
                wc, across_refs[slot][u], preferred_element_type=f32
            )
        else:
            row_sums += lax.dot_general(wc, high, turned, preferred_element_type=f32)
        row_field = field_of(padded(row_sums), spot_refs[slot][u, 0], spot_refs[slot][u, 1])
        column_field = field_of(column_sums, spot_refs[slot][u, 2], spot_refs[slot][u, 3])

        def store():
            field[row_leaf] = field[row_leaf] + row_field
            other_field[column_leaf] = other_field[column_leaf] + column_field

        return store

    pipeline(words, at, group, plan, early, late)


def pair_scratch(group):
    return (
        [pltpu.VMEM((group, LEAF, LEAF), bf16)] * 6
        + [pltpu.VMEM((group, 32, LEAF), bf16)] * 4
        + [pltpu.VMEM((group, 4, 8, LEAF), f32)] * 2
    )


def paired(scratch):
    return [scratch[at : at + 2] for at in range(0, len(scratch), 2)]


def front_kernel(places, *refs):
    stored, made, held, sems, chosen = refs[:7], refs[7:15], refs[15:23], refs[23], refs[24]
    bodies, moments, parents, words = made[:4]
    outs = made[4:]
    sources = (stored[0], stored[1], stored[2], *stored[2:])
    copies = [
        pltpu.make_async_copy(source, target, sems.at[at])
        for at, (source, target) in enumerate(zip(sources, held))
    ]
    for copy in copies:
        copy.start()
    send, send_p, counts, count_row, pairs, spots, masses, up = held
    place = placing(places)
    copies[3].wait()
    copies[4].wait()
    words[...] = work_lists(count_row[...], pairs[0], pairs[1], pairs[2])
    copies[2].wait()
    copies[5].wait()
    copies[6].wait()
    row = row_ids((8, HALF))

    def tile(g):
        count = jnp.zeros((8, HALF), i32)
        for u in range(8):
            leaf = 8 * g + u
            start = pl.multiple_of(leaf * LEAF, LEAF)
            low = spots[:, pl.ds(start, HALF)]
            high = spots[:, pl.ds(start + HALF, HALF)]
            blank = jnp.zeros((1, HALF), f32)
            bodies[pl.ds(pl.multiple_of(8 * leaf, 8), 8), :] = jnp.concatenate(
                [blank, low, blank, high], 0
            )
            count = jnp.where(row == u, counts[0, leaf], count)
        lane = lane_ids((8, HALF))
        for half in range(2):
            mass = masses[pl.ds(16 * g + half, 8, stride=2), :]
            bodies[pl.ds(64 * g + 4 * half, 8, stride=8), :] = jnp.where(
                lane + half * HALF < count, mass, 0.0
            )

    def cell_moments(g, parts):
        w, px, py, pz = parts
        cx, cy, cz = group_centre(place, g)
        axes = (px - cx, py - cy, pz - cz)
        table = {(0, 0, 0): w}
        lane = lane_ids((8, 128))
        built = jnp.zeros((8, 128), f32)
        for alpha in MULTI:
            if alpha not in table:
                lead = max(axis for axis in range(3) if alpha[axis])
                less = tuple(a - (axis == lead) for axis, a in enumerate(alpha))
                table[alpha] = table[less] * axes[lead]
            value = table[alpha]
            total = jnp.sum(value[:, :HALF] + value[:, HALF:], axis=1, keepdims=True)
            built = jnp.where(lane == PLACE[alpha], total, built)
        built = jnp.where(lane == CENTRE, cx, built)
        built = jnp.where(lane == CENTRE + 1, cy, built)
        built = jnp.where(lane == CENTRE + 2, cz, built)
        moments[pl.ds(pl.multiple_of(8 * g, 8), 8), :] = built

    def tile_step(g, carry):
        tile(g)
        return carry

    def group_step(g, carry):
        cell_moments(g, wide_rows(bodies, g))
        return carry

    lax.fori_loop(0, LEAVES // 8, tile_step, 0, unroll=4)
    lax.fori_loop(0, LEAVES // 8, group_step, 0, unroll=4)
    kind = row & 3
    bx = place[0].astype(f32) + 0.5
    by = place[1].astype(f32) + 0.5
    bodies[8 * LEAVES : 8 * LEAVES + 8, :] = jnp.where(
        kind == 1, bx, jnp.where(kind == 2, by, jnp.where(kind == 3, 0.5, 0.0))
    )
    copies[7].wait()
    half_z = CZ // 2
    summed = jnp.zeros((PARENTS, 128), f32)
    for at in range(8):
        first = (at >> 2 & 1) * CY * CZ + (at >> 1 & 1) * CZ + (at & 1)
        piece = jnp.concatenate(
            [moments[pl.ds(first + 2 * CZ * py, half_z, stride=2), :] for py in range(CY // 2)], 0
        )
        summed = summed + jnp.dot(
            piece[:, :FEATS],
            up[FEATS * at : FEATS * at + FEATS, :],
            precision=lax.Precision.HIGHEST,
            preferred_element_type=f32,
        )
    lane = lane_ids((PARENTS, 128))
    cell = row_ids((PARENTS, 128))
    summed = jnp.where(lane == CENTRE, place[0].astype(f32) + 1.0, summed)
    summed = jnp.where(
        lane == CENTRE + 1,
        place[1].astype(f32) + 1.0 + 2.0 * (cell // half_z).astype(f32),
        summed,
    )
    summed = jnp.where(lane == CENTRE + 2, 1.0 + 2.0 * (cell % half_z).astype(f32), summed)
    parents[...] = summed
    copies[0].wait()
    copies[1].wait()
    for way in range(4):

        def leaf_step(k, carry, way=way):
            leaf = send[0, way * SLOTS + k]
            outs[way][pl.ds(pl.multiple_of(8 * k, 8), 8), :] = bodies[
                pl.ds(pl.multiple_of(8 * leaf, 8), 8), :
            ]
            chosen[pl.ds(way * (SLOTS + PSLOTS) + k, 1), :] = moments[pl.ds(leaf, 1), :]
            return carry

        lax.fori_loop(0, SLOTS, leaf_step, 0, unroll=8)
        for k in range(PSLOTS):
            cell = send_p[0, way * PSLOTS + k]
            chosen[pl.ds(way * (SLOTS + PSLOTS) + SLOTS + k, 1), :] = parents[pl.ds(cell, 1), :]
        first = way * (SLOTS + PSLOTS)
        outs[way][BODY_ROWS:, :] = three_to_a_row(
            chosen[first : first + SLOTS, :], chosen[first + SLOTS : first + SLOTS + PSLOTS, :]
        )


def three_to_a_row(leaves, parents):
    rest = jnp.zeros((CELL_ROWS - parents.shape[0], 128), f32)
    return (
        leaves[:CELL_ROWS]
        + pltpu.roll(leaves[CELL_ROWS:], FEATS, 1)
        + pltpu.roll(jnp.concatenate([parents, rest], 0), 2 * FEATS, 1)
    )


def one_to_a_row(rows):
    keep = lane_ids(rows.shape) < FEATS
    parts = [rows, pltpu.roll(rows, 128 - FEATS, 1), pltpu.roll(rows, 128 - 2 * FEATS, 1)]
    parts = [jnp.where(keep, part, 0.0) for part in parts]
    return jnp.concatenate(parts[:2], 0), parts[2][:PSLOTS]


def wide_rows(bodies, g):
    return [
        jnp.concatenate(
            [bodies[pl.ds(64 * g + 4 * half + at, 8, stride=8), :] for half in range(2)], 1
        )
        for at in range(4)
    ]


def group_centre(place, g):
    cx = (place[0] + g // (CY * CZ // 8)).astype(f32) + 0.5
    cy = (place[1] + g // (CZ // 8) % CY).astype(f32) + 0.5
    base_z = (8 * (g % (CZ // 8))).astype(f32) + 0.5
    return cx, cy, row_ids((8, 1)).astype(f32) + base_z


def work_lists(counts, owned, partner, image):
    wide = (LEAVES, LEAVES)
    every = jnp.broadcast_to(counts.astype(f32), (8, LEAVES)).astype(bf16)

    def count_of(index):
        hot = jnp.where(row_ids(wide) == index, 1.0, 0.0).astype(bf16)
        return jnp.dot(every, hot, preferred_element_type=f32)[:1].astype(i32)

    mine = jnp.logical_and(partner >= 0, partner < LEAVES)
    other = partner >= LEAVES
    count_a = count_of(owned)
    count_b = count_of(partner)
    swapped = count_b < count_a
    lift = (image + 1) << 19
    own_word = (
        jnp.where(swapped, partner, owned)
        | jnp.where(swapped, owned, partner) << 9
        | jnp.where(swapped, 1, 0) << 18
        | lift
        | 4 << 21
    )
    spot = jnp.maximum(partner - LEAVES, 0)
    other_word = owned | spot << 9 | lift | (spot // SLOTS) << 21
    own_empty = LEAVES << 9 | 1 << 19 | 4 << 21
    other_empty = (4 * SLOTS) << 9 | 1 << 19 | 4 << 21
    yes = jnp.ones((1, LEAVES), jnp.bool_)
    lists = [
        (own_word, mine, jnp.minimum(count_a, count_b), own_empty, 2 * GROUP),
        (other_word, other, count_a, other_empty, GROUP),
        (lane_ids((1, LEAVES)), yes, counts, LEAVES, 2 * GROUP),
    ]
    flags = []
    for _, member, need, _, _ in lists:
        for at, size in enumerate(SIZES):
            fits = need <= size
            if at + 1 < len(SIZES):
                fits = jnp.logical_and(fits, need > SIZES[at + 1])
            flags.append(jnp.where(jnp.logical_and(member, fits), 1.0, 0.0))
    flags = jnp.concatenate(flags + [jnp.zeros((16 - len(flags), LEAVES), f32)], 0)
    before = jnp.where(row_ids(wide) < lane_ids(wide), 1.0, 0.0).astype(bf16)
    order = jnp.dot(flags.astype(bf16), before, preferred_element_type=f32)
    number = jnp.sum(flags, axis=1, keepdims=True)
    lane = lane_ids((1, LIST))
    rows = []
    for at, (word, member, _, empty, unit) in enumerate(lists):
        spot = jnp.zeros((1, LEAVES), f32)
        total = jnp.zeros((1, 1), f32)
        ends = []
        for row in range(len(SIZES) * at, len(SIZES) * (at + 1)):
            spot = spot + flags[row : row + 1] * (order[row : row + 1] + total)
            total = total + number[row : row + 1]
            ends.append((total.astype(i32) + (unit - 1)) // unit)
        spot = jnp.where(member, spot, -1.0).astype(i32)
        pieces = jnp.concatenate(
            [word & 255, word >> 8 & 255, word >> 16, jnp.zeros((5, LEAVES), i32)], 0
        )
        hot = jnp.where(row_ids(wide) == spot, 1.0, 0.0).astype(bf16)
        found = lax.dot_general(
            pieces.astype(f32).astype(bf16),
            hot,
            (((1,), (1,)), ((), ())),
            preferred_element_type=f32,
        ).astype(i32)
        joined = found[0:1] | found[1:2] << 8 | found[2:3] << 16
        joined = jnp.concatenate([joined, jnp.zeros((1, LIST - LEAVES), i32)], 1)
        joined = jnp.where(lane < total.astype(i32), joined, empty)
        for size_at, end in enumerate(ends):
            joined = jnp.where(lane == STEPS_AT + size_at, end, joined)
        rows.append(joined)
    return jnp.concatenate(rows + [jnp.zeros((5, LIST), i32)], 0)


def self_kernel(places, words, bodies, field, *scratch):
    place = placing(places)
    field[LEAVES] = jnp.zeros((8, HALF), f32)
    self_loop(words, 2, GROUP, EVERY_SIZE, place, bodies, field, paired(scratch))


def near_kernel(places, words, bodies, field_in, field, *scratch):
    place = placing(places)
    refs = paired(scratch)
    pair_loop(words, 0, GROUP, EVERY_SIZE, place, False, bodies, bodies, field, field, refs)


def derivatives(x, y, z):
    inverse = lax.rsqrt(x * x + y * y + z * z)
    square = inverse * inverse
    odd = [inverse]
    for _ in range(4):
        odd.append(odd[-1] * square)
    powers = monomials(x, y, z)
    result = {}
    for alpha in MULTI:
        degree = sum(alpha)
        total = None
        for p in range(alpha[0] // 2 + 1):
            for q in range(alpha[1] // 2 + 1):
                for s in range(alpha[2] // 2 + 1):
                    m = p + q + s
                    ways = math.prod(
                        math.factorial(a) // (2**c * math.factorial(c) * math.factorial(a - 2 * c))
                        for a, c in zip(alpha, (p, q, s))
                    )
                    sign = (-1.0) ** (degree - m)
                    double = math.prod(range(1, 2 * (degree - m), 2))
                    term = odd[degree - m] * (sign * double * ways)
                    rest = (alpha[0] - 2 * p, alpha[1] - 2 * q, alpha[2] - 2 * s)
                    if powers[rest] is not None:
                        term = term * powers[rest]
                    total = term if total is None else total + term
        result[alpha] = total
    return result


def remote_kernel(
    places,
    words,
    far,
    cells,
    bodies,
    moments,
    parents,
    in_0,
    in_1,
    in_2,
    in_3,
    field_in,
    field,
    leaf_terms,
    parent_terms,
    out_0,
    out_1,
    out_2,
    out_3,
    far_bodies,
    far_field,
    gather_a,
    gather_b,
    *scratch,
):
    place = placing(places)
    incoming = (in_0, in_1, in_2, in_3)
    outgoing = (out_0, out_1, out_2, out_3)
    for way in range(4):
        far_bodies[way * SLOTS : (way + 1) * SLOTS] = incoming[way][:BODY_ROWS, :].reshape(
            SLOTS, 8, HALF
        )
    far_bodies[4 * SLOTS] = bodies[LEAVES]
    far_field[...] = jnp.zeros_like(far_field)
    refs = paired(scratch)
    pair_loop(
        words, 1, GROUP // 2, SOME_SIZES, place, True, bodies, far_bodies, field, far_field, refs
    )
    for way in range(4):
        outgoing[way][:BODY_ROWS, :] = far_field[way * SLOTS : (way + 1) * SLOTS].reshape(
            BODY_ROWS, HALF
        )

    def moved(rows, way):
        lane = lane_ids(rows.shape)
        rows = jnp.where(lane == CENTRE, rows + place[2 + 2 * way].astype(f32), rows)
        return jnp.where(lane == CENTRE + 1, rows + place[3 + 2 * way].astype(f32), rows)

    arrived = [one_to_a_row(incoming[way][BODY_ROWS:, :]) for way in range(4)]
    table = [moments[...], parents[...]]
    for way in range(4):
        table.append(moved(arrived[way][0], way))
    for way in range(4):
        table.append(moved(arrived[way][1], way))
    table.append(jnp.zeros((ENTRIES - OWN - 4 * SLOTS - 4 * PSLOTS, 128), f32))
    columns = jnp.concatenate(table, 0).T[:FEATS]
    columns = jnp.concatenate(split3(columns), 0).astype(bf16)

    def one_hot(index, entries):
        return jnp.where(row_ids((entries, index.shape[1])) == index, 1.0, 0.0).astype(bf16)

    def joined(parts):
        return parts[:FEATS] + parts[FEATS : 2 * FEATS] + parts[2 * FEATS :]

    def far_block(block):
        if block < FAR_BLOCKS - 1:
            lanes = slice(LEAF * block, LEAF * block + LEAF)
            a, b, z = far[0, :, lanes], far[1, :, lanes], far[2, :, lanes]
            used = b >= 0
            b = jnp.where(b >= LEAVES, b + PARENTS, b)
        else:
            blank = jnp.zeros((1, 128 - cells.shape[2]), i32)
            a = jnp.concatenate([cells[0] + LEAVES, blank], 1)
            b = jnp.concatenate([cells[1], blank - 1], 1)
            z = jnp.concatenate([cells[2], blank], 1)
            used = b >= 0
            b = jnp.where(b >= PARENTS, b + (OWN + 4 * SLOTS - PARENTS), b + LEAVES)
            b = jnp.where(used, b, -1)
        a = jnp.where(used, a, -1)
        return a, b, (z * CZ).astype(f32), jnp.where(used, 1.0, 0.0)

    def far_rows(block):
        parts = range(2 * block, 2 * block + (2 if block < FAR_BLOCKS - 1 else 1))
        return [slice(FEATS * part, FEATS * part + FEATS) for part in parts]

    gather_a[...] = jnp.zeros_like(gather_a)
    gather_b[...] = jnp.zeros_like(gather_b)
    for block in range(FAR_BLOCKS):
        a, b, lift, used = far_block(block)
        place_of = row_ids((FEATS, a.shape[1]))
        got_a = joined(jnp.dot(columns[:, :OWN], one_hot(a, OWN), preferred_element_type=f32))
        got_b = joined(jnp.dot(columns, one_hot(b, ENTRIES), preferred_element_type=f32))
        got_a = jnp.where(place_of == LIVE, used, got_a)
        got_b = got_b + jnp.where(place_of == CENTRE + 2, lift, 0.0)
        for part, rows in enumerate(far_rows(block)):
            gather_a[rows, :] = got_a[:, 128 * part : 128 * part + 128]
            gather_b[rows, :] = got_b[:, 128 * part : 128 * part + 128]
    for chunk in range(2):
        start = 8 * chunk * FEATS

        def feature(ref, at, start=start):
            return ref[pl.ds(start + at, 8, stride=FEATS), :]

        def gap(axis):
            return feature(gather_a, CENTRE + axis) - feature(gather_b, CENTRE + axis)

        live = feature(gather_a, LIVE) > 0.0
        x = jnp.where(live, gap(0), 3.0)
        y = jnp.where(live, gap(1), 3.0)
        z = jnp.where(live, gap(2), 3.0)
        tensors = derivatives(x, y, z)
        held_a = {}
        held_b = {}
        for alpha in MULTI:
            held_a[alpha] = feature(gather_a, PLACE[alpha]) * (-1.0 / fact(alpha))
            held_b[alpha] = feature(gather_b, PLACE[alpha]) * (
                -((-1.0) ** sum(alpha)) / fact(alpha)
            )
        for beta in MULTI:
            to_a = None
            to_b = None
            for alpha in MULTI:
                if sum(alpha) + sum(beta) > 4:
                    continue
                tensor = tensors[added(alpha, beta)]
                term_a = held_b[alpha] * tensor
                term_b = held_a[alpha] * tensor
                to_a = term_a if to_a is None else to_a + term_a
                to_b = term_b if to_b is None else to_b + term_b
            if sum(beta) % 2:
                to_b = -to_b
            gather_a[pl.ds(start + PLACE[beta], 8, stride=FEATS), :] = to_a
            gather_b[pl.ds(start + PLACE[beta], 8, stride=FEATS), :] = to_b
    sums_a = jnp.zeros((3 * FEATS, OWN), f32)
    sums_b = jnp.zeros((3 * FEATS, ENTRIES), f32)
    turned = (((1,), (1,)), ((), ()))
    for block in range(FAR_BLOCKS):
        a, b, _, _ = far_block(block)
        rows = far_rows(block)
        got_a = jnp.concatenate([gather_a[part, :] for part in rows], 1)
        got_b = jnp.concatenate([gather_b[part, :] for part in rows], 1)
        parts_a = jnp.concatenate(split3(got_a), 0).astype(bf16)
        parts_b = jnp.concatenate(split3(got_b), 0).astype(bf16)
        hot_a = one_hot(a, OWN)
        hot_b = one_hot(b, ENTRIES)
        sums_a = sums_a + lax.dot_general(parts_a, hot_a, turned, preferred_element_type=f32)
        sums_b = sums_b + lax.dot_general(parts_b, hot_b, turned, preferred_element_type=f32)
    got_a = jnp.concatenate([joined(sums_a), jnp.zeros((128 - FEATS, OWN), f32)], 0)
    got_b = jnp.concatenate([joined(sums_b), jnp.zeros((128 - FEATS, ENTRIES), f32)], 0)
    keep = lane_ids((1, 128)) < TERMS
    terms_a = jnp.where(keep, got_a.T, 0.0)
    terms_b = jnp.where(keep, got_b.T, 0.0)
    leaf_terms[...] = terms_a[:LEAVES] + terms_b[:LEAVES]
    parent_terms[...] = terms_a[LEAVES:OWN] + terms_b[LEAVES:OWN]
    leaf_start = OWN
    parent_start = OWN + 4 * SLOTS
    for way in range(4):
        leaf_first = leaf_start + way * SLOTS
        parent_first = parent_start + way * PSLOTS
        outgoing[way][BODY_ROWS:, :] = three_to_a_row(
            terms_b[leaf_first : leaf_first + SLOTS],
            terms_b[parent_first : parent_first + PSLOTS],
        )


def back_kernel(
    places,
    counts,
    send,
    send_p,
    bodies,
    field_in,
    leaf_in,
    parent_in,
    down,
    in_0,
    in_1,
    in_2,
    in_3,
    result,
    field,
    leaf_terms,
    parent_terms,
    tiles,
    arrived,
    out,
    sems,
):
    place = placing(places)
    incoming = (in_0, in_1, in_2, in_3)
    leaf_terms[...] = leaf_in[...]
    parent_terms[...] = parent_in[...]
    for way in range(4):
        leaf_rows, parent_rows = one_to_a_row(incoming[way][BODY_ROWS:, :])
        arrived[:SLOTS, :] = leaf_rows
        arrived[SLOTS:, :] = parent_rows

        def leaf_step(g, carry, way=way):
            at = [16 * g + u for u in range(16)]
            leaves = [send[0, way * SLOTS + k] for k in at]
            bodies_now = [
                field[leaf] + incoming[way][pl.ds(pl.multiple_of(8 * k, 8), 8), :]
                for k, leaf in zip(at, leaves)
            ]
            terms_now = [
                leaf_terms[pl.ds(leaf, 1), :] + arrived[pl.ds(k, 1), :]
                for k, leaf in zip(at, leaves)
            ]
            for leaf, value, terms in zip(leaves, bodies_now, terms_now):
                field[leaf] = value
                leaf_terms[pl.ds(leaf, 1), :] = terms
            return carry

        lax.fori_loop(0, SLOTS // 16, leaf_step, 0)
        chosen = [send_p[0, way * PSLOTS + k] for k in range(PSLOTS)]
        terms_now = [
            parent_terms[pl.ds(cell, 1), :] + arrived[pl.ds(SLOTS + k, 1), :]
            for k, cell in enumerate(chosen)
        ]
        for cell, terms in zip(chosen, terms_now):
            parent_terms[pl.ds(cell, 1), :] = terms
    half_z = CZ // 2
    for at in range(8):
        moved = jnp.dot(
            parent_terms[:, :FEATS],
            down[:, 128 * at : 128 * at + 128],
            precision=lax.Precision.HIGHEST,
            preferred_element_type=f32,
        )
        first = (at >> 2 & 1) * CY * CZ + (at >> 1 & 1) * CZ + (at & 1)
        for py in range(CY // 2):
            rows = pl.ds(first + 2 * CZ * py, half_z, stride=2)
            leaf_terms[rows, :] = leaf_terms[rows, :] + moved[half_z * py : half_z * py + half_z]

    lane = lane_ids((8, 128))
    inverse_factorials = jnp.zeros((8, 128), f32)
    for alpha in MULTI:
        inverse_factorials = jnp.where(lane == PLACE[alpha], 1.0 / fact(alpha), inverse_factorials)

    def group_step(g, carry):
        rows = pl.ds(pl.multiple_of(8 * g, 8), 8)
        cx, cy, cz = group_centre(place, g)
        _, px, py, pz = wide_rows(bodies, g)
        x, y, z = px - cx, py - cy, pz - cz
        terms = leaf_terms[rows, :] * inverse_factorials

        def coefficient(*alpha):
            at = PLACE[alpha]
            return jnp.broadcast_to(terms[:, at : at + 1], (8, LEAF))

        def nested(values, t):
            total, slope = values[-1], None
            for value in values[-2::-1]:
                slope = total if slope is None else slope * t + total
                total = total * t + value
            return total, slope

        def plain(values, t):
            total = values[-1]
            for value in values[-2::-1]:
                total = total * t + value
            return total

        by_x = []
        by_x_y = []
        by_x_z = []
        for i in range(5):
            in_z = [
                nested([coefficient(i, j, k) for k in range(5 - i - j)], z) for j in range(5 - i)
            ]
            value, slope = nested([pair[0] for pair in in_z], y)
            by_x.append(value)
            if i < 4:
                by_x_y.append(slope)
                by_x_z.append(plain([pair[1] for pair in in_z[:-1]], y))
        value, slope = nested(by_x, x)
        values = [value, -slope, -plain(by_x_y, x), -plain(by_x_z, x)]
        for at, value in enumerate(values):
            tiles[pl.ds(64 * g + at, 8, stride=8), :] = value[:, :HALF]
            tiles[pl.ds(64 * g + 4 + at, 8, stride=8), :] = value[:, HALF:]
        row = row_ids((8, HALF))
        body = lane_ids((8, HALF)) + jnp.where(row < 4, 0, HALF)
        for u in range(8):
            leaf = 8 * g + u
            tile = tiles[pl.ds(pl.multiple_of(8 * leaf, 8), 8), :] + field[leaf]
            tile = jnp.where(body < counts[leaf], tile, 0.0)
            start = pl.multiple_of(leaf * LEAF, LEAF)
            out[:, pl.ds(start, HALF)] = tile[:4]
            out[:, pl.ds(start + HALF, HALF)] = tile[4:]
        return carry

    copies = []
    for part in range(4):
        groups = LEAVES // 32
        lax.fori_loop(groups * part, groups * (part + 1), group_step, 0, unroll=4)
        lanes = pl.ds(8 * LEAF * groups * part, 8 * LEAF * groups)
        copies.append(
            pltpu.make_async_copy(out.at[:, lanes], result.at[:, lanes], sems.at[part])
        )
        copies[-1].start()
    for copy in copies:
        copy.wait()


VMEM = pl.BlockSpec(memory_space=pltpu.VMEM)
SMEM = pl.BlockSpec(memory_space=pltpu.SMEM)
HBM = pl.BlockSpec(memory_space=pltpu.HBM)
params = pltpu.CompilerParams(vmem_limit_bytes=20 * 1024 * 1024)
packed = jax.ShapeDtypeStruct((PACK_ROWS, 128), f32)
tiled = jax.ShapeDtypeStruct((LEAVES + 1, 8, HALF), f32)
heavy = pl.CostEstimate(flops=20_000_000_000, bytes_accessed=2_000_000, transcendentals=0)


def shaped(*dims):
    return jax.ShapeDtypeStruct(dims, f32)


def on_device(
    positions, masses, leaf_counts, send_leaves, send_parents, near_pairs, far_pairs, parent_pairs
):
    slab_count = lax.axis_size("slab")
    sub_count = lax.axis_size("sub")
    places = (slab_count, sub_count)

    def rows_first(lists):
        return jnp.transpose(lists, (1, 0, 2))

    sent = pl.pallas_call(
        functools.partial(front_kernel, places),
        out_shape=[shaped(8 * LEAVES + 8, HALF), shaped(LEAVES, 128), shaped(PARENTS, 128)]
        + [jax.ShapeDtypeStruct((8, LIST), i32)]
        + [packed] * 4,
        in_specs=[HBM] * 7,
        out_specs=[VMEM] * 8,
        scratch_shapes=[
            pltpu.SMEM(send_leaves.shape, i32),
            pltpu.SMEM(send_parents.shape, i32),
            pltpu.SMEM((1, LEAVES), i32),
            pltpu.VMEM((1, LEAVES), i32),
            pltpu.VMEM((3, 1, near_pairs.shape[2]), i32),
            pltpu.VMEM(positions.shape, f32),
            pltpu.VMEM((2 * LEAVES, HALF), f32),
            pltpu.VMEM(UP.shape, f32),
            pltpu.SemaphoreType.DMA((8,)),
            pltpu.VMEM((4 * (SLOTS + PSLOTS), 128), f32),
        ],
        compiler_params=params,
        name="moments_and_packing",
    )(
        *(
            pltpu.with_memory_space_constraint(value, pltpu.HBM)
            for value in (
                send_leaves,
                send_parents,
                leaf_counts.reshape(1, LEAVES),
                rows_first(near_pairs),
                positions,
                masses.reshape(2 * LEAVES, HALF),
                jnp.asarray(UP),
            )
        )
    )
    bodies = sent[0].reshape(LEAVES + 1, 8, HALF)
    moments, parents, words = sent[1:4]

    def exchange(value, way, back):
        pairs = []
        for s in range(slab_count):
            for u in range(sub_count):
                here = s * sub_count + u
                there = (s + slab_steps[way]) % slab_count * sub_count + (
                    u + sub_steps[way]
                ) % sub_count
                pairs.append((here, there) if back else (there, here))
        return lax.ppermute(value, ("slab", "sub"), pairs)

    incoming = [exchange(sent[4 + way], way, False) for way in range(4)]

    field = pl.pallas_call(
        functools.partial(self_kernel, places),
        out_shape=tiled,
        in_specs=[SMEM, VMEM],
        out_specs=VMEM,
        scratch_shapes=[pltpu.VMEM((GROUP, LEAF, LEAF), bf16)] * 4
        + [pltpu.VMEM((GROUP, 32, LEAF), bf16)] * 2
        + [pltpu.VMEM((GROUP, 2, 8, LEAF), f32)] * 2,
        compiler_params=params,
        cost_estimate=heavy,
        name="self_pairs",
    )(words, bodies)

    middle = pl.pallas_call(
        functools.partial(remote_kernel, places),
        out_shape=[tiled, shaped(LEAVES, 128), shaped(PARENTS, 128)] + [packed] * 4,
        in_specs=[SMEM] + [VMEM] * 10,
        out_specs=[VMEM] * 7,
        scratch_shapes=[
            pltpu.VMEM((4 * SLOTS + 1, 8, HALF), f32),
            pltpu.VMEM((4 * SLOTS + 1, 8, HALF), f32),
            pltpu.VMEM((16 * FEATS, 128), f32),
            pltpu.VMEM((16 * FEATS, 128), f32),
        ]
        + pair_scratch(GROUP // 2),
        compiler_params=params,
        input_output_aliases={10: 0},
        name="pairs_with_others",
    )(
        words,
        rows_first(far_pairs),
        rows_first(parent_pairs),
        bodies,
        moments,
        parents,
        *incoming,
        field,
    )
    field, leaf_terms, parent_terms = middle[:3]
    arrived = [exchange(middle[3 + way], way, True) for way in range(4)]

    field = pl.pallas_call(
        functools.partial(near_kernel, places),
        out_shape=tiled,
        in_specs=[SMEM] + [VMEM] * 2,
        out_specs=VMEM,
        scratch_shapes=pair_scratch(GROUP),
        compiler_params=params,
        cost_estimate=heavy,
        input_output_aliases={2: 0},
        name="own_pairs",
    )(words, bodies, field)

    return pl.pallas_call(
        functools.partial(back_kernel, places),
        out_shape=[shaped(4, LEAVES * LEAF), tiled],
        in_specs=[SMEM] * 3 + [VMEM] * 9,
        out_specs=[HBM, VMEM],
        input_output_aliases={4: 1},
        scratch_shapes=[
            pltpu.VMEM((LEAVES, 128), f32),
            pltpu.VMEM((PARENTS, 128), f32),
            pltpu.VMEM((8 * LEAVES, HALF), f32),
            pltpu.VMEM((SLOTS + PSLOTS, 128), f32),
            pltpu.VMEM((4, LEAVES * LEAF), f32),
            pltpu.SemaphoreType.DMA((4,)),
        ],
        compiler_params=params,
        name="shift_and_evaluate",
    )(
        leaf_counts,
        send_leaves,
        send_parents,
        sent[0],
        field,
        leaf_terms,
        parent_terms,
        jnp.asarray(DOWN),
        *arrived,
    )[0]


def solution(mesh):
    return jax.shard_map(
        on_device,
        mesh=mesh,
        in_specs=(
            P(None, ("slab", "sub")),
            P(("slab", "sub")),
            P(("slab", "sub")),
            P(("slab", "sub"), None),
            P(("slab", "sub"), None),
            P(("slab", "sub"), None, None),
            P(("slab", "sub"), None, None),
            P(("slab", "sub"), None, None),
        ),
        out_specs=P(None, ("slab", "sub")),
        check_vma=False,
    )
```

```python
import functools
import math

import jax
import jax.numpy as jnp
import ml_dtypes
import numpy as np
from jax import lax
from jax.experimental import pallas as pl
from jax.experimental.pallas import tpu as pltpu
from jax.sharding import PartitionSpec as P

CX = 2
CY = 4
CZ = 32

soft_square = 0.0025
slab_steps = (1, 0, 1, 1)
sub_steps = (0, 1, 1, -1)

LEAVES = CX * CY * CZ
PARENTS = LEAVES // 8
SLOTS = LEAVES // 4
PSLOTS = PARENTS // 2
HALF = 128
LEAF = 2 * HALF
BODY_ROWS = 8 * SLOTS
CELL_ROWS = SLOTS // 2
PACK_ROWS = BODY_ROWS + CELL_ROWS
GROUP = 8
bf16 = jnp.bfloat16
f32 = jnp.float32
i32 = jnp.int32

MULTI = [
    (i, j, n - i - j) for n in range(5) for i in range(n, -1, -1) for j in range(n - i, -1, -1)
]
PLACE = {alpha: at for at, alpha in enumerate(MULTI)}
TERMS = len(MULTI)
CENTRE = TERMS
LIVE = TERMS + 3
SIZES = (256, 224, 192, 160, 128, 96)
EVERY_SIZE = tuple((size, at) for at, size in enumerate(SIZES))
LIST = 384
STEPS_AT = LIST - 8
FEATS = 40
OWN = LEAVES + PARENTS
ENTRIES = 640
FAR_BLOCKS = 5


def fact(alpha):
    return math.prod(math.factorial(a) for a in alpha)


def added(alpha, beta):
    return tuple(a + b for a, b in zip(alpha, beta))


def taken(alpha, beta):
    return tuple(a - b for a, b in zip(alpha, beta))


def octant(at):
    return tuple(0.5 if bit else -0.5 for bit in (at >> 2 & 1, at >> 1 & 1, at & 1))


def power(delta, alpha):
    return math.prod(d**a for d, a in zip(delta, alpha))


def shift_matrices():
    up = np.zeros((8, 128, 128), np.float32)
    down = np.zeros((8, 128, 128), np.float32)
    for at in range(8):
        delta = octant(at)
        for alpha in MULTI:
            for beta in MULTI:
                rest = taken(alpha, beta)
                if min(rest) < 0:
                    continue
                choose = math.prod(math.comb(a, b) for a, b in zip(alpha, beta))
                up[at, PLACE[beta], PLACE[alpha]] = choose * power(delta, rest)
                down[at, PLACE[alpha], PLACE[beta]] = power(delta, rest) / fact(rest)
    up = up[:, :FEATS].reshape(8 * FEATS, 128)
    return up, down[:, :FEATS].transpose(1, 0, 2).reshape(FEATS, 8 * 128)


UP, DOWN = shift_matrices()


def row_ids(shape):
    return lax.broadcasted_iota(i32, shape, 0)


def lane_ids(shape):
    return lax.broadcasted_iota(i32, shape, 1)


def monomials(x, y, z):
    table = {(0, 0, 0): None}
    axes = (x, y, z)
    for alpha in MULTI[1:]:
        lead = max(axis for axis in range(3) if alpha[axis])
        less = tuple(a - (axis == lead) for axis, a in enumerate(alpha))
        table[alpha] = axes[lead] if table[less] is None else table[less] * axes[lead]
    return table


def split3(value):
    high = value.astype(bf16).astype(f32)
    rest = value - high
    middle = rest.astype(bf16).astype(f32)
    return high, middle, rest - middle


def soft_parts():
    rest = np.float32(soft_square)
    parts = []
    for _ in range(3):
        part = np.float32(rest.astype(ml_dtypes.bfloat16))
        parts.append(float(part))
        rest = np.float32(rest - part)
    return parts


SOFT = soft_parts()


def spread(tile):
    row = row_ids((8, HALF))
    turned = pltpu.roll(tile, 4, 0)
    low = row < 4
    return jnp.concatenate([jnp.where(low, tile, turned), jnp.where(low, turned, tile)], 1)


def fold(field):
    row = row_ids((8, HALF))
    return jnp.where(row < 4, field[:, :HALF], pltpu.roll(field[:, HALF:], 4, 0))


def offset_rows(ox, oy, oz):
    row = row_ids((8, LEAF)) & 3
    return jnp.where(row == 1, ox, jnp.where(row == 2, oy, jnp.where(row == 3, oz, 0.0)))


def features(tile, offset, as_row, as_column, as_weight):
    wide = spread(tile)
    row = row_ids((8, LEAF))
    first = (row & 3) == 0
    low = row < 4
    weight = jnp.broadcast_to(wide[0:1], (8, LEAF))
    x = jnp.where(first, 0.0, wide + offset)
    square = x * x
    pairwise = square + pltpu.roll(square, 1, 0)
    q = pairwise + pltpu.roll(pairwise, 2, 0)
    y = jnp.where(first, q, x)
    zero = jnp.zeros((8, LEAF), f32)
    out = [x, q]
    if as_row or as_column or as_weight:
        h, m, l = split3(y)
    if as_row:
        part_a = jnp.where(row == 4, m, h)
        part_b = jnp.where(row == 0, l, jnp.where(row == 4, 1.0, m))
        part_c = jnp.where(first, 1.0, jnp.where(low, h, l))
        part_d = jnp.where(row < 3, 1.0, 0.0)
        out.append(jnp.concatenate([part_a, part_b, part_c, part_d], 0).astype(bf16))
    if as_column:
        scale = jnp.where(first, 1.0, -2.0)
        h2, m2, l2 = h * scale, m * scale, l * scale
        mixed = jnp.where(low, h2, m2)
        part_a = jnp.where(first, 1.0, mixed)
        part_b = jnp.where(row == 0, 1.0, jnp.where(row == 4, h, mixed))
        part_c = jnp.where(row == 0, m, jnp.where(row == 4, l, jnp.where(low, l2, h2)))
        part_d = jnp.where(
            row == 0, SOFT[0], jnp.where(row == 1, SOFT[1], jnp.where(row == 2, SOFT[2], 0.0))
        )
        out.append(jnp.concatenate([part_a, part_b, part_c, part_d], 0).astype(bf16))
    if as_weight:
        heavy = jnp.where(low, y, 1.0) * weight
        out.append(jnp.concatenate(list(split3(heavy)) + [zero], 0).astype(bf16))
    return out


def field_of(sums, x, q):
    total = sums[0:8] + sums[8:16] + sums[16:24]
    row = row_ids((8, LEAF))
    first = (row & 3) == 0
    plain = pltpu.roll(total, 4, 0)
    inner = total - jnp.where(first, q - soft_square, x) * plain
    along = x * inner
    dots = along[1:2] + along[2:3] + along[3:4]
    return fold(jnp.where(row == 0, 2.0 * dots - inner, inner))


def cubes(row_part, column_part):
    square = lax.dot_general(
        row_part, column_part, (((0,), (0,)), ((), ())), preferred_element_type=f32
    )
    inverse = lax.rsqrt(square)
    return inverse * inverse * inverse


def padded(sums):
    lanes = sums.shape[1]
    if lanes == LEAF:
        return sums
    return jnp.concatenate([sums, jnp.zeros((sums.shape[0], LEAF - lanes), f32)], 1)


def pipeline(words, at, group, plan, early, late):
    @pl.when(words[at, STEPS_AT + len(SIZES) - 1] > 0)
    def _():
        for u in range(group):
            early(SIZES[0], 0, 0, u)

    begin = jnp.int32(0)
    for size, last in plan:

        def step(k, carry, size=size):
            for slot in range(2):
                done = []
                for u in range(group):
                    done.append(late(size, 2 * k + slot, slot, u))
                    early(size, 2 * k + slot + 1, 1 - slot, u)
                for store in done:
                    store()
            return carry

        end = words[at, STEPS_AT + last]
        lax.fori_loop(begin, end, step, 0)
        begin = end


def placing(places):
    slab_count, sub_count = places
    slab_at = lax.axis_index("slab")
    sub_at = lax.axis_index("sub")
    numbers = [slab_at * CX, sub_at * CY]
    for way in range(4):
        reach_x = slab_at + slab_steps[way]
        reach_y = sub_at + sub_steps[way]
        numbers.append(jnp.where(reach_x >= slab_count, slab_count * CX, 0))
        high = jnp.where(reach_y >= sub_count, sub_count * CY, 0)
        numbers.append(jnp.where(reach_y < 0, -sub_count * CY, high))
    return numbers


def jump_of(place, way):
    jump_x = jnp.int32(0)
    jump_y = jnp.int32(0)
    for at in range(4):
        jump_x = jnp.where(way == at, place[2 + 2 * at], jump_x)
        jump_y = jnp.where(way == at, place[3 + 2 * at], jump_y)
    return jump_x.astype(f32), jump_y.astype(f32)


def leaf_centre(place, leaf):
    return (
        -(place[0] + leaf // (CY * CZ)).astype(f32) - 0.5,
        -(place[1] + leaf // CZ % CY).astype(f32) - 0.5,
        -(leaf % CZ).astype(f32) - 0.5,
    )


def tall(part):
    rows = part.shape[0]
    if rows == LEAF:
        return part
    return jnp.concatenate([part, jnp.zeros((LEAF - rows, LEAF), bf16)], 0)


def halves(c):
    high = c.astype(bf16)
    return high, (c - high.astype(f32)).astype(bf16)


def self_loop(words, at, group, plan, place, bodies, field, scratch):
    high_refs, low_refs, weight_refs, spot_refs = scratch

    def early(size, k, slot, u):
        leaf = words[at, k * group + u]
        x, q, rows, columns, weights = features(
            bodies[leaf], offset_rows(*leaf_centre(place, leaf & (LEAVES - 1))), True, True, True
        )
        wide = LEAF if size > HALF else HALF
        high, low = halves(cubes(rows[:, :size], columns[:, :wide]))
        high_refs[slot][u, :size, :wide] = high
        low_refs[slot][u, :size, :wide] = low
        weight_refs[slot][u] = weights
        spot_refs[slot][u, 0] = x
        spot_refs[slot][u, 1] = q

    def late(size, k, slot, u):
        leaf = words[at, k * group + u]
        wide = LEAF if size > HALF else HALF
        w = weight_refs[slot][u, :, :size]
        sums = jnp.dot(
            w, high_refs[slot][u, :size, :wide], preferred_element_type=f32
        ) + jnp.dot(w, low_refs[slot][u, :size, :wide], preferred_element_type=f32)
        result = field_of(padded(sums), spot_refs[slot][u, 0], spot_refs[slot][u, 1])
        itself = jnp.where((row_ids((8, HALF)) & 3) == 0, bodies[leaf], 0.0)
        result = result + itself * soft_square**-0.5

        def store():
            field[leaf] = result

        return store

    pipeline(words, at, group, plan, early, late)


def pair_loop(
    words, at, group, plan, place, jumping, bodies, others, field, other_field, scratch
):
    high_refs, low_refs, across_refs, row_refs, column_refs, spot_refs = scratch
    turned = (((1,), (1,)), ((), ()))

    def unpack(k, u):
        word = words[at, k * group + u]
        return word & 511, word >> 9 & 511, word >> 18 & 1, (word >> 19 & 3) - 1, word >> 21 & 7

    def early(size, k, slot, u):
        row_leaf, column_leaf, swapped, lift, way = unpack(k, u)
        frame = jnp.where(swapped == 1, column_leaf, row_leaf) & (LEAVES - 1)
        cx, cy, cz = leaf_centre(place, frame)
        raised = (lift * CZ).astype(f32)
        swap = (swapped == 1).astype(f32)
        jump_x, jump_y = jump_of(place, way) if jumping else (0.0, 0.0)
        row_offset = offset_rows(cx, cy, cz + swap * raised)
        column_offset = offset_rows(cx + jump_x, cy + jump_y, cz + (1.0 - swap) * raised)
        xr, qr, rows, row_weights = features(bodies[row_leaf], row_offset, True, False, True)
        xc, qc, columns, column_weights = features(
            others[column_leaf], column_offset, False, True, True
        )
        high, low = halves(cubes(rows[:, :size], columns))
        high_refs[slot][u, :size] = high
        low_refs[slot][u, :size] = low
        if size > HALF:
            across_refs[slot][u] = tall(high).T
        row_refs[slot][u] = row_weights
        column_refs[slot][u] = column_weights
        spot_refs[slot][u, 0] = xr
        spot_refs[slot][u, 1] = qr
        spot_refs[slot][u, 2] = xc
        spot_refs[slot][u, 3] = qc

    def late(size, k, slot, u):
        row_leaf, column_leaf, _, _, _ = unpack(k, u)
        wr = row_refs[slot][u, :, :size]
        wc = column_refs[slot][u]
        high = high_refs[slot][u, :size]
        low = low_refs[slot][u, :size]
        column_sums = jnp.dot(wr, high, preferred_element_type=f32) + jnp.dot(
            wr, low, preferred_element_type=f32
        )
        row_sums = lax.dot_general(wc, low, turned, preferred_element_type=f32)
        if size > HALF:
            row_sums = padded(row_sums) + jnp.dot(
                wc, across_refs[slot][u], preferred_element_type=f32
            )
        else:
            row_sums += lax.dot_general(wc, high, turned, preferred_element_type=f32)
        row_field = field_of(padded(row_sums), spot_refs[slot][u, 0], spot_refs[slot][u, 1])
        column_field = field_of(column_sums, spot_refs[slot][u, 2], spot_refs[slot][u, 3])

        def store():
            field[row_leaf] = field[row_leaf] + row_field
            other_field[column_leaf] = other_field[column_leaf] + column_field

        return store

    pipeline(words, at, group, plan, early, late)


def pair_scratch(group):
    return (
        [pltpu.VMEM((group, LEAF, LEAF), bf16)] * 6
        + [pltpu.VMEM((group, 32, LEAF), bf16)] * 4
        + [pltpu.VMEM((group, 4, 8, LEAF), f32)] * 2
    )


def paired(scratch):
    return [scratch[at : at + 2] for at in range(0, len(scratch), 2)]


def front_kernel(places, *refs):
    stored, made, held, sems, chosen = refs[:7], refs[7:15], refs[15:23], refs[23], refs[24]
    bodies, moments, parents, words = made[:4]
    outs = made[4:]
    sources = (stored[0], stored[1], stored[2], *stored[2:])
    copies = [
        pltpu.make_async_copy(source, target, sems.at[at])
        for at, (source, target) in enumerate(zip(sources, held))
    ]
    for copy in copies:
        copy.start()
    send, send_p, counts, count_row, pairs, spots, masses, up = held
    place = placing(places)
    copies[3].wait()
    copies[4].wait()
    words[...] = work_lists(count_row[...], pairs[0], pairs[1], pairs[2])
    copies[2].wait()
    copies[5].wait()
    copies[6].wait()
    row = row_ids((8, HALF))

    def tile(g):
        count = jnp.zeros((8, HALF), i32)
        for u in range(8):
            leaf = 8 * g + u
            start = pl.multiple_of(leaf * LEAF, LEAF)
            low = spots[:, pl.ds(start, HALF)]
            high = spots[:, pl.ds(start + HALF, HALF)]
            blank = jnp.zeros((1, HALF), f32)
            bodies[pl.ds(pl.multiple_of(8 * leaf, 8), 8), :] = jnp.concatenate(
                [blank, low, blank, high], 0
            )
            count = jnp.where(row == u, counts[0, leaf], count)
        lane = lane_ids((8, HALF))
        for half in range(2):
            mass = masses[pl.ds(16 * g + half, 8, stride=2), :]
            bodies[pl.ds(64 * g + 4 * half, 8, stride=8), :] = jnp.where(
                lane + half * HALF < count, mass, 0.0
            )

    def cell_moments(g, parts):
        w, px, py, pz = parts
        cx, cy, cz = group_centre(place, g)
        axes = (px - cx, py - cy, pz - cz)
        table = {(0, 0, 0): w}
        lane = lane_ids((8, 128))
        built = jnp.zeros((8, 128), f32)
        for alpha in MULTI:
            if alpha not in table:
                lead = max(axis for axis in range(3) if alpha[axis])
                less = tuple(a - (axis == lead) for axis, a in enumerate(alpha))
                table[alpha] = table[less] * axes[lead]
            value = table[alpha]
            total = jnp.sum(value[:, :HALF] + value[:, HALF:], axis=1, keepdims=True)
            built = jnp.where(lane == PLACE[alpha], total, built)
        built = jnp.where(lane == CENTRE, cx, built)
        built = jnp.where(lane == CENTRE + 1, cy, built)
        built = jnp.where(lane == CENTRE + 2, cz, built)
        moments[pl.ds(pl.multiple_of(8 * g, 8), 8), :] = built

    def tile_step(g, carry):
        tile(g)
        return carry

    def group_step(g, carry):
        cell_moments(g, wide_rows(bodies, g))
        return carry

    lax.fori_loop(0, LEAVES // 8, tile_step, 0, unroll=4)
    lax.fori_loop(0, LEAVES // 8, group_step, 0, unroll=4)
    kind = row & 3
    bx = place[0].astype(f32) + 0.5
    by = place[1].astype(f32) + 0.5
    bodies[8 * LEAVES : 8 * LEAVES + 8, :] = jnp.where(
        kind == 1, bx, jnp.where(kind == 2, by, jnp.where(kind == 3, 0.5, 0.0))
    )
    copies[7].wait()
    half_z = CZ // 2
    summed = jnp.zeros((PARENTS, 128), f32)
    for at in range(8):
        first = (at >> 2 & 1) * CY * CZ + (at >> 1 & 1) * CZ + (at & 1)
        piece = jnp.concatenate(
            [moments[pl.ds(first + 2 * CZ * py, half_z, stride=2), :] for py in range(CY // 2)], 0
        )
        summed = summed + jnp.dot(
            piece[:, :FEATS],
            up[FEATS * at : FEATS * at + FEATS, :],
            precision=lax.Precision.HIGHEST,
            preferred_element_type=f32,
        )
    lane = lane_ids((PARENTS, 128))
    cell = row_ids((PARENTS, 128))
    summed = jnp.where(lane == CENTRE, place[0].astype(f32) + 1.0, summed)
    summed = jnp.where(
        lane == CENTRE + 1,
        place[1].astype(f32) + 1.0 + 2.0 * (cell // half_z).astype(f32),
        summed,
    )
    summed = jnp.where(lane == CENTRE + 2, 1.0 + 2.0 * (cell % half_z).astype(f32), summed)
    parents[...] = summed
    copies[0].wait()
    copies[1].wait()
    for way in range(4):

        def leaf_step(k, carry, way=way):
            leaf = send[0, way * SLOTS + k]
            outs[way][pl.ds(pl.multiple_of(8 * k, 8), 8), :] = bodies[
                pl.ds(pl.multiple_of(8 * leaf, 8), 8), :
            ]
            chosen[pl.ds(way * (SLOTS + PSLOTS) + k, 1), :] = moments[pl.ds(leaf, 1), :]
            return carry

        lax.fori_loop(0, SLOTS, leaf_step, 0, unroll=8)
        for k in range(PSLOTS):
            cell = send_p[0, way * PSLOTS + k]
            chosen[pl.ds(way * (SLOTS + PSLOTS) + SLOTS + k, 1), :] = parents[pl.ds(cell, 1), :]
        first = way * (SLOTS + PSLOTS)
        outs[way][BODY_ROWS:, :] = three_to_a_row(
            chosen[first : first + SLOTS, :], chosen[first + SLOTS : first + SLOTS + PSLOTS, :]
        )


def three_to_a_row(leaves, parents):
    rest = jnp.zeros((CELL_ROWS - parents.shape[0], 128), f32)
    return (
        leaves[:CELL_ROWS]
        + pltpu.roll(leaves[CELL_ROWS:], FEATS, 1)
        + pltpu.roll(jnp.concatenate([parents, rest], 0), 2 * FEATS, 1)
    )


def one_to_a_row(rows):
    keep = lane_ids(rows.shape) < FEATS
    parts = [rows, pltpu.roll(rows, 128 - FEATS, 1), pltpu.roll(rows, 128 - 2 * FEATS, 1)]
    parts = [jnp.where(keep, part, 0.0) for part in parts]
    return jnp.concatenate(parts[:2], 0), parts[2][:PSLOTS]


def wide_rows(bodies, g):
    return [
        jnp.concatenate(
            [bodies[pl.ds(64 * g + 4 * half + at, 8, stride=8), :] for half in range(2)], 1
        )
        for at in range(4)
    ]


def group_centre(place, g):
    cx = (place[0] + g // (CY * CZ // 8)).astype(f32) + 0.5
    cy = (place[1] + g // (CZ // 8) % CY).astype(f32) + 0.5
    base_z = (8 * (g % (CZ // 8))).astype(f32) + 0.5
    return cx, cy, row_ids((8, 1)).astype(f32) + base_z


def work_lists(counts, owned, partner, image):
    wide = (LEAVES, LEAVES)
    every = jnp.broadcast_to(counts.astype(f32), (8, LEAVES)).astype(bf16)

    def count_of(index):
        hot = jnp.where(row_ids(wide) == index, 1.0, 0.0).astype(bf16)
        return jnp.dot(every, hot, preferred_element_type=f32)[:1].astype(i32)

    mine = jnp.logical_and(partner >= 0, partner < LEAVES)
    other = partner >= LEAVES
    count_a = count_of(owned)
    count_b = count_of(partner)
    swapped = count_b < count_a
    lift = (image + 1) << 19
    own_word = (
        jnp.where(swapped, partner, owned)
        | jnp.where(swapped, owned, partner) << 9
        | jnp.where(swapped, 1, 0) << 18
        | lift
        | 4 << 21
    )
    spot = jnp.maximum(partner - LEAVES, 0)
    other_word = owned | spot << 9 | lift | (spot // SLOTS) << 21
    own_empty = LEAVES << 9 | 1 << 19 | 4 << 21
    other_empty = (4 * SLOTS) << 9 | 1 << 19 | 4 << 21
    yes = jnp.ones((1, LEAVES), jnp.bool_)
    lists = [
        (own_word, mine, jnp.minimum(count_a, count_b), own_empty, 2 * GROUP),
        (other_word, other, count_a, other_empty, GROUP),
        (lane_ids((1, LEAVES)), yes, counts, LEAVES, 2 * GROUP),
    ]
    flags = []
    for _, member, need, _, _ in lists:
        for at, size in enumerate(SIZES):
            fits = need <= size
            if at + 1 < len(SIZES):
                fits = jnp.logical_and(fits, need > SIZES[at + 1])
            flags.append(jnp.where(jnp.logical_and(member, fits), 1.0, 0.0))
    flags = jnp.concatenate(flags + [jnp.zeros((32 - len(flags), LEAVES), f32)], 0)
    before = jnp.where(row_ids(wide) < lane_ids(wide), 1.0, 0.0).astype(bf16)
    order = jnp.dot(flags.astype(bf16), before, preferred_element_type=f32)
    number = jnp.sum(flags, axis=1, keepdims=True)
    lane = lane_ids((1, LIST))
    rows = []
    for at, (word, member, _, empty, unit) in enumerate(lists):
        spot = jnp.zeros((1, LEAVES), f32)
        total = jnp.zeros((1, 1), f32)
        ends = []
        for row in range(len(SIZES) * at, len(SIZES) * (at + 1)):
            spot = spot + flags[row : row + 1] * (order[row : row + 1] + total)
            total = total + number[row : row + 1]
            ends.append((total.astype(i32) + (unit - 1)) // unit)
        spot = jnp.where(member, spot, -1.0).astype(i32)
        pieces = jnp.concatenate(
            [word & 255, word >> 8 & 255, word >> 16, jnp.zeros((5, LEAVES), i32)], 0
        )
        hot = jnp.where(row_ids(wide) == spot, 1.0, 0.0).astype(bf16)
        found = lax.dot_general(
            pieces.astype(f32).astype(bf16),
            hot,
            (((1,), (1,)), ((), ())),
            preferred_element_type=f32,
        ).astype(i32)
        joined = found[0:1] | found[1:2] << 8 | found[2:3] << 16
        joined = jnp.concatenate([joined, jnp.zeros((1, LIST - LEAVES), i32)], 1)
        joined = jnp.where(lane < total.astype(i32), joined, empty)
        for size_at, end in enumerate(ends):
            joined = jnp.where(lane == STEPS_AT + size_at, end, joined)
        rows.append(joined)
    return jnp.concatenate(rows + [jnp.zeros((5, LIST), i32)], 0)


def self_kernel(places, words, bodies, field, *scratch):
    place = placing(places)
    field[LEAVES] = jnp.zeros((8, HALF), f32)
    self_loop(words, 2, GROUP, EVERY_SIZE, place, bodies, field, paired(scratch))


def near_kernel(places, words, bodies, field_in, field, *scratch):
    place = placing(places)
    refs = paired(scratch)
    pair_loop(words, 0, GROUP, EVERY_SIZE, place, False, bodies, bodies, field, field, refs)


def derivatives(x, y, z):
    inverse = lax.rsqrt(x * x + y * y + z * z)
    square = inverse * inverse
    odd = [inverse]
    for _ in range(4):
        odd.append(odd[-1] * square)
    powers = monomials(x, y, z)
    result = {}
    for alpha in MULTI:
        degree = sum(alpha)
        total = None
        for p in range(alpha[0] // 2 + 1):
            for q in range(alpha[1] // 2 + 1):
                for s in range(alpha[2] // 2 + 1):
                    m = p + q + s
                    ways = math.prod(
                        math.factorial(a) // (2**c * math.factorial(c) * math.factorial(a - 2 * c))
                        for a, c in zip(alpha, (p, q, s))
                    )
                    sign = (-1.0) ** (degree - m)
                    double = math.prod(range(1, 2 * (degree - m), 2))
                    term = odd[degree - m] * (sign * double * ways)
                    rest = (alpha[0] - 2 * p, alpha[1] - 2 * q, alpha[2] - 2 * s)
                    if powers[rest] is not None:
                        term = term * powers[rest]
                    total = term if total is None else total + term
        result[alpha] = total
    return result


def remote_kernel(
    places,
    words,
    far,
    cells,
    bodies,
    moments,
    parents,
    in_0,
    in_1,
    in_2,
    in_3,
    field_in,
    field,
    leaf_terms,
    parent_terms,
    out_0,
    out_1,
    out_2,
    out_3,
    far_bodies,
    far_field,
    gather_a,
    gather_b,
    *scratch,
):
    place = placing(places)
    incoming = (in_0, in_1, in_2, in_3)
    outgoing = (out_0, out_1, out_2, out_3)
    for way in range(4):
        far_bodies[way * SLOTS : (way + 1) * SLOTS] = incoming[way][:BODY_ROWS, :].reshape(
            SLOTS, 8, HALF
        )
    far_bodies[4 * SLOTS] = bodies[LEAVES]
    far_field[...] = jnp.zeros_like(far_field)
    refs = paired(scratch)
    pair_loop(
        words, 1, GROUP // 2, EVERY_SIZE, place, True, bodies, far_bodies, field, far_field, refs
    )
    for way in range(4):
        outgoing[way][:BODY_ROWS, :] = far_field[way * SLOTS : (way + 1) * SLOTS].reshape(
            BODY_ROWS, HALF
        )

    def moved(rows, way):
        lane = lane_ids(rows.shape)
        rows = jnp.where(lane == CENTRE, rows + place[2 + 2 * way].astype(f32), rows)
        return jnp.where(lane == CENTRE + 1, rows + place[3 + 2 * way].astype(f32), rows)

    arrived = [one_to_a_row(incoming[way][BODY_ROWS:, :]) for way in range(4)]
    table = [moments[...], parents[...]]
    for way in range(4):
        table.append(moved(arrived[way][0], way))
    for way in range(4):
        table.append(moved(arrived[way][1], way))
    table.append(jnp.zeros((ENTRIES - OWN - 4 * SLOTS - 4 * PSLOTS, 128), f32))
    columns = jnp.concatenate(table, 0).T[:FEATS]
    columns = jnp.concatenate(split3(columns), 0).astype(bf16)

    def one_hot(index, entries):
        return jnp.where(row_ids((entries, index.shape[1])) == index, 1.0, 0.0).astype(bf16)

    def joined(parts):
        return parts[:FEATS] + parts[FEATS : 2 * FEATS] + parts[2 * FEATS :]

    def far_block(block):
        if block < FAR_BLOCKS - 1:
            lanes = slice(LEAF * block, LEAF * block + LEAF)
            a, b, z = far[0, :, lanes], far[1, :, lanes], far[2, :, lanes]
            used = b >= 0
            b = jnp.where(b >= LEAVES, b + PARENTS, b)
        else:
            blank = jnp.zeros((1, 128 - cells.shape[2]), i32)
            a = jnp.concatenate([cells[0] + LEAVES, blank], 1)
            b = jnp.concatenate([cells[1], blank - 1], 1)
            z = jnp.concatenate([cells[2], blank], 1)
            used = b >= 0
            b = jnp.where(b >= PARENTS, b + (OWN + 4 * SLOTS - PARENTS), b + LEAVES)
            b = jnp.where(used, b, -1)
        a = jnp.where(used, a, -1)
        return a, b, (z * CZ).astype(f32), jnp.where(used, 1.0, 0.0)

    def far_rows(block):
        parts = range(2 * block, 2 * block + (2 if block < FAR_BLOCKS - 1 else 1))
        return [slice(FEATS * part, FEATS * part + FEATS) for part in parts]

    gather_a[...] = jnp.zeros_like(gather_a)
    gather_b[...] = jnp.zeros_like(gather_b)
    for block in range(FAR_BLOCKS):
        a, b, lift, used = far_block(block)
        place_of = row_ids((FEATS, a.shape[1]))
        got_a = joined(jnp.dot(columns[:, :OWN], one_hot(a, OWN), preferred_element_type=f32))
        got_b = joined(jnp.dot(columns, one_hot(b, ENTRIES), preferred_element_type=f32))
        got_a = jnp.where(place_of == LIVE, used, got_a)
        got_b = got_b + jnp.where(place_of == CENTRE + 2, lift, 0.0)
        for part, rows in enumerate(far_rows(block)):
            gather_a[rows, :] = got_a[:, 128 * part : 128 * part + 128]
            gather_b[rows, :] = got_b[:, 128 * part : 128 * part + 128]
    for chunk in range(2):
        start = 8 * chunk * FEATS

        def feature(ref, at, start=start):
            return ref[pl.ds(start + at, 8, stride=FEATS), :]

        def gap(axis):
            return feature(gather_a, CENTRE + axis) - feature(gather_b, CENTRE + axis)

        live = feature(gather_a, LIVE) > 0.0
        x = jnp.where(live, gap(0), 3.0)
        y = jnp.where(live, gap(1), 3.0)
        z = jnp.where(live, gap(2), 3.0)
        tensors = derivatives(x, y, z)
        held_a = {}
        held_b = {}
        for alpha in MULTI:
            held_a[alpha] = feature(gather_a, PLACE[alpha]) * (-1.0 / fact(alpha))
            held_b[alpha] = feature(gather_b, PLACE[alpha]) * (
                -((-1.0) ** sum(alpha)) / fact(alpha)
            )
        for beta in MULTI:
            to_a = None
            to_b = None
            for alpha in MULTI:
                if sum(alpha) + sum(beta) > 4:
                    continue
                tensor = tensors[added(alpha, beta)]
                term_a = held_b[alpha] * tensor
                term_b = held_a[alpha] * tensor
                to_a = term_a if to_a is None else to_a + term_a
                to_b = term_b if to_b is None else to_b + term_b
            if sum(beta) % 2:
                to_b = -to_b
            gather_a[pl.ds(start + PLACE[beta], 8, stride=FEATS), :] = to_a
            gather_b[pl.ds(start + PLACE[beta], 8, stride=FEATS), :] = to_b
    sums_a = jnp.zeros((3 * FEATS, OWN), f32)
    sums_b = jnp.zeros((3 * FEATS, ENTRIES), f32)
    turned = (((1,), (1,)), ((), ()))
    for block in range(FAR_BLOCKS):
        a, b, _, _ = far_block(block)
        rows = far_rows(block)
        got_a = jnp.concatenate([gather_a[part, :] for part in rows], 1)
        got_b = jnp.concatenate([gather_b[part, :] for part in rows], 1)
        parts_a = jnp.concatenate(split3(got_a), 0).astype(bf16)
        parts_b = jnp.concatenate(split3(got_b), 0).astype(bf16)
        hot_a = one_hot(a, OWN)
        hot_b = one_hot(b, ENTRIES)
        sums_a = sums_a + lax.dot_general(parts_a, hot_a, turned, preferred_element_type=f32)
        sums_b = sums_b + lax.dot_general(parts_b, hot_b, turned, preferred_element_type=f32)
    got_a = jnp.concatenate([joined(sums_a), jnp.zeros((128 - FEATS, OWN), f32)], 0)
    got_b = jnp.concatenate([joined(sums_b), jnp.zeros((128 - FEATS, ENTRIES), f32)], 0)
    keep = lane_ids((1, 128)) < TERMS
    terms_a = jnp.where(keep, got_a.T, 0.0)
    terms_b = jnp.where(keep, got_b.T, 0.0)
    leaf_terms[...] = terms_a[:LEAVES] + terms_b[:LEAVES]
    parent_terms[...] = terms_a[LEAVES:OWN] + terms_b[LEAVES:OWN]
    leaf_start = OWN
    parent_start = OWN + 4 * SLOTS
    for way in range(4):
        leaf_first = leaf_start + way * SLOTS
        parent_first = parent_start + way * PSLOTS
        outgoing[way][BODY_ROWS:, :] = three_to_a_row(
            terms_b[leaf_first : leaf_first + SLOTS],
            terms_b[parent_first : parent_first + PSLOTS],
        )


def back_kernel(
    places,
    counts,
    send,
    send_p,
    bodies,
    field_in,
    leaf_in,
    parent_in,
    down,
    in_0,
    in_1,
    in_2,
    in_3,
    result,
    field,
    leaf_terms,
    parent_terms,
    tiles,
    arrived,
    out,
    sems,
):
    place = placing(places)
    incoming = (in_0, in_1, in_2, in_3)
    leaf_terms[...] = leaf_in[...]
    parent_terms[...] = parent_in[...]
    for way in range(4):
        leaf_rows, parent_rows = one_to_a_row(incoming[way][BODY_ROWS:, :])
        arrived[:SLOTS, :] = leaf_rows
        arrived[SLOTS:, :] = parent_rows

        def leaf_step(g, carry, way=way):
            at = [16 * g + u for u in range(16)]
            leaves = [send[0, way * SLOTS + k] for k in at]
            bodies_now = [
                field[leaf] + incoming[way][pl.ds(pl.multiple_of(8 * k, 8), 8), :]
                for k, leaf in zip(at, leaves)
            ]
            terms_now = [
                leaf_terms[pl.ds(leaf, 1), :] + arrived[pl.ds(k, 1), :]
                for k, leaf in zip(at, leaves)
            ]
            for leaf, value, terms in zip(leaves, bodies_now, terms_now):
                field[leaf] = value
                leaf_terms[pl.ds(leaf, 1), :] = terms
            return carry

        lax.fori_loop(0, SLOTS // 16, leaf_step, 0)
        chosen = [send_p[0, way * PSLOTS + k] for k in range(PSLOTS)]
        terms_now = [
            parent_terms[pl.ds(cell, 1), :] + arrived[pl.ds(SLOTS + k, 1), :]
            for k, cell in enumerate(chosen)
        ]
        for cell, terms in zip(chosen, terms_now):
            parent_terms[pl.ds(cell, 1), :] = terms
    half_z = CZ // 2
    for at in range(8):
        moved = jnp.dot(
            parent_terms[:, :FEATS],
            down[:, 128 * at : 128 * at + 128],
            precision=lax.Precision.HIGHEST,
            preferred_element_type=f32,
        )
        first = (at >> 2 & 1) * CY * CZ + (at >> 1 & 1) * CZ + (at & 1)
        for py in range(CY // 2):
            rows = pl.ds(first + 2 * CZ * py, half_z, stride=2)
            leaf_terms[rows, :] = leaf_terms[rows, :] + moved[half_z * py : half_z * py + half_z]

    lane = lane_ids((8, 128))
    inverse_factorials = jnp.zeros((8, 128), f32)
    for alpha in MULTI:
        inverse_factorials = jnp.where(lane == PLACE[alpha], 1.0 / fact(alpha), inverse_factorials)

    def group_step(g, carry):
        rows = pl.ds(pl.multiple_of(8 * g, 8), 8)
        cx, cy, cz = group_centre(place, g)
        _, px, py, pz = wide_rows(bodies, g)
        x, y, z = px - cx, py - cy, pz - cz
        terms = leaf_terms[rows, :] * inverse_factorials

        def coefficient(*alpha):
            at = PLACE[alpha]
            return jnp.broadcast_to(terms[:, at : at + 1], (8, LEAF))

        def nested(values, t):
            total, slope = values[-1], None
            for value in values[-2::-1]:
                slope = total if slope is None else slope * t + total
                total = total * t + value
            return total, slope

        def plain(values, t):
            total = values[-1]
            for value in values[-2::-1]:
                total = total * t + value
            return total

        by_x = []
        by_x_y = []
        by_x_z = []
        for i in range(5):
            in_z = [
                nested([coefficient(i, j, k) for k in range(5 - i - j)], z) for j in range(5 - i)
            ]
            value, slope = nested([pair[0] for pair in in_z], y)
            by_x.append(value)
            if i < 4:
                by_x_y.append(slope)
                by_x_z.append(plain([pair[1] for pair in in_z[:-1]], y))
        value, slope = nested(by_x, x)
        values = [value, -slope, -plain(by_x_y, x), -plain(by_x_z, x)]
        for at, value in enumerate(values):
            tiles[pl.ds(64 * g + at, 8, stride=8), :] = value[:, :HALF]
            tiles[pl.ds(64 * g + 4 + at, 8, stride=8), :] = value[:, HALF:]
        row = row_ids((8, HALF))
        body = lane_ids((8, HALF)) + jnp.where(row < 4, 0, HALF)
        for u in range(8):
            leaf = 8 * g + u
            tile = tiles[pl.ds(pl.multiple_of(8 * leaf, 8), 8), :] + field[leaf]
            tile = jnp.where(body < counts[leaf], tile, 0.0)
            start = pl.multiple_of(leaf * LEAF, LEAF)
            out[:, pl.ds(start, HALF)] = tile[:4]
            out[:, pl.ds(start + HALF, HALF)] = tile[4:]
        return carry

    copies = []
    for part in range(4):
        groups = LEAVES // 32
        lax.fori_loop(groups * part, groups * (part + 1), group_step, 0, unroll=4)
        lanes = pl.ds(8 * LEAF * groups * part, 8 * LEAF * groups)
        copies.append(
            pltpu.make_async_copy(out.at[:, lanes], result.at[:, lanes], sems.at[part])
        )
        copies[-1].start()
    for copy in copies:
        copy.wait()


VMEM = pl.BlockSpec(memory_space=pltpu.VMEM)
SMEM = pl.BlockSpec(memory_space=pltpu.SMEM)
HBM = pl.BlockSpec(memory_space=pltpu.HBM)
params = pltpu.CompilerParams(vmem_limit_bytes=20 * 1024 * 1024)
packed = jax.ShapeDtypeStruct((PACK_ROWS, 128), f32)
tiled = jax.ShapeDtypeStruct((LEAVES + 1, 8, HALF), f32)
heavy = pl.CostEstimate(flops=20_000_000_000, bytes_accessed=2_000_000, transcendentals=0)


def shaped(*dims):
    return jax.ShapeDtypeStruct(dims, f32)


def on_device(
    positions, masses, leaf_counts, send_leaves, send_parents, near_pairs, far_pairs, parent_pairs
):
    slab_count = lax.axis_size("slab")
    sub_count = lax.axis_size("sub")
    places = (slab_count, sub_count)

    def rows_first(lists):
        return jnp.transpose(lists, (1, 0, 2))

    sent = pl.pallas_call(
        functools.partial(front_kernel, places),
        out_shape=[shaped(8 * LEAVES + 8, HALF), shaped(LEAVES, 128), shaped(PARENTS, 128)]
        + [jax.ShapeDtypeStruct((8, LIST), i32)]
        + [packed] * 4,
        in_specs=[HBM] * 7,
        out_specs=[VMEM] * 8,
        scratch_shapes=[
            pltpu.SMEM(send_leaves.shape, i32),
            pltpu.SMEM(send_parents.shape, i32),
            pltpu.SMEM((1, LEAVES), i32),
            pltpu.VMEM((1, LEAVES), i32),
            pltpu.VMEM((3, 1, near_pairs.shape[2]), i32),
            pltpu.VMEM(positions.shape, f32),
            pltpu.VMEM((2 * LEAVES, HALF), f32),
            pltpu.VMEM(UP.shape, f32),
            pltpu.SemaphoreType.DMA((8,)),
            pltpu.VMEM((4 * (SLOTS + PSLOTS), 128), f32),
        ],
        compiler_params=params,
        name="moments_and_packing",
    )(
        *(
            pltpu.with_memory_space_constraint(value, pltpu.HBM)
            for value in (
                send_leaves,
                send_parents,
                leaf_counts.reshape(1, LEAVES),
                rows_first(near_pairs),
                positions,
                masses.reshape(2 * LEAVES, HALF),
                jnp.asarray(UP),
            )
        )
    )
    bodies = sent[0].reshape(LEAVES + 1, 8, HALF)
    moments, parents, words = sent[1:4]

    def exchange(value, way, back):
        pairs = []
        for s in range(slab_count):
            for u in range(sub_count):
                here = s * sub_count + u
                there = (s + slab_steps[way]) % slab_count * sub_count + (
                    u + sub_steps[way]
                ) % sub_count
                pairs.append((here, there) if back else (there, here))
        return lax.ppermute(value, ("slab", "sub"), pairs)

    incoming = [exchange(sent[4 + way], way, False) for way in range(4)]

    field = pl.pallas_call(
        functools.partial(self_kernel, places),
        out_shape=tiled,
        in_specs=[SMEM, VMEM],
        out_specs=VMEM,
        scratch_shapes=[pltpu.VMEM((GROUP, LEAF, LEAF), bf16)] * 4
        + [pltpu.VMEM((GROUP, 32, LEAF), bf16)] * 2
        + [pltpu.VMEM((GROUP, 2, 8, LEAF), f32)] * 2,
        compiler_params=params,
        cost_estimate=heavy,
        name="self_pairs",
    )(words, bodies)

    middle = pl.pallas_call(
        functools.partial(remote_kernel, places),
        out_shape=[tiled, shaped(LEAVES, 128), shaped(PARENTS, 128)] + [packed] * 4,
        in_specs=[SMEM] + [VMEM] * 10,
        out_specs=[VMEM] * 7,
        scratch_shapes=[
            pltpu.VMEM((4 * SLOTS + 1, 8, HALF), f32),
            pltpu.VMEM((4 * SLOTS + 1, 8, HALF), f32),
            pltpu.VMEM((16 * FEATS, 128), f32),
            pltpu.VMEM((16 * FEATS, 128), f32),
        ]
        + pair_scratch(GROUP // 2),
        compiler_params=params,
        input_output_aliases={10: 0},
        name="pairs_with_others",
    )(
        words,
        rows_first(far_pairs),
        rows_first(parent_pairs),
        bodies,
        moments,
        parents,
        *incoming,
        field,
    )
    field, leaf_terms, parent_terms = middle[:3]
    arrived = [exchange(middle[3 + way], way, True) for way in range(4)]

    field = pl.pallas_call(
        functools.partial(near_kernel, places),
        out_shape=tiled,
        in_specs=[SMEM] + [VMEM] * 2,
        out_specs=VMEM,
        scratch_shapes=pair_scratch(GROUP),
        compiler_params=params,
        cost_estimate=heavy,
        input_output_aliases={2: 0},
        name="own_pairs",
    )(words, bodies, field)

    return pl.pallas_call(
        functools.partial(back_kernel, places),
        out_shape=[shaped(4, LEAVES * LEAF), tiled],
        in_specs=[SMEM] * 3 + [VMEM] * 9,
        out_specs=[HBM, VMEM],
        input_output_aliases={4: 1},
        scratch_shapes=[
            pltpu.VMEM((LEAVES, 128), f32),
            pltpu.VMEM((PARENTS, 128), f32),
            pltpu.VMEM((8 * LEAVES, HALF), f32),
            pltpu.VMEM((SLOTS + PSLOTS, 128), f32),
            pltpu.VMEM((4, LEAVES * LEAF), f32),
            pltpu.SemaphoreType.DMA((4,)),
        ],
        compiler_params=params,
        name="shift_and_evaluate",
    )(
        leaf_counts,
        send_leaves,
        send_parents,
        sent[0],
        field,
        leaf_terms,
        parent_terms,
        jnp.asarray(DOWN),
        *arrived,
    )[0]


def solution(mesh):
    return jax.shard_map(
        on_device,
        mesh=mesh,
        in_specs=(
            P(None, ("slab", "sub")),
            P(("slab", "sub")),
            P(("slab", "sub")),
            P(("slab", "sub"), None),
            P(("slab", "sub"), None),
            P(("slab", "sub"), None, None),
            P(("slab", "sub"), None, None),
            P(("slab", "sub"), None, None),
        ),
        out_specs=P(None, ("slab", "sub")),
        check_vma=False,
    )
```
